32 devices in a mesh: stream: 2 (over y), page: 16 (over z, x, core).
Axes of the slice: x: 2, y: 2, z: 4, core: 2. Of those that a mesh axis runs over, the one named last changes fastest.
Arguments:
- block_input: bfloat16 [2, 9216, 768], P('stream', 'page'), may hold values from -6 to 6
- cotangent: bfloat16 [2, 9216, 768], P('stream', 'page'), may hold values from -6 to 6
- norm_gain: float32 [2, 768, 3], P('stream'), may hold values from 0.5 to 1.5
- norm_bias: float32 [2, 768, 3], P('stream'), may hold values from -2 to 2
- w_qkv: bfloat16 [2, 768, 2304], P('stream'), may hold values from -0.21875 to 0.21875
- w_out: bfloat16 [2, 768, 768], P('stream'), may hold values from -0.625 to 0.625
- w_query: bfloat16 [2, 768, 768], P('stream'), may hold values from -0.21875 to 0.21875
- w_keyval: bfloat16 [2, 768, 1536], P('stream'), may hold values from -0.21875 to 0.21875
- w_cross: bfloat16 [2, 768, 768], P('stream'), may hold values from -0.875 to 0.875
- w_up: bfloat16 [2, 768, 3072], P('stream'), may hold values from -0.21875 to 0.21875
- b_up: float32 [2, 3072], P('stream'), may hold values from -3 to 3
- w_down: bfloat16 [2, 3072, 768], P('stream'), may hold values from -0.109375 to 0.109375
- b_down: float32 [2, 768], P('stream'), may hold values from -2 to 2
- row_page: int32 [192], replicated, may hold values from 0 to 3, never falling along the last dimension, each value on 1 to 96 neighbouring positions
- lengths: int32 [16], P('page'), may hold values from 1 to 576, 4608 in all
Outputs:
- block_output: bfloat16 [2, 9216, 768], P('stream', 'page')
- input_grad: bfloat16 [2, 9216, 768], P('stream', 'page')
- gain_grad: float32 [2, 768, 3], P('stream', 'page')
- bias_grad: float32 [2, 768, 3], P('stream', 'page')
- qkv_grad: float32 [2, 768, 2304], P('stream', 'page')
- out_grad: float32 [2, 768, 768], P('stream', 'page')
- query_grad: float32 [2, 768, 768], P('stream', 'page')
- keyval_grad: float32 [2, 768, 1536], P('stream', 'page')
- cross_grad: float32 [2, 768, 768], P('stream', 'page')
- up_grad: float32 [2, 768, 3072], P('stream', 'page')
- up_bias_grad: float32 [2, 3072], P('stream', 'page')
- down_grad: float32 [2, 3072, 768], P('stream', 'page')
- down_bias_grad: float32 [2, 768], P('stream', 'page')
The draws below stay inside these ranges and needn't reach their ends.
Inputs may be any that keep to these rules, and one draw needn't show every extreme that they name: `row_page`: page numbers never fall along the rows; each page has 1 to (96) rows and one has exactly (96). The lengths sum to 4608 and the longest is 576.
All inputs are finite; a program needn't handle non-finite values. No bound on the sum of `lengths` on one device may be relied on, other than what follows from the above.
Results may differ from the reference program's by a relative error of at most 0.019.
Values may be sent and summed in bfloat16 or wider, within the bound.
No kernel may reach another device: no remote copies, remote signals or barrier semaphores. Data moves between devices by JAX's collectives and lax.ppermute only.
A program may use at most 256 MiB of HBM per device.

```python
import math
import jax
import jax.numpy as jnp
import numpy as np
from jax import lax

D = 768
HEADS = 12
HEAD = 64
FF = 3072
WIN = 12
SHIFT = 6
COLS = 48
TOK_DEV = 576
TOKENS = 9216
NROW = 192
PAGES = 4
N_PAGE = 16


def levels(own_key, extent, split, least, largest):
    gain, own = 1.0, jax.random.fold_in(own_key, 6)
    for dim, shards_of in split:
        heights = jnp.exp(jax.random.uniform(jax.random.fold_in(own, dim), (shards_of,), jnp.float32, least / len(split), largest / len(split)))
        gain = gain * jnp.repeat(heights, extent[dim] // shards_of).reshape([-1 if axis == dim else 1 for axis in range(len(extent))])
    return gain


def length_profile(number_of, total, bound, lean):
    portions = [(1 << 20) // math.isqrt(rank ** lean) + 1 for rank in range(2, number_of + 1)]
    rest, given = total - bound - (number_of - 1), [1] * (number_of - 1)
    while rest > 0:
        movable = [i for i in range(number_of - 1) if given[i] < bound]
        mass, left = sum([portions[i] for i in movable]), rest
        for i in movable:
            addition = min(bound - given[i], max(1, left * portions[i] // mass), rest)
            given[i] = given[i] + addition
            rest = rest - addition
    return np.array([bound] + given)


def uneven_parts(stream_key, number_of, total, limit, skew):
    if number_of == 2:
        one = jax.random.randint(stream_key, (), max(1, total - limit), min(limit, total - 1) + 1)
        return jnp.stack([one, total - one])
    sizes = jnp.asarray(length_profile(number_of, total, limit, skew), jnp.int32)
    couples = (number_of - 1) // 2
    donor, taker = sizes[1:1 + 2 * couples:2], sizes[2:2 + 2 * couples:2]
    margin = jnp.minimum(donor - 1, limit - taker)
    shifted = jax.random.randint(jax.random.fold_in(stream_key, 1), (couples,), 0, 1 << 20) % (margin + 1)
    sizes = sizes.at[1:1 + 2 * couples:2].set(donor - shifted).at[2:2 + 2 * couples:2].set(taker + shifted)
    return sizes[jax.random.permutation(jax.random.fold_in(stream_key, 2), number_of)]


def bell_draw(key, dims, scale, reach, split=(), dtype=jnp.bfloat16):
    values = jax.random.normal(key, dims, jnp.float32) * scale
    if len(split) > 0:
        values = levels(key, dims, split, -0.22, 0.18) * values
    return jnp.clip(values, min=-reach, max=reach).astype(dtype)


def setup_inputs(seed: int = 0) -> dict:
    key_of = jax.random.split(jax.random.key(seed), 16)
    return {
        "block_input": bell_draw(key_of[0], (2, TOKENS, D), 1.0, 6.0, ((0, 2), (1, 16))),
        "cotangent": bell_draw(key_of[1], (2, TOKENS, D), 1.0, 6.0, ((0, 2), (1, 16))),
        "norm_gain": jnp.clip(1.0 + 0.1 * jax.random.normal(key_of[2], (2, D, 3), jnp.float32), 0.5, 1.5),
        "norm_bias": bell_draw(key_of[3], (2, D, 3), 0.3, 2.0, ((0, 2),), jnp.float32),
        "w_qkv": bell_draw(key_of[4], (2, D, 3 * D), D ** -0.5, 0.21875, ((0, 2),)),
        "w_out": bell_draw(key_of[5], (2, D, D), (D // 8) ** -0.5, 0.625, ((0, 2),)),
        "w_query": bell_draw(key_of[6], (2, D, D), D ** -0.5, 0.21875, ((0, 2),)),
        "w_keyval": bell_draw(key_of[7], (2, D, 2 * D), D ** -0.5, 0.21875, ((0, 2),)),
        "w_cross": bell_draw(key_of[8], (2, D, D), (D // 16) ** -0.5, 0.875, ((0, 2),)),
        "w_up": bell_draw(key_of[9], (2, D, FF), D ** -0.5, 0.21875, ((0, 2),)),
        "b_up": bell_draw(key_of[10], (2, FF), 0.5, 3.0, ((0, 2),), jnp.float32),
        "w_down": bell_draw(key_of[11], (2, FF, D), FF ** -0.5, 0.109375, ((0, 2),)),
        "b_down": bell_draw(key_of[12], (2, D), 0.3, 2.0, ((0, 2),), jnp.float32),
        "row_page": jnp.searchsorted(jnp.cumsum(uneven_parts(key_of[13], PAGES, NROW, 8 * WIN, 2)), jnp.arange(NROW), side="right").astype(jnp.int32),
        "lengths": uneven_parts(key_of[14], N_PAGE, N_PAGE * TOK_DEV // 2, TOK_DEV, 2).astype(jnp.int32),
    }


@jax.custom_vjp
def low(v):
    return lax.optimization_barrier(v.astype(jnp.bfloat16)).astype(jnp.float32)

@jax.custom_vjp
def low_back(v):
    return v

def low_keep(v):
    return (low(v), None)

def low_pass(kept, grad):
    return (grad,)

def back_keep(v):
    return (v, None)

def back_low(kept, grad):
    return (low(grad),)
low.defvjp(low_keep, low_pass)
low_back.defvjp(back_keep, back_low)
norm_eps = 1e-05
masked_score = -1e+30
highest = lax.Precision.HIGHEST

def normed(inputs, scales, shifts):
    average = lax.optimization_barrier(jnp.mean(inputs, axis=-1, keepdims=True))
    centred = inputs - average
    spread = lax.optimization_barrier(jnp.mean(centred * centred, axis=-1, keepdims=True))
    return centred * lax.rsqrt(spread + norm_eps) * scales + shifts

def matmul(left, right):
    return jnp.dot(left, right, precision=highest, preferred_element_type=jnp.float32)

def attend(queries, key_part, value_part, allowed):
    scores = low_back(jnp.einsum('qhd,khd->hqk', queries, key_part, precision=highest) * HEAD ** (-0.5))
    scores = jnp.where(allowed[None], scores, masked_score)
    peak = lax.optimization_barrier(jnp.max(scores, axis=-1, keepdims=True))
    weights = jnp.exp(scores - peak)
    probs = low(weights / lax.optimization_barrier(jnp.sum(weights, axis=-1, keepdims=True)))
    return jnp.einsum('hqk,khd->qhd', probs, value_part, precision=highest)

def window_self(queries, key_part, value_part, row_page):
    blocks = COLS // WIN

    def tiles(values):
        grid = jnp.roll(values.reshape(NROW, COLS, HEADS, HEAD), (-SHIFT, -SHIFT), (0, 1))
        grid = grid.reshape(N_PAGE, WIN, blocks, WIN, HEADS, HEAD)
        return grid.transpose(0, 2, 1, 3, 4, 5).reshape(N_PAGE, blocks, WIN * WIN, HEADS, HEAD)
    band_pages = jnp.roll(row_page, -SHIFT).reshape(N_PAGE, WIN)
    wrapped = jnp.roll(jnp.arange(COLS) < SHIFT, -SHIFT).reshape(blocks, WIN)
    token_wrap = jnp.tile(wrapped, (1, WIN))
    same_wrap = token_wrap[:, :, None] == token_wrap[:, None, :]

    def one_band(pieces):
        band_query, band_keys, band_values, pages = pieces
        token_page = jnp.repeat(pages, WIN)
        allowed = same_wrap & (token_page[:, None] == token_page[None, :])[None]
        return jax.vmap(attend)(band_query, band_keys, band_values, allowed)
    mixed = lax.map(jax.checkpoint(one_band), (tiles(queries), tiles(key_part), tiles(value_part), band_pages))
    mixed = mixed.reshape(N_PAGE, blocks, WIN, WIN, HEADS, HEAD).transpose(0, 2, 1, 3, 4, 5)
    mixed = jnp.roll(mixed.reshape(NROW, COLS, HEADS, HEAD), (SHIFT, SHIFT), (0, 1))
    return mixed.reshape(TOKENS, D)

def shaped(values):
    return values.reshape(N_PAGE, TOK_DEV, HEADS, HEAD)

def causal_self(queries, key_part, value_part, lengths):
    positions = jnp.arange(TOK_DEV)

    def one_sequence(pieces):
        seq_query, seq_keys, seq_values, length = pieces
        allowed = (positions[None, :] <= positions[:, None]) & (positions[None, :] < length)
        return attend(seq_query, seq_keys, seq_values, allowed)
    mixed = lax.map(jax.checkpoint(one_sequence), (shaped(queries), shaped(key_part), shaped(value_part), lengths))
    return mixed.reshape(TOKENS, D)

def cross_attend(queries, key_part, value_part, key_valid):

    def one_pair(pieces):
        pair_query, pair_keys, pair_values, valid_keys = pieces
        allowed = jnp.broadcast_to(valid_keys[None, :], (TOK_DEV, TOK_DEV))
        return attend(pair_query, pair_keys, pair_values, allowed)
    mixed = lax.map(jax.checkpoint(one_pair), (shaped(queries), shaped(key_part), shaped(value_part), key_valid))
    return mixed.reshape(TOKENS, D)

def feed_forward(normal_rows, up_weight, up_shift, down_weight, down_shift):

    def one_block(block_rows):
        pre_act = low_back(matmul(block_rows, up_weight) + up_shift)
        hidden = low(jax.nn.gelu(pre_act, approximate=True))
        return low_back(matmul(hidden, down_weight) + down_shift)
    result = lax.map(jax.checkpoint(one_block), normal_rows.reshape(N_PAGE, TOK_DEV, D))
    return result.reshape(TOKENS, D)

def forward(block_input, norm_gain, norm_bias, w_qkv, w_out, w_query, w_keyval, w_cross, w_up, b_up, w_down, b_down, row_page, lengths):
    positions = jnp.arange(TOK_DEV)
    key_valid = [positions[None, :] < lengths[:, None], jnp.ones((N_PAGE, TOK_DEV), jnp.bool_)]
    after_self = []
    for stream in range(2):
        first = low(normed(block_input[stream], norm_gain[stream, :, 0], norm_bias[stream, :, 0]))
        packed = low(low_back(matmul(first, w_qkv[stream])))
        queries = packed[:, :D]
        key_part = packed[:, D:2 * D]
        value_part = packed[:, 2 * D:]
        if stream == 0:
            mixed = window_self(queries, key_part, value_part, row_page)
        else:
            mixed = causal_self(queries, key_part, value_part, lengths)
        mixed = low(low_back(mixed))
        after_self.append(block_input[stream] + low_back(matmul(mixed, w_out[stream])))
    second = [low(normed(after_self[stream], norm_gain[stream, :, 1], norm_bias[stream, :, 1])) for stream in range(2)]
    results = []
    for stream in range(2):
        cross_queries = low(low_back(matmul(second[stream], w_query[stream])))
        cross_pair = low(low_back(matmul(low_back(second[1 - stream]), w_keyval[stream])))
        mixed = cross_attend(cross_queries, cross_pair[:, :D], cross_pair[:, D:], key_valid[stream])
        mixed = low(low_back(mixed))
        after_cross = after_self[stream] + low_back(matmul(mixed, w_cross[stream]))
        third = low(normed(after_cross, norm_gain[stream, :, 2], norm_bias[stream, :, 2]))
        results.append(after_cross + feed_forward(third, w_up[stream], b_up[stream], w_down[stream], b_down[stream]))
    return jnp.stack(results)

def reference(block_input, cotangent, norm_gain, norm_bias, w_qkv, w_out, w_query, w_keyval, w_cross, w_up, b_up, w_down, b_down, row_page, lengths):
    floats = tuple((array.astype(jnp.float32) for array in (block_input, norm_gain, norm_bias, w_qkv, w_out, w_query, w_keyval, w_cross, w_up, b_up, w_down, b_down)))

    def whole_layer(*params):
        return forward(*params, row_page, lengths)
    output, pull = jax.vjp(whole_layer, *floats)
    grads = pull(cotangent.astype(jnp.float32))
    return (output.astype(jnp.bfloat16), grads[0].astype(jnp.bfloat16), grads[1], grads[2], grads[3], grads[4], grads[5], grads[6], grads[7], grads[8], grads[9], grads[10], grads[11])
```

```python
import functools

import jax
import jax.numpy as jnp
from jax import lax
from jax.experimental import pallas as pl
from jax.experimental.pallas import tpu as pltpu
from jax.sharding import PartitionSpec as P

HEADS = 12
HEAD = 64
WIN = 12
SHIFT = 6
NORM_EPS = 1e-05
MASKED = -1e30


def dot_nt(a,b):
    return lax.dot_general(a,b,(((1,),(1,)),((),())),preferred_element_type=jnp.float32)
def dot_nn(a,b):
    return lax.dot_general(a,b,(((1,),(0,)),((),())),preferred_element_type=jnp.float32)

def fill_self_bias(info, bias):
    tokens=bias.shape[0]; half=tokens//2
    cols=tokens//12
    def codes(shape,dim):
        t=lax.broadcasted_iota(jnp.int32,shape,dim)
        row=jnp.zeros(shape,jnp.int32)
        page=jnp.full(shape,info[2],jnp.int32)
        for r in range(1,12):
            inside=t>=r*cols
            row=jnp.where(inside,r,row)
            page=jnp.where(inside,info[2+r],page)
        c=t-row*cols
        win=jnp.zeros(shape,jnp.int32)
        for w in range(1,cols//12):
            win=jnp.where((c>=6+12*(w-1))&(c<6+12*w),w,win)
        win=jnp.where(c>=cols-6,cols//12+1,win)
        slot=jnp.where(t<half,t+half,t-half)
        return page*16+win,slot
    ck,sk=codes((tokens,1),0)
    cq,sq=codes((1,tokens),1)
    length=info[1]
    @pl.when(info[0]==1)
    def _():
        ok=(sk<=sq)&(sk<length)
        bias[...]=jnp.where(ok,0.0,MASKED)
    @pl.when(info[0]==0)
    def _():
        bias[...]=jnp.where(ck==cq,0.0,MASKED)

def fill_cross_bias(info,bias):
    tokens=bias.shape[0]
    t=lax.broadcasted_iota(jnp.int32,bias.shape,0)
    bias[...]=jnp.where((t<info[1])|(info[0]==1),0.0,MASKED)

def lane_pick(e,scale):
    lane=lax.broadcasted_iota(jnp.int32,(1,2*HEAD),1)
    return jnp.where((lane>=HEAD)==bool(e),scale,0.0).astype(jnp.bfloat16)

def fwd_kernel(fill,info,q_ref,k_ref,v_ref,o_ref,lse_ref,bias):
    @pl.when(pl.program_id(0)==0)
    def _():
        fill(info,bias)
    q=q_ref[...]; k=k_ref[...]; v=v_ref[...]
    vt=v.T
    outs=[]
    for e in range(2):
        qe=q*lane_pick(e,HEAD**-0.5)
        st=dot_nt(k,qe)+bias[...]
        mx=jnp.max(st,axis=0,keepdims=True)
        p=jnp.exp(st-mx)
        l=jnp.sum(p,axis=0,keepdims=True)
        ot=dot_nn(vt[e*HEAD:(e+1)*HEAD],p.astype(jnp.bfloat16))
        outs.append(ot*(1.0/l))
        lse_ref[0,e:e+1,:]=mx+jnp.log(l)
    o_ref[...]=jnp.concatenate(outs,0).T.astype(jnp.bfloat16)

def attn_fwd(info,q,k,v,qo,ko,vo,fill,name):
    t=q.shape[0]; d=768; pairs=d//128
    spec=lambda off: pl.BlockSpec((t,128),lambda j,info:(0,off+j))
    return pl.pallas_call(
        functools.partial(fwd_kernel,fill),
        grid_spec=pltpu.PrefetchScalarGridSpec(num_scalar_prefetch=1,grid=(pairs,),
            in_specs=[spec(qo),spec(ko),spec(vo)],
            out_specs=[spec(0),pl.BlockSpec((1,2,t),lambda j,info:(j,0,0))],
            scratch_shapes=[pltpu.VMEM((t,t),jnp.float32)]),
        out_shape=[jax.ShapeDtypeStruct((t,d),jnp.bfloat16),jax.ShapeDtypeStruct((pairs,2,t),jnp.float32)],
        compiler_params=pltpu.CompilerParams(vmem_limit_bytes=32*2**20),
        cost_estimate=pl.CostEstimate(flops=4*t*t*d,bytes_accessed=8*t*d,transcendentals=t*t*12),
        name=name,
    )(info,q,k,v)

def bwd_kernel(fill,info,q_ref,k_ref,v_ref,do_ref,lse_ref,dq_ref,dk_ref,dv_ref,bias):
    @pl.when(pl.program_id(0)==0)
    def _():
        fill(info,bias)
    q=q_ref[...]; k=k_ref[...]; v=v_ref[...]; do=do_ref[...]
    kt=k.T
    dqs=[]; dk=None; dv=None
    for e in range(2):
        qe=q*lane_pick(e,HEAD**-0.5)
        doe=do*lane_pick(e,1.0)
        st=dot_nt(k,qe)+bias[...]
        p=jnp.exp(st-lse_ref[0,e:e+1,:])
        pd=p*dot_nt(v,doe)
        delta=jnp.sum(pd,axis=0,keepdims=True)
        ds=(pd-p*delta).astype(jnp.bfloat16)
        pb=p.astype(jnp.bfloat16)
        dve=dot_nn(pb,doe); dke=dot_nn(ds,qe)
        dv=dve if dv is None else dv+dve
        dk=dke if dk is None else dk+dke
        dqs.append(dot_nn(kt[e*HEAD:(e+1)*HEAD],ds)*HEAD**-0.5)
    dq_ref[...]=jnp.concatenate(dqs,0).T.astype(jnp.bfloat16)
    dk_ref[...]=dk.astype(jnp.bfloat16)
    dv_ref[...]=dv.astype(jnp.bfloat16)

def attn_bwd(info,q,k,v,qo,ko,vo,do,lse,fill,name):
    t=q.shape[0]; d=768; pairs=d//128
    spec=lambda off: pl.BlockSpec((t,128),lambda j,info:(0,off+j))
    sh=jax.ShapeDtypeStruct((t,d),jnp.bfloat16)
    return pl.pallas_call(
        functools.partial(bwd_kernel,fill),
        grid_spec=pltpu.PrefetchScalarGridSpec(num_scalar_prefetch=1,grid=(pairs,),
            in_specs=[spec(qo),spec(ko),spec(vo),spec(0),pl.BlockSpec((1,2,t),lambda j,info:(j,0,0))],
            out_specs=[spec(0)]*3,
            scratch_shapes=[pltpu.VMEM((t,t),jnp.float32)]),
        out_shape=[sh]*3,
        compiler_params=pltpu.CompilerParams(vmem_limit_bytes=32*2**20),
        cost_estimate=pl.CostEstimate(flops=10*t*t*d,bytes_accessed=16*t*d,transcendentals=t*t*12),
        name=name,
    )(info,q,k,v,do,lse)


def narrow_kernel(order, x_ref, dy_ref, *rest):
    send_ref, keep_ref, across, sorted_rows = rest[-4:]
    rows = x_ref.shape[1] // 16
    half = 8 * rows

    @pl.when(pl.program_id(0) == 0)
    def _():
        across[...] = x_ref[...].T
        for i in range(16):
            start = pl.multiple_of(order[i] * rows, 16)
            sorted_rows[i * rows : (i + 1) * rows, :] = across[pl.ds(start, rows), :]

    grad = dot_nn(sorted_rows[...], dy_ref[...]).astype(jnp.bfloat16)
    send_ref[...] = grad[:half].reshape(send_ref.shape)
    keep_ref[...] = grad[half:].reshape(keep_ref.shape)


def grad_narrow(order, x, dy, height, place, carried, name):
    tokens, wide = dy.shape
    steps = wide // 768
    rows = x.shape[1] // 16
    out = jax.ShapeDtypeStruct((8, height, 768), jnp.bfloat16)
    piece = pl.BlockSpec((8, rows, 768), lambda j, order: (0, place + j, 0))
    in_specs = [
        pl.BlockSpec(x.shape, lambda j, order: (0, 0)),
        pl.BlockSpec((tokens, 768), lambda j, order: (0, j)),
    ]
    operands = [order, x, dy]
    aliases = {}
    if carried is not None:
        in_specs += [pl.BlockSpec(memory_space=pl.ANY)] * 2
        operands += list(carried)
        aliases = {3: 0, 4: 1}
    return pl.pallas_call(
        narrow_kernel,
        grid_spec=pltpu.PrefetchScalarGridSpec(
            num_scalar_prefetch=1,
            grid=(steps,),
            in_specs=in_specs,
            out_specs=[piece, piece],
            scratch_shapes=[
                pltpu.VMEM((x.shape[1], tokens), jnp.bfloat16),
                pltpu.VMEM((x.shape[1], tokens), jnp.bfloat16),
            ],
        ),
        out_shape=[out, out],
        input_output_aliases=aliases,
        compiler_params=pltpu.CompilerParams(vmem_limit_bytes=24 * 2**20),
        cost_estimate=pl.CostEstimate(
            flops=2 * tokens * wide * x.shape[1],
            bytes_accessed=2 * (x.size + dy.size + 768 * wide),
            transcendentals=0,
        ),
        name=name,
    )(*operands)


def early_kernel(x_ref, dy_ref, *rest):
    out_ref, across = rest[-2:]

    @pl.when(pl.program_id(0) == 0)
    def _():
        across[...] = x_ref[...].T

    out_ref[...] = dot_nn(across[...], dy_ref[...]).astype(jnp.bfloat16).reshape(out_ref.shape)


def early_down_kernel(x_ref, dy_ref, out_ref):
    out_ref[...] = dot_nn(x_ref[...].T, dy_ref[...]).astype(jnp.bfloat16).reshape(out_ref.shape)


def early_grads(hidden, dy, third, pre_low):
    tokens, deep = hidden.shape
    out = jax.ShapeDtypeStruct((16, 384, 768), jnp.bfloat16)
    cost = pl.CostEstimate(
        flops=2 * tokens * deep * 768, bytes_accessed=2 * 768 * (deep + tokens), transcendentals=0
    )
    params = pltpu.CompilerParams(vmem_limit_bytes=24 * 2**20)
    down = pl.pallas_call(
        early_down_kernel,
        grid=(8,),
        in_specs=[
            pl.BlockSpec((tokens, 384), lambda j: (0, j)),
            pl.BlockSpec(dy.shape, lambda j: (0, 0)),
        ],
        out_specs=pl.BlockSpec((2, 192, 768), lambda j: (j, 0, 0)),
        out_shape=out,
        compiler_params=params,
        cost_estimate=cost,
        name="gdown",
    )(hidden, dy)
    return pl.pallas_call(
        early_kernel,
        grid=(4,),
        in_specs=[
            pl.BlockSpec(third.shape, lambda j: (0, 0)),
            pl.BlockSpec((tokens, 768), lambda j: (0, j)),
            pl.BlockSpec(memory_space=pl.ANY),
        ],
        out_specs=pl.BlockSpec((16, 48, 768), lambda j: (0, 4 + j, 0)),
        out_shape=out,
        scratch_shapes=[pltpu.VMEM((768, tokens), jnp.bfloat16)],
        input_output_aliases={2: 0},
        compiler_params=params,
        cost_estimate=cost,
        name="gup",
    )(third, pre_low, down)


def swap(x, bit):
    return lax.ppermute(x, "page", [(i, i ^ bit) for i in range(16)])


def halved_small(x):
    device = lax.axis_index("page")
    bit = 1
    while x.shape[0] > 1:
        pairs = x.reshape(x.shape[0] // 2, 2, x.shape[1])
        mine = device // bit % 2
        other = lax.dynamic_index_in_dim(pairs, 1 - mine, 1, keepdims=False)
        x = lax.dynamic_index_in_dim(pairs, mine, 1, keepdims=False) + swap(other, bit)
        bit *= 2
    return x[0]


def halved_first(send, keep):
    arrived = swap(send, 1)
    return keep[:4] + arrived[:4], keep[4:] + arrived[4:]


def halved_rest(outgoing, stay):
    for bit, count in ((2, 2), (4, 1), (8, 0)):
        arrived = swap(outgoing, bit)
        if count == 0:
            return stay[0].astype(jnp.float32) + arrived[0].astype(jnp.float32)
        outgoing = stay[:count] + arrived[:count]
        stay = stay[count:] + arrived[count:]


def layer_norm(inputs, scales, shifts):
    average = jnp.mean(inputs, axis=1, keepdims=True)
    centred = inputs - average
    spread = jnp.mean(centred * centred, axis=1, keepdims=True)
    inverse = lax.rsqrt(spread + NORM_EPS)
    unit = centred * inverse
    return (unit * scales + shifts).astype(jnp.bfloat16), unit, inverse


def norm_back(upstream, unit, inverse, scales):
    scaled = upstream * scales
    inner = (
        scaled
        - jnp.mean(scaled, axis=1, keepdims=True)
        - unit * jnp.mean(scaled * unit, axis=1, keepdims=True)
    )
    return (inverse * inner, jnp.sum(upstream * unit, axis=0), jnp.sum(upstream, axis=0))


def matmul(left, right):
    return jnp.dot(left, right, preferred_element_type=jnp.float32)


def gelu_pair(pre):
    root = 0.7978845608028654
    square = pre * pre
    turned = jnp.tanh(root * pre * (1.0 + 0.044715 * square))
    value = 0.5 * pre * (1.0 + turned)
    slope = 0.5 * (1.0 + turned) + 0.5 * pre * (1.0 - turned * turned) * root * (
        1.0 + 3 * 0.044715 * square
    )
    return value, slope


def on_device(
    block_input,
    cotangent,
    norm_gain,
    norm_bias,
    w_qkv,
    w_out,
    w_query,
    w_keyval,
    w_cross,
    w_up,
    b_up,
    w_down,
    b_down,
    row_page,
    lengths,
):
    x = block_input[0]
    dy = cotangent[0]
    tokens, width = x.shape
    half = tokens // 2
    pages = lax.axis_size("page")
    device = lax.axis_index("page")
    stream = lax.axis_index("stream")
    scales = norm_gain[0].T
    shifts = norm_bias[0].T
    padded = jnp.concatenate([row_page, row_page[:SHIFT]])
    info = jnp.concatenate(
        [
            stream.astype(jnp.int32)[None],
            lengths,
            lax.dynamic_slice_in_dim(padded, device * WIN + SHIFT, WIN),
        ]
    )
    stay = [(pages + i, pages + i) for i in range(pages)]
    both = ("stream", "page")
    forth = [((i + 1) % pages, i) for i in range(pages)] + stay
    back = [(i, (i + 1) % pages) for i in range(pages)] + stay

    def to_windows(rows):
        return jnp.concatenate([rows[half:], lax.ppermute(rows[:half], both, forth)])

    def to_bands(rows):
        return jnp.concatenate([lax.ppermute(rows[half:], both, back), rows[:half]])

    def partner_of(rows):
        return lax.ppermute(rows, "stream", [(0, 1), (1, 0)])

    moved = to_windows(x)
    first, unit_one, inverse_one = layer_norm(moved.astype(jnp.float32), scales[0], shifts[0])
    packed = matmul(first, w_qkv[0]).astype(jnp.bfloat16)
    moved_mixed, self_log = attn_fwd(info, packed, packed, packed, 0, 6, 12, fill_self_bias, "selff")
    self_mixed = to_bands(moved_mixed)
    after_self = x.astype(jnp.float32) + matmul(self_mixed, w_out[0])
    second, unit_two, inverse_two = layer_norm(after_self, scales[1], shifts[1])
    partner = partner_of(second)
    cross_q = matmul(second, w_query[0]).astype(jnp.bfloat16)
    cross_pair = matmul(partner, w_keyval[0]).astype(jnp.bfloat16)
    cross_mixed, cross_log = attn_fwd(
        info, cross_q, cross_pair, cross_pair, 0, 0, 6, fill_cross_bias, "crossf"
    )
    after_cross = after_self + matmul(cross_mixed, w_cross[0])
    third, unit_three, inverse_three = layer_norm(after_cross, scales[2], shifts[2])
    pre_act = matmul(third, w_up[0]) + b_up[0]
    value, slope = gelu_pair(pre_act)
    hidden = value.astype(jnp.bfloat16)
    output = after_cross + matmul(hidden, w_down[0]) + b_down[0]
    upstream = dy.astype(jnp.float32)
    grad_down_bias = jnp.sum(upstream, axis=0)
    grad_pre = dot_nt(dy, w_down[0]) * slope
    pre_low = grad_pre.astype(jnp.bfloat16)
    grad_up_bias = jnp.sum(pre_low.astype(jnp.float32), axis=0)
    back_three, gain_three, shift_three = norm_back(
        dot_nt(pre_low, w_up[0]), unit_three, inverse_three, scales[2]
    )
    grad_cross_in = upstream + back_three
    cross_low = grad_cross_in.astype(jnp.bfloat16)
    grad_cmix = dot_nt(cross_low, w_cross[0]).astype(jnp.bfloat16)
    if pages == 16:
        early = early_grads(hidden, dy, third, pre_low)
        grad_cmix, early = lax.optimization_barrier((grad_cmix, early))
        early = lax.psum_scatter(early, "page", scatter_dimension=0, tiled=True)[0]
        ordinal = jnp.arange(16, dtype=jnp.int32)
        turned = 15 - ordinal
        turned = (turned & 1) << 3 | (turned & 2) << 1 | (turned & 4) >> 1 | (turned & 8) >> 3
        order = device.astype(jnp.int32) ^ turned
    cross_dq, cross_dk, cross_dv = attn_bwd(
        info, cross_q, cross_pair, cross_pair, 0, 0, 6, grad_cmix, cross_log,
        fill_cross_bias, "crossb",
    )
    given = dot_nt(cross_dk, w_keyval[0][:, :width]) + dot_nt(cross_dv, w_keyval[0][:, width:])
    returned = partner_of(given.astype(jnp.bfloat16))
    second_grad = dot_nt(cross_dq, w_query[0]) + returned.astype(jnp.float32)
    back_two, gain_two, shift_two = norm_back(second_grad, unit_two, inverse_two, scales[1])
    grad_self_in = grad_cross_in + back_two
    moved_low = to_windows(grad_self_in.astype(jnp.bfloat16))
    grad_smix = dot_nt(moved_low, w_out[0]).astype(jnp.bfloat16)
    if pages == 16:
        part = grad_narrow(order, cross_mixed, cross_low, 192, 0, None, "gcross")
        part = grad_narrow(order, second, cross_dq, 192, 1, part, "gquery")
        part = grad_narrow(order, partner, cross_dk, 192, 2, part, "gkey")
        part = grad_narrow(order, partner, cross_dv, 192, 3, part, "gvalue")
        cross_part = halved_first(*part)
        grad_smix, cross_part = lax.optimization_barrier((grad_smix, cross_part))
        cross_part = halved_rest(*cross_part)
    self_dq, self_dk, self_dv = attn_bwd(
        info, packed, packed, packed, 0, 6, 12, grad_smix, self_log, fill_self_bias, "selfb",
    )
    grad_first = (
        dot_nt(self_dq, w_qkv[0][:, :width])
        + dot_nt(self_dk, w_qkv[0][:, width : 2 * width])
        + dot_nt(self_dv, w_qkv[0][:, 2 * width :])
    )
    back_one, gain_one, shift_one = norm_back(grad_first, unit_one, inverse_one, scales[0])
    input_grad = to_bands((moved_low.astype(jnp.float32) + back_one).astype(jnp.bfloat16))
    small = [gain_one, gain_two, gain_three, shift_one, shift_two, shift_three, grad_down_bias]
    if pages == 16:
        part = grad_narrow(order, moved_mixed, moved_low, 192, 0, None, "gout")
        part = grad_narrow(order, first, self_dq, 192, 1, part, "gq")
        part = grad_narrow(order, first, self_dk, 192, 2, part, "gk")
        part = grad_narrow(order, first, self_dv, 192, 3, part, "gv")
        self_part = halved_rest(*halved_first(*part))

        def across(block, first_row, count):
            return jnp.concatenate(
                [block[first_row + 48 * i : first_row + 48 * (i + 1)] for i in range(count)], 1
            )

        early = early.astype(jnp.float32)
        grad_down = early[:192]
        grad_up = across(early, 192, 4)
        grad_cross = across(cross_part, 0, 1)
        grad_query = across(cross_part, 48, 1)
        grad_keyval = across(cross_part, 96, 2)
        grad_out = across(self_part, 0, 1)
        grad_qkv = across(self_part, 48, 3)
    else:

        def scattered(left, right):
            grad = lax.dot_general(
                left, right, (((0,), (0,)), ((), ())), preferred_element_type=jnp.float32
            )
            return lax.psum_scatter(grad, "page", scatter_dimension=0, tiled=True)

        grad_down = scattered(hidden, dy)
        grad_up = scattered(third, pre_low)
        grad_cross = scattered(cross_mixed, cross_low)
        grad_query = scattered(second, cross_dq)
        grad_keyval = scattered(partner, jnp.concatenate([cross_dk, cross_dv], 1))
        grad_out = scattered(moved_mixed, moved_low)
        grad_qkv = scattered(first, jnp.concatenate([self_dq, self_dk, self_dv], 1))
    stacked = jnp.concatenate(
        [v.reshape(pages, width // pages) for v in small]
        + [grad_up_bias.reshape(pages, grad_up_bias.shape[0] // pages)],
        1,
    )
    if pages == 16:
        summed = halved_small(stacked)
    else:
        summed = lax.psum_scatter(stacked, "page", scatter_dimension=0, tiled=True)[0]
    share = width // pages
    piece = [summed[i * share : (i + 1) * share] for i in range(7)]
    return (
        output.astype(jnp.bfloat16)[None],
        input_grad[None],
        jnp.stack(piece[:3], 1)[None],
        jnp.stack(piece[3:6], 1)[None],
        grad_qkv[None],
        grad_out[None],
        grad_query[None],
        grad_keyval[None],
        grad_cross[None],
        grad_up[None],
        summed[7 * share :][None],
        grad_down[None],
        piece[6][None],
    )


def solution(mesh):
    tokens = P("stream", "page", None)
    whole = P("stream", None, None)
    placed = (tokens, tokens) + (whole,) * 8 + (P("stream", None), whole, P("stream", None))
    return jax.shard_map(
        on_device,
        mesh=mesh,
        in_specs=placed + (P(), P("page")),
        out_specs=(tokens,) * 10 + (P("stream", "page"), tokens, P("stream", "page")),
        check_vma=False,
    )
```

```python
import functools

import jax
import jax.numpy as jnp
from jax import lax
from jax.experimental import pallas as pl
from jax.experimental.pallas import tpu as pltpu
from jax.sharding import PartitionSpec as P

HEADS = 12
HEAD = 64
WIN = 12
SHIFT = 6
NORM_EPS = 1e-05
MASKED = -1e30


def dot_nt(a,b):
    return lax.dot_general(a,b,(((1,),(1,)),((),())),preferred_element_type=jnp.float32)
def dot_nn(a,b):
    return lax.dot_general(a,b,(((1,),(0,)),((),())),preferred_element_type=jnp.float32)

def fill_self_bias(info, bias, first=0):
    tokens, count = bias.shape
    half=tokens//2
    cols=tokens//12
    def codes(shape,dim,start):
        t=lax.broadcasted_iota(jnp.int32,shape,dim)+start
        row=jnp.zeros(shape,jnp.int32)
        page=jnp.full(shape,info[2],jnp.int32)
        for r in range(1,12):
            inside=t>=r*cols
            row=jnp.where(inside,r,row)
            page=jnp.where(inside,info[2+r],page)
        c=t-row*cols
        win=jnp.zeros(shape,jnp.int32)
        for w in range(1,cols//12):
            win=jnp.where((c>=6+12*(w-1))&(c<6+12*w),w,win)
        win=jnp.where(c>=cols-6,cols//12+1,win)
        slot=jnp.where(t<half,t+half,t-half)
        return page*16+win,slot
    ck,sk=codes((tokens,1),0,0)
    cq,sq=codes((1,count),1,first)
    length=info[1]
    @pl.when(info[0]==1)
    def _():
        ok=(sk<=sq)&(sk<length)
        bias[...]=jnp.where(ok,0.0,MASKED)
    @pl.when(info[0]==0)
    def _():
        bias[...]=jnp.where(ck==cq,0.0,MASKED)

def fill_cross_bias(info,bias,first=0):
    tokens=bias.shape[0]
    t=lax.broadcasted_iota(jnp.int32,bias.shape,0)
    bias[...]=jnp.where((t<info[1])|(info[0]==1),0.0,MASKED)

def lane_pick(e,scale):
    lane=lax.broadcasted_iota(jnp.int32,(1,2*HEAD),1)
    return jnp.where((lane>=HEAD)==bool(e),scale,0.0).astype(jnp.bfloat16)

def fwd_kernel(fill, info, q_ref, k_ref, v_ref, o_ref, p_ref, bias):
    @pl.when(pl.program_id(0) == 0)
    def _():
        fill(info, bias)

    q, k = q_ref[...], k_ref[...]
    vt = v_ref[...].T
    scores = [dot_nt(k, q * lane_pick(e, HEAD**-0.5)) + bias[...] for e in range(2)]
    outs = []
    for e in range(2):
        weights = jnp.exp(scores[e] - jnp.max(scores[e], axis=0, keepdims=True))
        inverse = 1.0 / jnp.sum(weights, axis=0, keepdims=True)
        probs = (weights * inverse).astype(jnp.bfloat16)
        p_ref[e] = probs
        outs.append(dot_nn(vt[e * HEAD : (e + 1) * HEAD], probs))
    o_ref[...] = jnp.concatenate(outs, 0).T.astype(jnp.bfloat16)


NOTHING = pl.CostEstimate(flops=1000, bytes_accessed=1000, transcendentals=0)


def attn_fwd(info, q, k, v, qo, ko, vo, fill, name):
    tokens = q.shape[0]
    spec = lambda off: pl.BlockSpec((tokens, 128), lambda j, info: (0, off + j))
    return pl.pallas_call(
        functools.partial(fwd_kernel, fill),
        grid_spec=pltpu.PrefetchScalarGridSpec(
            num_scalar_prefetch=1,
            grid=(HEADS // 2,),
            in_specs=[spec(qo), spec(ko), spec(vo)],
            out_specs=[spec(0), pl.BlockSpec((2, tokens, tokens), lambda j, info: (j, 0, 0))],
            scratch_shapes=[pltpu.VMEM((tokens, tokens), jnp.float32)],
        ),
        out_shape=[
            jax.ShapeDtypeStruct((tokens, HEADS * HEAD), jnp.bfloat16),
            pltpu.HBM((HEADS, tokens, tokens), jnp.bfloat16),
        ],
        compiler_params=pltpu.CompilerParams(vmem_limit_bytes=24 * 2**20),
        cost_estimate=NOTHING,
        name=name,
    )(info, q, k, v)


def bwd_kernel(q_ref, k_ref, v_ref, do_ref, p_ref, d_ref):
    grads = backward_heads(q_ref[...], k_ref[...], v_ref[...], do_ref[...], p_ref)
    for i in range(3):
        d_ref[i] = grads[i]


def attn_bwd(q, k, v, qo, ko, vo, do, probs, name):
    tokens = q.shape[0]
    spec = lambda off: pl.BlockSpec((tokens, 128), lambda j: (0, off + j))
    return pl.pallas_call(
        bwd_kernel,
        grid=(HEADS // 2,),
        in_specs=[spec(qo), spec(ko), spec(vo), spec(0)]
        + [pl.BlockSpec((2, tokens, tokens), lambda j: (j, 0, 0))],
        out_specs=pl.BlockSpec((3, tokens, 128), lambda j: (0, 0, j)),
        out_shape=jax.ShapeDtypeStruct((3, tokens, HEADS * HEAD), jnp.bfloat16),
        compiler_params=pltpu.CompilerParams(vmem_limit_bytes=24 * 2**20),
        cost_estimate=NOTHING,
        name=name,
    )(q, k, v, do, probs)


def layer_norm(inputs, scales, shifts):
    average = jnp.mean(inputs, axis=1, keepdims=True)
    centred = inputs - average
    spread = jnp.mean(centred * centred, axis=1, keepdims=True)
    inverse = lax.rsqrt(spread + NORM_EPS)
    unit = centred * inverse
    return (unit * scales + shifts).astype(jnp.bfloat16), unit, inverse


def norm_back(upstream, unit, inverse, scales):
    scaled = upstream * scales
    inner = (
        scaled
        - jnp.mean(scaled, axis=1, keepdims=True)
        - unit * jnp.mean(scaled * unit, axis=1, keepdims=True)
    )
    return (inverse * inner, jnp.sum(upstream * unit, axis=0), jnp.sum(upstream, axis=0))


def matmul(left, right):
    return jnp.dot(left, right, preferred_element_type=jnp.float32)


def gelu_pair(pre):
    root = 0.7978845608028654
    square = pre * pre
    gate = 0.5 + 0.5 * jnp.tanh(pre * (root + root * 0.044715 * square))
    value = pre * gate
    return value, gate + value * (1.0 - gate) * (2 * root + 6 * root * 0.044715 * square)


def layer_parts(v):
    average = jnp.mean(v, axis=1, keepdims=True)
    centred = v - average
    inverse = lax.rsqrt(jnp.mean(centred * centred, axis=1, keepdims=True) + NORM_EPS)
    return centred * inverse, inverse


def layer_back(grad, unit, inverse, scale):
    scaled = grad * scale
    return inverse * (
        scaled
        - jnp.mean(scaled, axis=1, keepdims=True)
        - unit * jnp.mean(scaled * unit, axis=1, keepdims=True)
    )


def column_sums(*values):
    rows = [jnp.sum(v, axis=0, keepdims=True) for v in values]
    rows.append(jnp.zeros((8 - len(rows), rows[0].shape[1]), jnp.float32))
    return jnp.concatenate(rows)


def sort_rows(order, x, across, sorted_rows):
    rows = sorted_rows.shape[0] // 16
    across[...] = x.T
    for n in range(16):
        start = pl.multiple_of(order[n] * rows, 16)
        sorted_rows[n * rows : (n + 1) * rows, :] = across[pl.ds(start, rows), :]


def feed_kernel(
    order, after_ref, mixed_ref, dy_ref, scales_ref, shifts_ref, cross_ref, down_bias_ref,
    up_ref, up_bias_ref, down_ref,
    out_ref, grad_ref, low_ref, mix_ref, sums_ref, bias_ref,
    down_send, down_keep, up_send, up_keep,
    third_rows, across, sorted_rows, after, total, grad_total,
):
    step = pl.program_id(0)
    rows = dy_ref.shape[1] // 16
    half = 8 * rows

    @pl.when(step == 0)
    def _():
        after[...] = after_ref[...] + dot_nn(mixed_ref[...], cross_ref[0])
        unit = layer_parts(after[...])[0]
        third_rows[...] = (unit * scales_ref[2:3, :] + shifts_ref[2:3, :]).astype(jnp.bfloat16)
        sort_rows(order, third_rows[...], across, sorted_rows)
        total[...] = after[...] + down_bias_ref[...]
        grad_total[...] = jnp.zeros_like(grad_total)

    dy, third = dy_ref[...], third_rows[...]
    tile = up_ref.shape[2] // 2
    deep = tile // 2
    parts = [slice(0, tile), slice(tile, 2 * tile)]
    pre = [dot_nn(third, up_ref[0, :, p]) + up_bias_ref[:, p] for p in parts]
    grad_hidden = [dot_nt(dy, down_ref[0, p, :]) for p in parts]
    out = grad_third = 0.0
    grads = []
    for i, p in enumerate(parts):
        value, slope = gelu_pair(pre[i])
        hidden = value.astype(jnp.bfloat16)
        low = (grad_hidden[i] * slope).astype(jnp.bfloat16)
        bias_ref[0, :, p] = jnp.sum(low.astype(jnp.float32), axis=0, keepdims=True)
        grad = dot_nn(sorted_rows[...], low).astype(jnp.bfloat16)
        up_send[:, :, p] = grad[:half].reshape(8, rows, tile)
        up_keep[:, :, p] = grad[half:].reshape(8, rows, tile)
        grads.append(dot_nn(hidden.T, dy).astype(jnp.bfloat16))
        out += dot_nn(hidden, down_ref[0, p, :])
        grad_third += dot_nt(low, up_ref[0, :, p])
    total[...] += out
    grad_total[...] += grad_third
    for odd in range(2):
        for far in range(2):

            @pl.when((order[15] % 2 == odd) & (order[15] // 2 % 2 == far))
            def _():
                for n in range(2):
                    both = grads[n ^ far ^ 1]
                    down_send[n, 0] = both[deep * (1 - odd) : deep * (2 - odd)]
                    down_keep[n, 0] = both[deep * odd : deep * (odd + 1)]

    @pl.when(step == pl.num_programs(0) - 1)
    def _():
        out_ref[...] = total[...].astype(jnp.bfloat16)
        upstream = dy_ref[...].astype(jnp.float32)
        unit, inverse = layer_parts(after[...])
        grad = grad_total[...]
        sums_ref[...] = column_sums(grad * unit, grad, upstream)
        grad_ref[...] = upstream + layer_back(grad, unit, inverse, scales_ref[2:3, :])
        low_ref[...] = grad_ref[...].astype(jnp.bfloat16)
        mix_ref[...] = dot_nt(low_ref[...], cross_ref[0]).astype(jnp.bfloat16)


def feed_forward(order, after, mixed, dy, scales, shifts, w_cross, w_up, b_up, w_down, b_down):
    tokens, width = dy.shape
    deep = w_up.shape[2]
    tile = deep // 4
    rows = width // 16
    whole = lambda *shape: pl.BlockSpec(shape, lambda j, order: (0,) * len(shape))
    where = lambda j, order: order[8 + j] // 4
    token = whole(tokens, width)
    down_half = jax.ShapeDtypeStruct((2, 4, deep // 16, width), jnp.bfloat16)
    up_half = jax.ShapeDtypeStruct((8, 4 * rows, tile), jnp.bfloat16)
    down_piece = pl.BlockSpec((2, 1, deep // 16, width), lambda j, order: (0, j, 0, 0))
    up_piece = pl.BlockSpec((8, rows, tile), lambda j, order: (0, where(j, order), 0))
    low = jax.ShapeDtypeStruct((tokens, width), jnp.bfloat16)
    full = jax.ShapeDtypeStruct((tokens, width), jnp.float32)
    out = pl.pallas_call(
        feed_kernel,
        grid_spec=pltpu.PrefetchScalarGridSpec(
            num_scalar_prefetch=1,
            grid=(4,),
            in_specs=[
                token,
                token,
                token,
                whole(3, width),
                whole(3, width),
                whole(1, width, width),
                whole(1, width),
                pl.BlockSpec((1, width, tile), lambda j, order: (0, 0, where(j, order))),
                pl.BlockSpec((1, tile), lambda j, order: (0, where(j, order))),
                pl.BlockSpec((1, tile, width), lambda j, order: (0, where(j, order), 0)),
            ],
            out_specs=[
                token,
                token,
                token,
                token,
                whole(8, width),
                pl.BlockSpec((1, 1, tile), lambda j, order: (where(j, order), 0, 0)),
                down_piece,
                down_piece,
                up_piece,
                up_piece,
            ],
            scratch_shapes=[pltpu.VMEM((tokens, width), jnp.bfloat16)]
            + [pltpu.VMEM((width, tokens), jnp.bfloat16)] * 2
            + [pltpu.VMEM((tokens, width), jnp.float32)] * 3,
        ),
        out_shape=[
            low,
            full,
            low,
            low,
            jax.ShapeDtypeStruct((8, width), jnp.float32),
            jax.ShapeDtypeStruct((4, 1, tile), jnp.float32),
            down_half,
            down_half,
            up_half,
            up_half,
        ],
        compiler_params=pltpu.CompilerParams(vmem_limit_bytes=48 * 2**20),
        cost_estimate=NOTHING,
        name="feed",
    )(order, after, mixed, dy, scales, shifts, w_cross, b_down, w_up, b_up, w_down)
    flat = lambda part: part.reshape(8, deep // 16, width)
    return (*out[:6], (flat(out[6]), flat(out[7])), (out[8], out[9]))


def backward_heads(q, k, v, do, p_ref):
    kt = k.T
    queries = []
    keys = values = 0.0
    picked = [do * lane_pick(e, 1.0) for e in range(2)]
    grads = [dot_nt(v, picked[e]) for e in range(2)]
    for e in range(2):
        probs = p_ref[e]
        wide = probs.astype(jnp.float32)
        part = wide * grads[e]
        total = jnp.sum(part, axis=0, keepdims=True)
        ds = (part - wide * total).astype(jnp.bfloat16)
        values += dot_nn(probs, picked[e])
        keys += dot_nn(ds, q * lane_pick(e, HEAD**-0.5))
        queries.append(dot_nn(kt[e * HEAD : (e + 1) * HEAD], ds) * HEAD**-0.5)
    queries = jnp.concatenate(queries, 0).T
    return [g.astype(jnp.bfloat16) for g in (queries, keys, values)]


def self_back_kernel(q_ref, k_ref, v_ref, near_ref, far_ref, out_ref, p_ref, d_ref):
    low = jnp.concatenate([near_ref[...], far_ref[...]])
    do = dot_nt(low, out_ref[0]).astype(jnp.bfloat16)
    grads = backward_heads(q_ref[...], k_ref[...], v_ref[...], do, p_ref)
    for i in range(3):
        d_ref[i] = grads[i]


def self_back(packed, near, far, w_out, probs):
    tokens, width = packed.shape[0], near.shape[1]
    spec = lambda off: pl.BlockSpec((tokens, 128), lambda j: (0, off + j))
    rows = pl.BlockSpec(near.shape, lambda j: (0, 0))
    return pl.pallas_call(
        self_back_kernel,
        grid=(HEADS // 2,),
        in_specs=[spec(0), spec(6), spec(12), rows, rows]
        + [pl.BlockSpec((1, 128, width), lambda j: (0, j, 0))]
        + [pl.BlockSpec((2, tokens, tokens), lambda j: (j, 0, 0))],
        out_specs=pl.BlockSpec((3, tokens, 128), lambda j: (0, 0, j)),
        out_shape=jax.ShapeDtypeStruct((3, tokens, width), jnp.bfloat16),
        compiler_params=pltpu.CompilerParams(vmem_limit_bytes=24 * 2**20),
        cost_estimate=NOTHING,
        name="selfb",
    )(packed, packed, packed, near, far, w_out, pltpu.with_memory_space_constraint(probs, pltpu.HBM))


def second_kernel(back_ref, returned_ref, after_ref, grad_ref, scales_ref, low_ref, sums_ref):
    unit, inverse = layer_parts(after_ref[...])
    grad = back_ref[...] + returned_ref[...].astype(jnp.float32)
    sums_ref[...] = column_sums(grad * unit, grad)
    back = layer_back(grad, unit, inverse, scales_ref[1:2, :])
    low_ref[...] = (grad_ref[...] + back).astype(jnp.bfloat16)


def second_back(which, back, returned, after, grad, scales):
    half, width = returned.shape
    rows = pl.BlockSpec((half, width), lambda j: (which, 0))
    first = pl.BlockSpec((half, width), lambda j: (0, 0))
    return pl.pallas_call(
        second_kernel,
        grid=(1,),
        in_specs=[rows, first, rows, rows, pl.BlockSpec((3, width), lambda j: (0, 0))],
        out_specs=[first, pl.BlockSpec((8, width), lambda j: (0, 0))],
        out_shape=[
            jax.ShapeDtypeStruct((half, width), jnp.bfloat16),
            jax.ShapeDtypeStruct((8, width), jnp.float32),
        ],
        compiler_params=pltpu.CompilerParams(vmem_limit_bytes=24 * 2**20),
        cost_estimate=NOTHING,
        name="second",
    )(back, returned, after, grad, scales)


def first_kernel(
    d_ref, w_ref, moved_ref, near_ref, far_ref, scales_ref, stay_ref, gone_ref, sums_ref, total
):
    step = pl.program_id(0)
    part = dot_nt(d_ref[0], w_ref[0])

    @pl.when(step == 0)
    def _():
        total[...] = part

    @pl.when(step > 0)
    def _():
        total[...] += part

    @pl.when(step == pl.num_programs(0) - 1)
    def _():
        half = stay_ref.shape[0]
        unit, inverse = layer_parts(moved_ref[...].astype(jnp.float32))
        grad = total[...]
        sums_ref[...] = column_sums(grad * unit, grad)
        back = layer_back(grad, unit, inverse, scales_ref[0:1, :])
        stay_ref[...] = (near_ref[...].astype(jnp.float32) + back[:half]).astype(jnp.bfloat16)
        gone_ref[...] = (far_ref[...].astype(jnp.float32) + back[half:]).astype(jnp.bfloat16)


def first_back(grads, w_qkv, moved, near, far, scales):
    tokens, width = moved.shape
    half = tokens // 2
    whole = lambda *shape: pl.BlockSpec(shape, lambda j: (0,) * len(shape))
    rows = jax.ShapeDtypeStruct((half, width), jnp.bfloat16)
    return pl.pallas_call(
        first_kernel,
        grid=(3,),
        in_specs=[
            pl.BlockSpec((1, tokens, width), lambda j: (j, 0, 0)),
            pl.BlockSpec((1, width, width), lambda j: (0, 0, j)),
            whole(tokens, width),
            whole(half, width),
            whole(half, width),
            whole(3, width),
        ],
        out_specs=[whole(half, width), whole(half, width), whole(8, width)],
        out_shape=[rows, rows, jax.ShapeDtypeStruct((8, width), jnp.float32)],
        scratch_shapes=[pltpu.VMEM((tokens, width), jnp.float32)],
        compiler_params=pltpu.CompilerParams(vmem_limit_bytes=32 * 2**20),
        cost_estimate=NOTHING,
        name="first",
    )(grads, w_qkv, moved, near, far, scales)


def group_kernel(plan, halves, pieces, order, *refs):
    refs = list(refs)
    groups = [[refs.pop(0) for _ in range(n)] for n in halves]
    joined = lambda group: jnp.concatenate([r[...] for r in group]) if len(group) > 1 else group[0][...]
    outs, (across, sorted_rows) = refs[:-2], refs[-2:]
    half = sorted_rows.shape[0] // 2
    before = None
    for i, (x, dy, lead, target) in enumerate(plan):
        turn = x != before
        before = x

        @pl.when(pl.program_id(0) == i)
        def _():
            if turn:
                sort_rows(order, joined(groups[x]), across, sorted_rows)
            right = joined(groups[dy]) if lead is None else groups[dy][0][0]
            grad = dot_nn(sorted_rows[...], right).astype(jnp.bfloat16)
            send_ref, keep_ref = outs[2 * target], outs[2 * target + 1]
            send_ref[...] = grad[:half].reshape(send_ref.shape)
            keep_ref[...] = grad[half:].reshape(keep_ref.shape)


def grad_group(order, operands, plan, name):
    width = operands[0][0].shape[-1]
    rows = width // 16
    tokens = sum(a.shape[-2] for a in operands[0])
    in_specs = []
    for n, group in enumerate(operands):
        for a in group:
            if a.ndim == 2:
                in_specs.append(pl.BlockSpec(a.shape, lambda j, order: (0, 0)))
            else:
                first = min(i for i, p in enumerate(plan) if p[1] == n)
                in_specs.append(
                    pl.BlockSpec(
                        (1, *a.shape[1:]),
                        lambda j, order, first=first, last=a.shape[0] - 1: (
                            jnp.clip(j - first, 0, last),
                            0,
                            0,
                        ),
                    )
                )
    out_specs, out_shape = [], []
    for target in range(1 + max(p[3] for p in plan)):
        steps = [i for i, p in enumerate(plan) if p[3] == target]
        spec = pl.BlockSpec(
            (8, rows, width),
            lambda j, order, first=steps[0], last=len(steps) - 1: (
                0,
                jnp.clip(j - first, 0, last),
                0,
            ),
        )
        out_specs += [spec, spec]
        out_shape += [jax.ShapeDtypeStruct((8, rows * len(steps), width), jnp.bfloat16)] * 2
    outs = pl.pallas_call(
        functools.partial(group_kernel, plan, [len(g) for g in operands], len(out_specs)),
        grid_spec=pltpu.PrefetchScalarGridSpec(
            num_scalar_prefetch=1,
            grid=(len(plan),),
            in_specs=in_specs,
            out_specs=out_specs,
            scratch_shapes=[pltpu.VMEM((width, tokens), jnp.bfloat16)] * 2,
        ),
        out_shape=out_shape,
        compiler_params=pltpu.CompilerParams(vmem_limit_bytes=32 * 2**20),
        cost_estimate=NOTHING,
        name=name,
    )(order, *[a for group in operands for a in group])
    return [(outs[i], outs[i + 1]) for i in range(0, len(outs), 2)]


def add_kernel(count, *refs):
    at = 0
    for n in range(count):
        keep, arrived = refs[2 * n], refs[2 * n + 1]
        rows = keep.shape[-2]
        for i, out in enumerate(refs[2 * count :]):
            out[0, at : at + rows, :] = keep[i, 0] + arrived[i, 0]
        at += rows


def add_halves(keeps, arrivals, name="add"):
    pairs = keeps[0].shape[0] // 2
    width = keeps[0].shape[2]
    rows = sum(k.shape[1] for k in keeps)
    operands = []
    for keep, arrived in zip(keeps, arrivals):
        operands += [a.reshape(2, pairs, *a.shape[1:]) for a in (keep, arrived)]
    out = pl.BlockSpec((1, rows, width), lambda j: (j, 0, 0))
    return pl.pallas_call(
        functools.partial(add_kernel, len(keeps)),
        grid=(pairs,),
        in_specs=[
            pl.BlockSpec((2, 1, *a.shape[2:]), lambda j: (0, j, 0, 0)) for a in operands
        ],
        out_specs=[out, out],
        out_shape=[jax.ShapeDtypeStruct((pairs, rows, width), jnp.bfloat16)] * 2,
        compiler_params=pltpu.CompilerParams(vmem_limit_bytes=16 * 2**20),
        cost_estimate=NOTHING,
        name=name,
    )(*operands)


def last_kernel(keep_ref, arrived_ref, *outs):
    total = keep_ref[0].astype(jnp.float32) + arrived_ref[0].astype(jnp.float32)
    width = total.shape[1]
    at = 0
    for out in outs:
        rows, columns = out.shape
        for n in range(columns // width):
            out[:, n * width : (n + 1) * width] = total[at : at + rows]
            at += rows


def last_sum(keep, arrived, shapes):
    return pl.pallas_call(
        last_kernel,
        out_shape=[jax.ShapeDtypeStruct(s, jnp.float32) for s in shapes],
        compiler_params=pltpu.CompilerParams(vmem_limit_bytes=16 * 2**20),
        cost_estimate=NOTHING,
        name="last",
    )(keep, arrived)


def swap(x, bit):
    return lax.ppermute(x, "page", [(i, i ^ bit) for i in range(16)])


pin = lax.optimization_barrier


def on_device(
    block_input,
    cotangent,
    norm_gain,
    norm_bias,
    w_qkv,
    w_out,
    w_query,
    w_keyval,
    w_cross,
    w_up,
    b_up,
    w_down,
    b_down,
    row_page,
    lengths,
):
    x = block_input[0]
    dy = cotangent[0]
    tokens, width = x.shape
    half = tokens // 2
    pages = lax.axis_size("page")
    device = lax.axis_index("page")
    stream = lax.axis_index("stream")
    scales = norm_gain[0].T
    shifts = norm_bias[0].T
    share = width // pages
    padded = jnp.concatenate([row_page, row_page[:SHIFT]])
    info = jnp.concatenate(
        [
            stream.astype(jnp.int32)[None],
            lengths,
            lax.dynamic_slice_in_dim(padded, device * WIN + SHIFT, WIN),
        ]
    )
    stay = [(pages + i, pages + i) for i in range(pages)]
    both = ("stream", "page")
    forth = [((i + 1) % pages, i) for i in range(pages)] + stay
    back = [(i, (i + 1) % pages) for i in range(pages)] + stay

    def partner_of(rows):
        return lax.ppermute(rows, "stream", [(0, 1), (1, 0)])

    moved = jnp.concatenate([x[half:], lax.ppermute(x[:half], both, forth)])
    first, unit_one, inverse_one = layer_norm(moved.astype(jnp.float32), scales[0], shifts[0])
    packed = matmul(first, w_qkv[0]).astype(jnp.bfloat16)
    moved_mixed, self_probs = attn_fwd(
        info, packed, packed, packed, 0, 6, 12, fill_self_bias, "selff"
    )
    gone, near = moved_mixed[half:], moved_mixed[:half]
    after_gone = moved[half:].astype(jnp.float32) + matmul(gone, w_out[0])
    second_gone = layer_norm(after_gone, scales[1], shifts[1])[0]
    partner_top = lax.ppermute(
        second_gone,
        both,
        [(i, pages + (i + 1) % pages) for i in range(pages)]
        + [(pages + i, i) for i in range(pages)],
    )
    back_mixed = lax.ppermute(gone, both, back)
    after_low = moved[:half].astype(jnp.float32) + matmul(near, w_out[0])
    second_low = layer_norm(after_low, scales[1], shifts[1])[0]
    partner_low = partner_of(second_low)
    back_mixed, second_low, partner_top = pin((back_mixed, second_low, partner_top))
    after_top = x[:half].astype(jnp.float32) + matmul(back_mixed, w_out[0])
    second_top = layer_norm(after_top, scales[1], shifts[1])[0]
    after_self = jnp.concatenate([after_top, after_low])
    second = jnp.concatenate([second_top, second_low])
    cross_q = matmul(second, w_query[0]).astype(jnp.bfloat16)
    cross_q, after_self, partner_top, partner_low = pin(
        (cross_q, after_self, partner_top, partner_low)
    )
    partner = jnp.concatenate([partner_top, partner_low])
    cross_pair = matmul(partner, w_keyval[0]).astype(jnp.bfloat16)
    cross_mixed, cross_probs = attn_fwd(
        info, cross_q, cross_pair, cross_pair, 0, 0, 6, fill_cross_bias, "crossf"
    )
    if pages == 16:
        ordinal = jnp.arange(16, dtype=jnp.int32)
        turned = 15 - ordinal
        turned = (turned & 1) << 3 | (turned & 2) << 1 | (turned & 4) >> 1 | (turned & 8) >> 3
        order = device.astype(jnp.int32) ^ turned
        output, grad_cross_in, cross_low, grad_cmix, sums_three, up_bias, down, up = feed_forward(
            order, after_self, cross_mixed, dy, scales, shifts, w_cross, w_up, b_up, w_down, b_down
        )

        def onward(keeps, sends, bit):
            return add_halves(keeps, [swap(s, bit) for s in sends])

        down = onward([down[1]], [down[0]], 1)
        grad_cmix, down = pin((grad_cmix, down))
        cross_grads = attn_bwd(
            cross_q, cross_pair, cross_pair, 0, 0, 6, grad_cmix, cross_probs, "crossb"
        )

        def given(rows):
            keys = dot_nt(cross_grads[1, rows], w_keyval[0][:, :width])
            return (keys + dot_nt(cross_grads[2, rows], w_keyval[0][:, width:])).astype(jnp.bfloat16)

        returned_top = partner_of(given(slice(0, half)))
        returned_low = partner_of(given(slice(half, tokens)))
        query_back = dot_nt(cross_grads[0], w_query[0])
        (cross_part,) = grad_group(
            order,
            (
                (cross_mixed,),
                (second_top, second_low),
                (partner_top, partner_low),
                (cross_low,),
                (cross_grads,),
            ),
            ((0, 3, None, 0), (1, 4, 0, 0), (2, 4, 1, 0), (2, 4, 2, 0)),
            "gcross",
        )
        down = onward([down[1]], [down[0]], 2)
        up = onward([up[1]], [up[0]], 1)
        returned_top, cross_part, down, up = pin((returned_top, cross_part, down, up))
        low_top, sums_top = second_back(
            0, query_back, returned_top, after_self, grad_cross_in, scales
        )
        arrived_low = lax.ppermute(low_top, both, forth)
        low_top, cross_keep = pin((low_top, cross_part[1]))
        cross_part = onward([cross_keep], [cross_part[0]], 1)
        returned_low, arrived_low, cross_part = pin((returned_low, arrived_low, cross_part))
        low_low, sums_low = second_back(
            1, query_back, returned_low, after_self, grad_cross_in, scales
        )
        self_grads = self_back(packed, low_low, arrived_low, w_out, self_probs)
        self_grads, down_keep, up_keep = pin((self_grads, down[1], up[1]))
        down = onward([down_keep], [down[0]], 4)
        up = onward([up_keep], [up[0]], 2)
        self_grads, down, up = pin((self_grads, down, up))
        parts = grad_group(
            order,
            ((first,), (self_grads,), (back_mixed, near), (low_top, low_low)),
            ((0, 1, 0, 2), (0, 1, 1, 0), (0, 1, 2, 1), (2, 3, None, 3)),
            "gself",
        )
        parts, cross_keep, down_keep = pin((parts, cross_part[1], down[1]))
        (grad_down,) = last_sum(down_keep, swap(down[0], 8), [(192, width)])
        cross_part = onward([cross_keep], [cross_part[0]], 2)
        cross_part, up_keep = pin((cross_part, up[1]))
        up = onward([up_keep], [up[0]], 4)
        sends, keeps = [p[0] for p in parts], [p[1] for p in parts]
        keeps, up = pin((keeps, up))
        pair_part = onward(keeps[:2], sends[:2], 1)
        rest_part = onward(keeps[2:], sends[2:], 1)
        pair_part, rest_part, cross_part, up, self_grads, grad_down = pin(
            (pair_part, rest_part, cross_part, up, self_grads, grad_down)
        )
        input_stay, input_gone, sums_one = first_back(
            self_grads, w_qkv, moved, low_low, arrived_low, scales
        )
        sums_one, pair_keep, cross_keep = pin((sums_one, pair_part[1], cross_part[1]))
        input_top = lax.ppermute(input_gone, both, back)
        sums = jnp.concatenate(
            [sums_one[:2], sums_top[:2] + sums_low[:2], sums_three[:3], up_bias.reshape(4, width)]
        )
        sums = sums + swap(sums, 1)
        pair_part = onward([pair_keep], [pair_part[0]], 2)
        cross_part = onward([cross_keep], [cross_part[0]], 4)
        (grad_up,) = last_sum(up[1], swap(up[0], 8), [(48, 4 * width)])
        pair_part, cross_part, sums, rest_keep, grad_up = pin(
            (pair_part, cross_part, sums, rest_part[1], grad_up)
        )
        rest_part = onward([rest_keep], [rest_part[0]], 2)
        pair_part = onward([pair_part[1]], [pair_part[0]], 4)
        sums = sums + swap(sums, 2)
        rest_part, pair_part, sums = pin((rest_part, pair_part, sums))
        rest_part = onward([rest_part[1]], [rest_part[0]], 4)
        (grad_pair,) = last_sum(pair_part[1], swap(pair_part[0], 8), [(48, 2 * width)])
        grad_cross, grad_query, grad_keyval = last_sum(
            cross_part[1],
            swap(cross_part[0], 8),
            [(48, width), (48, width), (48, 2 * width)],
        )
        sums = sums + swap(sums, 4)
        rest_part, grad_pair, grad_cross, grad_query, grad_keyval, sums = pin(
            (rest_part, grad_pair, grad_cross, grad_query, grad_keyval, sums)
        )
        grad_first, grad_out = last_sum(
            rest_part[1], swap(rest_part[0], 8), [(48, width), (48, width)]
        )
        sums = sums + swap(sums, 8)
        grad_qkv = jnp.concatenate([grad_first, grad_pair], 1)
        mine = lax.dynamic_slice_in_dim(sums[:7], device * share, share, 1)
        gains, biases = mine[0:6:2], mine[1:6:2]
        down_bias = mine[6]
        up_bias = lax.dynamic_slice_in_dim(sums[7:].reshape(-1), device * 192, 192)
        input_grad = jnp.concatenate([input_top, input_stay])
    else:
        _, unit_two, inverse_two = layer_norm(after_self, scales[1], shifts[1])
        after_cross = after_self + matmul(cross_mixed, w_cross[0])
        third, unit_three, inverse_three = layer_norm(after_cross, scales[2], shifts[2])
        value, slope = gelu_pair(matmul(third, w_up[0]) + b_up[0])
        hidden = value.astype(jnp.bfloat16)
        output = (after_cross + matmul(hidden, w_down[0]) + b_down[0]).astype(jnp.bfloat16)
        upstream = dy.astype(jnp.float32)
        pre_low = (dot_nt(dy, w_down[0]) * slope).astype(jnp.bfloat16)
        back_three, gain_three, shift_three = norm_back(
            dot_nt(pre_low, w_up[0]), unit_three, inverse_three, scales[2]
        )
        grad_cross_in = upstream + back_three
        cross_low = grad_cross_in.astype(jnp.bfloat16)
        grad_cmix = dot_nt(cross_low, w_cross[0]).astype(jnp.bfloat16)
        cross_grads = attn_bwd(
            cross_q, cross_pair, cross_pair, 0, 0, 6, grad_cmix, cross_probs, "crossb"
        )
        pair = jnp.concatenate([cross_grads[1], cross_grads[2]], 1)
        returned = partner_of(dot_nt(pair, w_keyval[0]).astype(jnp.bfloat16))
        back_two, gain_two, shift_two = norm_back(
            dot_nt(cross_grads[0], w_query[0]) + returned.astype(jnp.float32),
            unit_two,
            inverse_two,
            scales[1],
        )
        self_low = (grad_cross_in + back_two).astype(jnp.bfloat16)
        moved_low = jnp.concatenate([self_low[half:], lax.ppermute(self_low[:half], both, forth)])
        grad_smix = dot_nt(moved_low, w_out[0]).astype(jnp.bfloat16)
        self_grads = attn_bwd(packed, packed, packed, 0, 6, 12, grad_smix, self_probs, "selfb")
        packed_grad = jnp.concatenate([self_grads[0], self_grads[1], self_grads[2]], 1)
        back_one, gain_one, shift_one = norm_back(
            dot_nt(packed_grad, w_qkv[0]), unit_one, inverse_one, scales[0]
        )
        moved_grad = (moved_low.astype(jnp.float32) + back_one).astype(jnp.bfloat16)
        input_grad = jnp.concatenate([lax.ppermute(moved_grad[half:], both, back), moved_grad[:half]])

        def summed(grad):
            return lax.psum_scatter(grad, "page", scatter_dimension=0, tiled=True)

        def scattered(left, right):
            return summed(
                lax.dot_general(
                    left, right, (((0,), (0,)), ((), ())), preferred_element_type=jnp.float32
                )
            )

        grad_down = scattered(hidden, dy)
        grad_up = scattered(third, pre_low)
        grad_cross = scattered(cross_mixed, cross_low)
        grad_query = scattered(second, cross_grads[0])
        grad_keyval = scattered(partner, pair)
        grad_out = scattered(jnp.concatenate([back_mixed, near]), self_low)
        grad_qkv = scattered(first, packed_grad)
        gains = summed(jnp.stack([gain_one, gain_two, gain_three], 1)).T
        biases = summed(jnp.stack([shift_one, shift_two, shift_three], 1)).T
        down_bias = summed(jnp.sum(upstream, axis=0))
        up_bias = summed(jnp.sum(pre_low.astype(jnp.float32), axis=0))
    return (
        output[None],
        input_grad[None],
        gains.T[None],
        biases.T[None],
        grad_qkv[None],
        grad_out[None],
        grad_query[None],
        grad_keyval[None],
        grad_cross[None],
        grad_up[None],
        up_bias[None],
        grad_down[None],
        down_bias[None],
    )


def solution(mesh):
    tokens = P("stream", "page", None)
    whole = P("stream", None, None)
    placed = (tokens, tokens) + (whole,) * 8 + (P("stream", None), whole, P("stream", None))
    return jax.shard_map(
        on_device,
        mesh=mesh,
        in_specs=placed + (P(), P("page")),
        out_specs=(tokens,) * 10 + (P("stream", "page"), tokens, P("stream", "page")),
        check_vma=False,
    )
```

```python
import functools

import jax
import jax.numpy as jnp
from jax import lax
from jax.experimental import pallas as pl
from jax.experimental.pallas import tpu as pltpu
from jax.sharding import PartitionSpec as P

HEADS = 12
HEAD = 64
WIN = 12
SHIFT = 6
NORM_EPS = 1e-05
MASKED = -1e30


def dot_nt(a,b):
    return lax.dot_general(a,b,(((1,),(1,)),((),())),preferred_element_type=jnp.float32)
def dot_nn(a,b):
    return lax.dot_general(a,b,(((1,),(0,)),((),())),preferred_element_type=jnp.float32)

def fill_self_bias(info, bias, first=0):
    tokens, count = bias.shape
    half=tokens//2
    cols=tokens//12
    def codes(shape,dim,start):
        t=lax.broadcasted_iota(jnp.int32,shape,dim)+start
        row=jnp.zeros(shape,jnp.int32)
        page=jnp.full(shape,info[2],jnp.int32)
        for r in range(1,12):
            inside=t>=r*cols
            row=jnp.where(inside,r,row)
            page=jnp.where(inside,info[2+r],page)
        c=t-row*cols
        win=jnp.zeros(shape,jnp.int32)
        for w in range(1,cols//12):
            win=jnp.where((c>=6+12*(w-1))&(c<6+12*w),w,win)
        win=jnp.where(c>=cols-6,cols//12+1,win)
        slot=jnp.where(t<half,t+half,t-half)
        return page*16+win,slot
    ck,sk=codes((tokens,1),0,0)
    cq,sq=codes((1,count),1,first)
    length=info[1]
    @pl.when(info[0]==1)
    def _():
        ok=(sk<=sq)&(sk<length)
        bias[...]=jnp.where(ok,0.0,MASKED)
    @pl.when(info[0]==0)
    def _():
        bias[...]=jnp.where(ck==cq,0.0,MASKED)

def fill_cross_bias(info,bias,first=0):
    tokens=bias.shape[0]
    t=lax.broadcasted_iota(jnp.int32,bias.shape,0)
    bias[...]=jnp.where((t<info[1])|(info[0]==1),0.0,MASKED)

def lane_pick(e,scale):
    lane=lax.broadcasted_iota(jnp.int32,(1,2*HEAD),1)
    return jnp.where((lane>=HEAD)==bool(e),scale,0.0).astype(jnp.bfloat16)

def fwd_kernel(fill, info, q_ref, k_ref, v_ref, o_ref, p_ref, bias):
    @pl.when(pl.program_id(0) == 0)
    def _():
        fill(info, bias)

    q, k = q_ref[...], k_ref[...]
    vt = v_ref[...].T
    scores = [dot_nt(k, q * lane_pick(e, HEAD**-0.5)) + bias[...] for e in range(2)]
    outs = []
    for e in range(2):
        weights = jnp.exp(scores[e] - jnp.max(scores[e], axis=0, keepdims=True))
        inverse = 1.0 / jnp.sum(weights, axis=0, keepdims=True)
        probs = (weights * inverse).astype(jnp.bfloat16)
        p_ref[e] = probs
        outs.append(dot_nn(vt[e * HEAD : (e + 1) * HEAD], probs))
    o_ref[...] = jnp.concatenate(outs, 0).T.astype(jnp.bfloat16)


NOTHING = pl.CostEstimate(flops=1000, bytes_accessed=1000, transcendentals=0)


def attn_fwd(info, q, k, v, qo, ko, vo, fill, name):
    tokens = q.shape[0]
    spec = lambda off: pl.BlockSpec((tokens, 128), lambda j, info: (0, off + j))
    return pl.pallas_call(
        functools.partial(fwd_kernel, fill),
        grid_spec=pltpu.PrefetchScalarGridSpec(
            num_scalar_prefetch=1,
            grid=(HEADS // 2,),
            in_specs=[spec(qo), spec(ko), spec(vo)],
            out_specs=[spec(0), pl.BlockSpec((2, tokens, tokens), lambda j, info: (j, 0, 0))],
            scratch_shapes=[pltpu.VMEM((tokens, tokens), jnp.float32)],
        ),
        out_shape=[
            jax.ShapeDtypeStruct((tokens, HEADS * HEAD), jnp.bfloat16),
            pltpu.HBM((HEADS, tokens, tokens), jnp.bfloat16),
        ],
        compiler_params=pltpu.CompilerParams(vmem_limit_bytes=24 * 2**20),
        cost_estimate=NOTHING,
        name=name,
    )(info, q, k, v)


def bwd_kernel(q_ref, k_ref, v_ref, do_ref, p_ref, d_ref):
    grads = backward_heads(q_ref[...], k_ref[...], v_ref[...], do_ref[...], p_ref)
    for i in range(3):
        d_ref[i] = grads[i]


def attn_bwd(q, k, v, qo, ko, vo, do, probs, name):
    tokens = q.shape[0]
    spec = lambda off: pl.BlockSpec((tokens, 128), lambda j: (0, off + j))
    return pl.pallas_call(
        bwd_kernel,
        grid=(HEADS // 2,),
        in_specs=[spec(qo), spec(ko), spec(vo), spec(0)]
        + [pl.BlockSpec((2, tokens, tokens), lambda j: (j, 0, 0))],
        out_specs=pl.BlockSpec((3, tokens, 128), lambda j: (0, 0, j)),
        out_shape=jax.ShapeDtypeStruct((3, tokens, HEADS * HEAD), jnp.bfloat16),
        compiler_params=pltpu.CompilerParams(vmem_limit_bytes=24 * 2**20),
        cost_estimate=NOTHING,
        name=name,
    )(q, k, v, do, pltpu.with_memory_space_constraint(probs, pltpu.HBM))


def layer_norm(inputs, scales, shifts):
    average = jnp.mean(inputs, axis=1, keepdims=True)
    centred = inputs - average
    spread = jnp.mean(centred * centred, axis=1, keepdims=True)
    inverse = lax.rsqrt(spread + NORM_EPS)
    unit = centred * inverse
    return (unit * scales + shifts).astype(jnp.bfloat16), unit, inverse


def norm_back(upstream, unit, inverse, scales):
    scaled = upstream * scales
    inner = (
        scaled
        - jnp.mean(scaled, axis=1, keepdims=True)
        - unit * jnp.mean(scaled * unit, axis=1, keepdims=True)
    )
    return (inverse * inner, jnp.sum(upstream * unit, axis=0), jnp.sum(upstream, axis=0))


def matmul(left, right):
    return jnp.dot(left, right, preferred_element_type=jnp.float32)


def gelu_pair(pre):
    root = 0.7978845608028654
    square = pre * pre
    gate = 0.5 + 0.5 * jnp.tanh(pre * (root + root * 0.044715 * square))
    value = pre * gate
    return value, gate + value * (1.0 - gate) * (2 * root + 6 * root * 0.044715 * square)


def layer_parts(v):
    average = jnp.mean(v, axis=1, keepdims=True)
    centred = v - average
    inverse = lax.rsqrt(jnp.mean(centred * centred, axis=1, keepdims=True) + NORM_EPS)
    return centred * inverse, inverse


def layer_back(grad, unit, inverse, scale):
    scaled = grad * scale
    return inverse * (
        scaled
        - jnp.mean(scaled, axis=1, keepdims=True)
        - unit * jnp.mean(scaled * unit, axis=1, keepdims=True)
    )


def column_sums(*values):
    rows = [jnp.sum(v, axis=0, keepdims=True) for v in values]
    rows.append(jnp.zeros((8 - len(rows), rows[0].shape[1]), jnp.float32))
    return jnp.concatenate(rows)


def sort_rows(order, x, across, sorted_rows):
    rows = sorted_rows.shape[0] // 16
    across[...] = x.T
    for n in range(16):
        start = pl.multiple_of(order[n] * rows, 16)
        sorted_rows[n * rows : (n + 1) * rows, :] = across[pl.ds(start, rows), :]


def feed_kernel(
    order, after_ref, mixed_ref, dy_ref, scales_ref, shifts_ref, cross_ref, down_bias_ref,
    up_ref, up_bias_ref, down_ref,
    out_ref, grad_ref, kept_ref, bias_ref,
    down_send, down_keep, up_send, up_keep,
    third_rows, across, sorted_rows, after, total, grad_total,
):
    step = pl.program_id(0)
    rows = dy_ref.shape[1] // 16
    half = 8 * rows

    @pl.when(step == 0)
    def _():
        after[...] = after_ref[...] + dot_nn(mixed_ref[...], cross_ref[0])
        unit = layer_parts(after[...])[0]
        third_rows[...] = (unit * scales_ref[2:3, :] + shifts_ref[2:3, :]).astype(jnp.bfloat16)
        sort_rows(order, third_rows[...], across, sorted_rows)
        total[...] = after[...] + down_bias_ref[...]
        grad_total[...] = jnp.zeros_like(grad_total)

    dy, third = dy_ref[...], third_rows[...]
    tile = up_ref.shape[2] // 2
    deep = tile // 2
    parts = [slice(0, tile), slice(tile, 2 * tile)]
    pre = [dot_nn(third, up_ref[0, :, p]) + up_bias_ref[:, p] for p in parts]
    grad_hidden = [dot_nt(dy, down_ref[0, p, :]) for p in parts]
    out = grad_third = 0.0
    grads = []
    for i, p in enumerate(parts):
        value, slope = gelu_pair(pre[i])
        hidden = value.astype(jnp.bfloat16)
        low = (grad_hidden[i] * slope).astype(jnp.bfloat16)
        bias_ref[0, :, p] = jnp.sum(low.astype(jnp.float32), axis=0, keepdims=True)
        grad = dot_nn(sorted_rows[...], low).astype(jnp.bfloat16)
        up_send[:, :, p] = grad[:half].reshape(8, rows, tile)
        up_keep[:, :, p] = grad[half:].reshape(8, rows, tile)
        grads.append(dot_nn(hidden.T, dy).astype(jnp.bfloat16))
        out += dot_nn(hidden, down_ref[0, p, :])
        grad_third += dot_nt(low, up_ref[0, :, p])
    total[...] += out
    grad_total[...] += grad_third
    for odd in range(2):
        for far in range(2):

            @pl.when((order[15] % 2 == odd) & (order[15] // 2 % 2 == far))
            def _():
                for n in range(2):
                    both = grads[n ^ far ^ 1]
                    down_send[n] = both[deep * (1 - odd) : deep * (2 - odd)]
                    down_keep[n] = both[deep * odd : deep * (odd + 1)]

    @pl.when(step == pl.num_programs(0) - 1)
    def _():
        out_ref[...] = total[...].astype(jnp.bfloat16)
        grad_ref[...] = grad_total[...]
        kept_ref[...] = after[...]


def third_kernel(third_ref, after_ref, dy_ref, scales_ref, cross_ref, grad_ref, low_ref, mix_ref, sums_ref):
    upstream = dy_ref[...].astype(jnp.float32)
    unit, inverse = layer_parts(after_ref[...])
    grad = third_ref[...]
    sums_ref[...] = column_sums(grad * unit, grad, upstream)
    grad_ref[...] = upstream + layer_back(grad, unit, inverse, scales_ref[2:3, :])
    low_ref[...] = grad_ref[...].astype(jnp.bfloat16)
    mix_ref[...] = dot_nt(low_ref[...], cross_ref[0]).astype(jnp.bfloat16)


def third_back(grad, after, dy, scales, w_cross):
    full = jax.ShapeDtypeStruct(after.shape, jnp.float32)
    low = jax.ShapeDtypeStruct(after.shape, jnp.bfloat16)
    return pl.pallas_call(
        third_kernel,
        out_shape=[full, low, low, jax.ShapeDtypeStruct((8, after.shape[1]), jnp.float32)],
        compiler_params=pltpu.CompilerParams(vmem_limit_bytes=32 * 2**20),
        cost_estimate=NOTHING,
        name="third",
    )(grad, after, dy, scales, w_cross)


def feed_forward(order, after, mixed, dy, scales, shifts, w_cross, w_up, b_up, w_down, b_down):
    tokens, width = dy.shape
    deep = w_up.shape[2]
    tile = deep // 4
    rows = width // 16
    whole = lambda *shape: pl.BlockSpec(shape, lambda j, order: (0,) * len(shape))
    where = lambda j, order: order[8 + j] // 4
    token = whole(tokens, width)
    down_half = jax.ShapeDtypeStruct((8, deep // 16, width), jnp.bfloat16)
    up_half = jax.ShapeDtypeStruct((8, 4 * rows, tile), jnp.bfloat16)
    down_piece = pl.BlockSpec((2, deep // 16, width), lambda j, order: (j, 0, 0))
    up_piece = pl.BlockSpec((8, rows, tile), lambda j, order: (0, where(j, order), 0))
    low = jax.ShapeDtypeStruct((tokens, width), jnp.bfloat16)
    full = jax.ShapeDtypeStruct((tokens, width), jnp.float32)
    out = pl.pallas_call(
        feed_kernel,
        grid_spec=pltpu.PrefetchScalarGridSpec(
            num_scalar_prefetch=1,
            grid=(4,),
            in_specs=[
                token,
                token,
                token,
                whole(3, width),
                whole(3, width),
                whole(1, width, width),
                whole(1, width),
                pl.BlockSpec((1, width, tile), lambda j, order: (0, 0, where(j, order))),
                pl.BlockSpec((1, tile), lambda j, order: (0, where(j, order))),
                pl.BlockSpec((1, tile, width), lambda j, order: (0, where(j, order), 0)),
            ],
            out_specs=[
                token,
                token,
                token,
                pl.BlockSpec((1, 1, tile), lambda j, order: (where(j, order), 0, 0)),
                down_piece,
                down_piece,
                up_piece,
                up_piece,
            ],
            scratch_shapes=[pltpu.VMEM((tokens, width), jnp.bfloat16)]
            + [pltpu.VMEM((width, tokens), jnp.bfloat16)] * 2
            + [pltpu.VMEM((tokens, width), jnp.float32)] * 3,
        ),
        out_shape=[
            low,
            full,
            full,
            jax.ShapeDtypeStruct((4, 1, tile), jnp.float32),
            down_half,
            down_half,
            up_half,
            up_half,
        ],
        compiler_params=pltpu.CompilerParams(vmem_limit_bytes=48 * 2**20),
        cost_estimate=NOTHING,
        name="feed",
    )(order, after, mixed, dy, scales, shifts, w_cross, b_down, w_up, b_up, w_down)
    return (*out[:4], (out[4], out[5]), (out[6], out[7]))


def backward_heads(q, k, v, do, p_ref):
    kt = k.T
    queries = []
    keys = values = 0.0
    picked = [do * lane_pick(e, 1.0) for e in range(2)]
    grads = [dot_nt(v, picked[e]) for e in range(2)]
    for e in range(2):
        probs = p_ref[e]
        wide = probs.astype(jnp.float32)
        part = wide * grads[e]
        total = jnp.sum(part, axis=0, keepdims=True)
        ds = (part - wide * total).astype(jnp.bfloat16)
        values += dot_nn(probs, picked[e])
        keys += dot_nn(ds, q * lane_pick(e, HEAD**-0.5))
        queries.append(dot_nn(kt[e * HEAD : (e + 1) * HEAD], ds) * HEAD**-0.5)
    queries = jnp.concatenate(queries, 0).T
    return [g.astype(jnp.bfloat16) for g in (queries, keys, values)]


def self_back_kernel(q_ref, k_ref, v_ref, near_ref, far_ref, out_ref, p_ref, d_ref):
    low = jnp.concatenate([near_ref[...], far_ref[...]])
    do = dot_nt(low, out_ref[0]).astype(jnp.bfloat16)
    grads = backward_heads(q_ref[...], k_ref[...], v_ref[...], do, p_ref)
    for i in range(3):
        d_ref[i] = grads[i]


def self_back(packed, near, far, w_out, probs):
    tokens, width = packed.shape[0], near.shape[1]
    spec = lambda off: pl.BlockSpec((tokens, 128), lambda j: (0, off + j))
    rows = pl.BlockSpec(near.shape, lambda j: (0, 0))
    return pl.pallas_call(
        self_back_kernel,
        grid=(HEADS // 2,),
        in_specs=[spec(0), spec(6), spec(12), rows, rows]
        + [pl.BlockSpec((1, 128, width), lambda j: (0, j, 0))]
        + [pl.BlockSpec((2, tokens, tokens), lambda j: (j, 0, 0))],
        out_specs=pl.BlockSpec((3, tokens, 128), lambda j: (0, 0, j)),
        out_shape=jax.ShapeDtypeStruct((3, tokens, width), jnp.bfloat16),
        compiler_params=pltpu.CompilerParams(vmem_limit_bytes=24 * 2**20),
        cost_estimate=NOTHING,
        name="selfb",
    )(packed, packed, packed, near, far, w_out, pltpu.with_memory_space_constraint(probs, pltpu.HBM))


def second_kernel(back_ref, returned_ref, after_ref, grad_ref, scales_ref, low_ref, sums_ref):
    unit, inverse = layer_parts(after_ref[...])
    grad = back_ref[...] + returned_ref[...].astype(jnp.float32)
    sums_ref[...] = column_sums(grad * unit, grad)
    back = layer_back(grad, unit, inverse, scales_ref[1:2, :])
    low_ref[...] = (grad_ref[...] + back).astype(jnp.bfloat16)


def second_back(which, back, returned, after, grad, scales):
    half, width = returned.shape
    rows = pl.BlockSpec((half, width), lambda j: (which, 0))
    first = pl.BlockSpec((half, width), lambda j: (0, 0))
    return pl.pallas_call(
        second_kernel,
        grid=(1,),
        in_specs=[rows, first, rows, rows, pl.BlockSpec((3, width), lambda j: (0, 0))],
        out_specs=[first, pl.BlockSpec((8, width), lambda j: (0, 0))],
        out_shape=[
            jax.ShapeDtypeStruct((half, width), jnp.bfloat16),
            jax.ShapeDtypeStruct((8, width), jnp.float32),
        ],
        compiler_params=pltpu.CompilerParams(vmem_limit_bytes=24 * 2**20),
        cost_estimate=NOTHING,
        name="second",
    )(back, returned, after, grad, scales)


def tail_kernel(
    order, d_ref, w_ref, first_ref, top_ref, bottom_ref, moved_ref, near_ref, far_ref, scales_ref, swapped_ref,
    *refs,
):
    step = pl.program_id(0)
    stay_ref, gone_ref, sums_ref = refs[8:11]
    across, sorted_rows, total = refs[11:]
    half = sorted_rows.shape[0] // 2

    @pl.when(step == 0)
    def _():
        sort_rows(order, first_ref[...], across, sorted_rows)

    for i in range(3):

        @pl.when(step == i)
        def _():
            part = dot_nt(d_ref[0], w_ref[0])
            grad = dot_nn(sorted_rows[...], d_ref[0]).astype(jnp.bfloat16)
            refs[2 * i][...] = grad[:half].reshape(refs[0].shape)
            refs[2 * i + 1][...] = grad[half:].reshape(refs[0].shape)
            if i == 0:
                total[...] = part
            else:
                total[...] += part

    @pl.when(step == 3)
    def _():
        mixed = jnp.concatenate([top_ref[...], bottom_ref[...]])
        sort_rows(order, mixed, across, sorted_rows)
        low = jnp.concatenate([swapped_ref[...], near_ref[...]])
        grad = dot_nn(sorted_rows[...], low).astype(jnp.bfloat16)
        refs[6][...] = grad[:half].reshape(refs[0].shape)
        refs[7][...] = grad[half:].reshape(refs[0].shape)
        rows = stay_ref.shape[0]
        unit, inverse = layer_parts(moved_ref[...].astype(jnp.float32))
        grad = total[...]
        sums_ref[...] = column_sums(grad * unit, grad)
        back = layer_back(grad, unit, inverse, scales_ref[0:1, :])
        stay_ref[...] = (near_ref[...].astype(jnp.float32) + back[:rows]).astype(jnp.bfloat16)
        gone_ref[...] = (far_ref[...].astype(jnp.float32) + back[rows:]).astype(jnp.bfloat16)


def tail_grads(order, grads, w_qkv, first, top, bottom, moved, near, far, scales, swapped):
    tokens, width = moved.shape
    half = tokens // 2
    whole = lambda *shape: pl.BlockSpec(shape, lambda j, order: (0,) * len(shape))
    rows = jax.ShapeDtypeStruct((half, width), jnp.bfloat16)
    piece = (8, width // 16, width)
    last = lambda j: jnp.minimum(j, 2)
    outs = pl.pallas_call(
        tail_kernel,
        grid_spec=pltpu.PrefetchScalarGridSpec(
            num_scalar_prefetch=1,
            grid=(4,),
            in_specs=[
                pl.BlockSpec((1, tokens, width), lambda j, order: (last(j), 0, 0)),
                pl.BlockSpec((1, width, width), lambda j, order: (0, 0, last(j))),
                whole(tokens, width),
                whole(half, width),
                whole(half, width),
                whole(tokens, width),
                whole(half, width),
                whole(half, width),
                whole(3, width),
                whole(half, width),
            ],
            out_specs=[whole(*piece)] * 8 + [whole(half, width)] * 2 + [whole(8, width)],
            scratch_shapes=[pltpu.VMEM((width, tokens), jnp.bfloat16)] * 2
            + [pltpu.VMEM((tokens, width), jnp.float32)],
        ),
        out_shape=[jax.ShapeDtypeStruct(piece, jnp.bfloat16)] * 8
        + [rows, rows, jax.ShapeDtypeStruct((8, width), jnp.float32)],
        compiler_params=pltpu.CompilerParams(vmem_limit_bytes=40 * 2**20),
        cost_estimate=NOTHING,
        name="tail",
    )(order, grads, w_qkv, first, top, bottom, moved, near, far, scales, swapped)
    return [(outs[i], outs[i + 1]) for i in range(0, 8, 2)], *outs[8:]


def group_kernel(plan, halves, pieces, order, *refs):
    refs = list(refs)
    groups = [[refs.pop(0) for _ in range(n)] for n in halves]
    joined = lambda group: jnp.concatenate([r[...] for r in group]) if len(group) > 1 else group[0][...]
    outs, (across, sorted_rows) = refs[:-2], refs[-2:]
    half = sorted_rows.shape[0] // 2
    before = None
    for i, (x, dy, lead, target) in enumerate(plan):
        turn = x != before
        before = x

        @pl.when(pl.program_id(0) == i)
        def _():
            if turn:
                sort_rows(order, joined(groups[x]), across, sorted_rows)
            right = joined(groups[dy]) if lead is None else groups[dy][0][0]
            grad = dot_nn(sorted_rows[...], right).astype(jnp.bfloat16)
            send_ref, keep_ref = outs[2 * target], outs[2 * target + 1]
            send_ref[...] = grad[:half].reshape(send_ref.shape)
            keep_ref[...] = grad[half:].reshape(keep_ref.shape)


def grad_group(order, operands, plan, name):
    width = operands[0][0].shape[-1]
    rows = width // 16
    tokens = sum(a.shape[-2] for a in operands[0])
    in_specs = []
    for n, group in enumerate(operands):
        for a in group:
            if a.ndim == 2:
                in_specs.append(pl.BlockSpec(a.shape, lambda j, order: (0, 0)))
            else:
                first = min(i for i, p in enumerate(plan) if p[1] == n)
                in_specs.append(
                    pl.BlockSpec(
                        (1, *a.shape[1:]),
                        lambda j, order, first=first, last=a.shape[0] - 1: (
                            jnp.clip(j - first, 0, last),
                            0,
                            0,
                        ),
                    )
                )
    out_specs, out_shape = [], []
    for target in range(1 + max(p[3] for p in plan)):
        steps = [i for i, p in enumerate(plan) if p[3] == target]
        spec = pl.BlockSpec(
            (8, rows, width),
            lambda j, order, first=steps[0], last=len(steps) - 1: (
                0,
                jnp.clip(j - first, 0, last),
                0,
            ),
        )
        out_specs += [spec, spec]
        out_shape += [jax.ShapeDtypeStruct((8, rows * len(steps), width), jnp.bfloat16)] * 2
    outs = pl.pallas_call(
        functools.partial(group_kernel, plan, [len(g) for g in operands], len(out_specs)),
        grid_spec=pltpu.PrefetchScalarGridSpec(
            num_scalar_prefetch=1,
            grid=(len(plan),),
            in_specs=in_specs,
            out_specs=out_specs,
            scratch_shapes=[pltpu.VMEM((width, tokens), jnp.bfloat16)] * 2,
        ),
        out_shape=out_shape,
        compiler_params=pltpu.CompilerParams(vmem_limit_bytes=32 * 2**20),
        cost_estimate=NOTHING,
        name=name,
    )(order, *[a for group in operands for a in group])
    return [(outs[i], outs[i + 1]) for i in range(0, len(outs), 2)]


def add_kernel(count, *refs):
    at = 0
    for n in range(count):
        keep, arrived = refs[2 * n], refs[2 * n + 1]
        rows = keep.shape[-2]
        for i, out in enumerate(refs[2 * count :]):
            out[0, at : at + rows, :] = keep[i, 0] + arrived[i, 0]
        at += rows


def add_halves(keeps, arrivals, name="add"):
    pairs = keeps[0].shape[0] // 2
    width = keeps[0].shape[2]
    rows = sum(k.shape[1] for k in keeps)
    operands = []
    for keep, arrived in zip(keeps, arrivals):
        operands += [a.reshape(2, pairs, *a.shape[1:]) for a in (keep, arrived)]
    out = pl.BlockSpec((1, rows, width), lambda j: (j, 0, 0))
    return pl.pallas_call(
        functools.partial(add_kernel, len(keeps)),
        grid=(pairs,),
        in_specs=[
            pl.BlockSpec((2, 1, *a.shape[2:]), lambda j: (0, j, 0, 0)) for a in operands
        ],
        out_specs=[out, out],
        out_shape=[jax.ShapeDtypeStruct((pairs, rows, width), jnp.bfloat16)] * 2,
        compiler_params=pltpu.CompilerParams(vmem_limit_bytes=16 * 2**20),
        cost_estimate=NOTHING,
        name=name,
    )(*operands)


def last_kernel(keep_ref, arrived_ref, *outs):
    total = keep_ref[0].astype(jnp.float32) + arrived_ref[0].astype(jnp.float32)
    width = total.shape[1]
    at = 0
    for out in outs:
        rows, columns = out.shape
        for n in range(columns // width):
            out[:, n * width : (n + 1) * width] = total[at : at + rows]
            at += rows


def last_sum(keep, arrived, shapes):
    return pl.pallas_call(
        last_kernel,
        out_shape=[jax.ShapeDtypeStruct(s, jnp.float32) for s in shapes],
        compiler_params=pltpu.CompilerParams(vmem_limit_bytes=16 * 2**20),
        cost_estimate=NOTHING,
        name="last",
    )(keep, arrived)


def swap(x, bit):
    return lax.ppermute(x, "page", [(i, i ^ bit) for i in range(16)])


pin = lax.optimization_barrier


def on_device(
    block_input,
    cotangent,
    norm_gain,
    norm_bias,
    w_qkv,
    w_out,
    w_query,
    w_keyval,
    w_cross,
    w_up,
    b_up,
    w_down,
    b_down,
    row_page,
    lengths,
):
    x = block_input[0]
    dy = cotangent[0]
    tokens, width = x.shape
    half = tokens // 2
    pages = lax.axis_size("page")
    device = lax.axis_index("page")
    stream = lax.axis_index("stream")
    scales = norm_gain[0].T
    shifts = norm_bias[0].T
    share = width // pages
    padded = jnp.concatenate([row_page, row_page[:SHIFT]])
    info = jnp.concatenate(
        [
            stream.astype(jnp.int32)[None],
            lengths,
            lax.dynamic_slice_in_dim(padded, device * WIN + SHIFT, WIN),
        ]
    )
    stay = [(pages + i, pages + i) for i in range(pages)]
    both = ("stream", "page")
    forth = [((i + 1) % pages, i) for i in range(pages)] + stay
    back = [(i, (i + 1) % pages) for i in range(pages)] + stay

    def partner_of(rows):
        return lax.ppermute(rows, "stream", [(0, 1), (1, 0)])

    moved = jnp.concatenate([x[half:], lax.ppermute(x[:half], both, forth)])
    first, unit_one, inverse_one = layer_norm(moved.astype(jnp.float32), scales[0], shifts[0])
    packed = matmul(first, w_qkv[0]).astype(jnp.bfloat16)
    moved_mixed, self_probs = attn_fwd(
        info, packed, packed, packed, 0, 6, 12, fill_self_bias, "selff"
    )
    gone, near = moved_mixed[half:], moved_mixed[:half]
    after_gone = moved[half:].astype(jnp.float32) + matmul(gone, w_out[0])
    second_gone = layer_norm(after_gone, scales[1], shifts[1])[0]
    partner_top = lax.ppermute(
        second_gone,
        both,
        [(i, pages + (i + 1) % pages) for i in range(pages)]
        + [(pages + i, i) for i in range(pages)],
    )
    back_mixed = lax.ppermute(gone, both, back)
    after_low = moved[:half].astype(jnp.float32) + matmul(near, w_out[0])
    second_low = layer_norm(after_low, scales[1], shifts[1])[0]
    partner_low = partner_of(second_low)
    back_mixed, second_low, partner_top = pin((back_mixed, second_low, partner_top))
    after_top = x[:half].astype(jnp.float32) + matmul(back_mixed, w_out[0])
    second_top = layer_norm(after_top, scales[1], shifts[1])[0]
    after_self = jnp.concatenate([after_top, after_low])
    second = jnp.concatenate([second_top, second_low])
    cross_q = matmul(second, w_query[0]).astype(jnp.bfloat16)
    cross_q, after_self, partner_top, partner_low = pin(
        (cross_q, after_self, partner_top, partner_low)
    )
    partner = jnp.concatenate([partner_top, partner_low])
    cross_pair = matmul(partner, w_keyval[0]).astype(jnp.bfloat16)
    cross_mixed, cross_probs = attn_fwd(
        info, cross_q, cross_pair, cross_pair, 0, 0, 6, fill_cross_bias, "crossf"
    )
    if pages == 16:
        ordinal = jnp.arange(16, dtype=jnp.int32)
        turned = 15 - ordinal
        turned = (turned & 1) << 3 | (turned & 2) << 1 | (turned & 4) >> 1 | (turned & 8) >> 3
        order = device.astype(jnp.int32) ^ turned
        output, grad_third, after_cross, up_bias, down, up = feed_forward(
            order, after_self, cross_mixed, dy, scales, shifts, w_cross, w_up, b_up, w_down, b_down
        )
        grad_cross_in, cross_low, grad_cmix, sums_three = third_back(
            grad_third, after_cross, dy, scales, w_cross
        )

        def onward(keeps, sends, bit):
            return add_halves(keeps, [swap(s, bit) for s in sends])

        grad_cmix, down_keep = pin((grad_cmix, down[1]))
        down = onward([down_keep], [down[0]], 1)
        grad_cmix, down = pin((grad_cmix, down))
        cross_grads = attn_bwd(
            cross_q, cross_pair, cross_pair, 0, 0, 6, grad_cmix, cross_probs, "crossb"
        )

        def given(rows):
            keys = dot_nt(cross_grads[1, rows], w_keyval[0][:, :width])
            return (keys + dot_nt(cross_grads[2, rows], w_keyval[0][:, width:])).astype(jnp.bfloat16)

        returned_top = partner_of(given(slice(0, half)))
        returned_low = partner_of(given(slice(half, tokens)))
        query_back = dot_nt(cross_grads[0], w_query[0])
        (cross_part,) = grad_group(
            order,
            (
                (cross_mixed,),
                (second_top, second_low),
                (partner_top, partner_low),
                (cross_low,),
                (cross_grads,),
            ),
            ((0, 3, None, 0), (1, 4, 0, 0), (2, 4, 1, 0), (2, 4, 2, 0)),
            "gcross",
        )
        down = onward([down[1]], [down[0]], 4)
        up = onward([up[1]], [up[0]], 1)
        returned_top, cross_part, down, up = pin((returned_top, cross_part, down, up))
        low_top, sums_top = second_back(
            0, query_back, returned_top, after_self, grad_cross_in, scales
        )
        arrived_low = lax.ppermute(low_top, both, forth)
        low_top, cross_keep = pin((low_top, cross_part[1]))
        cross_part = onward([cross_keep], [cross_part[0]], 1)
        returned_low, arrived_low, cross_part = pin((returned_low, arrived_low, cross_part))
        low_low, sums_low = second_back(
            1, query_back, returned_low, after_self, grad_cross_in, scales
        )
        self_grads = self_back(packed, low_low, arrived_low, w_out, self_probs)
        self_grads, down_keep, up_keep = pin((self_grads, down[1], up[1]))
        down = onward([down_keep], [down[0]], 8)
        up = onward([up_keep], [up[0]], 2)
        self_grads, down, up = pin((self_grads, down, up))
        parts, input_stay, input_gone, sums_one = tail_grads(
            order, self_grads, w_qkv, first, back_mixed, near, moved, low_low, arrived_low, scales,
            low_top,
        )
        parts = [parts[1], parts[2], parts[0], parts[3]]
        parts, cross_keep, up_keep, down_keep = pin((parts, cross_part[1], up[1], down[1]))
        cross_part = onward([cross_keep], [cross_part[0]], 2)
        up = onward([up_keep], [up[0]], 4)
        sends, keeps = [p[0] for p in parts], [p[1] for p in parts]
        cross_part, keeps, up = pin((cross_part, keeps, up))
        pair_part = onward(keeps[:2], sends[:2], 1)
        rest_part = onward(keeps[2:], sends[2:], 1)
        pair_part, rest_part, cross_part, input_gone, up, sums_one = pin(
            (pair_part, rest_part, cross_part, input_gone, up, sums_one)
        )
        input_top = lax.ppermute(input_gone, both, back)
        sums = jnp.concatenate(
            [sums_one[:2], sums_top[:2] + sums_low[:2], sums_three[:3], up_bias.reshape(4, width)]
        )
        sums = sums + swap(sums, 1)
        pair_keep, sums = pin((pair_part[1], sums))
        pair_part = onward([pair_keep], [pair_part[0]], 2)
        cross_keep, up_keep, pair_part = pin((cross_part[1], up[1], pair_part))
        (grad_up,) = last_sum(up_keep, swap(up[0], 8), [(48, 4 * width)])
        cross_part = onward([cross_keep], [cross_part[0]], 4)
        cross_part, pair_keep, grad_up = pin((cross_part, pair_part[1], grad_up))
        pair_part = onward([pair_keep], [pair_part[0]], 4)
        pair_part, cross_keep = pin((pair_part, cross_part[1]))
        grad_cross, grad_query, grad_keyval = last_sum(
            cross_keep,
            swap(cross_part[0], 8),
            [(48, width), (48, width), (48, 2 * width)],
        )
        rest_keep, grad_cross, grad_query, grad_keyval = pin(
            (rest_part[1], grad_cross, grad_query, grad_keyval)
        )
        rest_part = onward([rest_keep], [rest_part[0]], 2)
        sums = sums + swap(sums, 2)
        rest_keep, pair_keep, sums = pin((rest_part[1], pair_part[1], sums))
        rest_part = onward([rest_keep], [rest_part[0]], 4)
        (grad_pair,) = last_sum(pair_keep, swap(pair_part[0], 8), [(48, 2 * width)])
        (grad_down,) = last_sum(down_keep, swap(down[0], 2), [(192, width)])
        sums = sums + swap(sums, 4)
        rest_part, sums, grad_pair, grad_down = pin((rest_part, sums, grad_pair, grad_down))
        grad_first, grad_out = last_sum(
            rest_part[1], swap(rest_part[0], 8), [(48, width), (48, width)]
        )
        sums = sums + swap(sums, 8)
        grad_qkv = jnp.concatenate([grad_first, grad_pair], 1)
        mine = lax.dynamic_slice_in_dim(sums[:7], device * share, share, 1)
        gains, biases = mine[0:6:2], mine[1:6:2]
        down_bias = mine[6]
        up_bias = lax.dynamic_slice_in_dim(sums[7:].reshape(-1), device * 192, 192)
        input_grad = jnp.concatenate([input_top, input_stay])
    else:
        _, unit_two, inverse_two = layer_norm(after_self, scales[1], shifts[1])
        after_cross = after_self + matmul(cross_mixed, w_cross[0])
        third, unit_three, inverse_three = layer_norm(after_cross, scales[2], shifts[2])
        value, slope = gelu_pair(matmul(third, w_up[0]) + b_up[0])
        hidden = value.astype(jnp.bfloat16)
        output = (after_cross + matmul(hidden, w_down[0]) + b_down[0]).astype(jnp.bfloat16)
        upstream = dy.astype(jnp.float32)
        pre_low = (dot_nt(dy, w_down[0]) * slope).astype(jnp.bfloat16)
        back_three, gain_three, shift_three = norm_back(
            dot_nt(pre_low, w_up[0]), unit_three, inverse_three, scales[2]
        )
        grad_cross_in = upstream + back_three
        cross_low = grad_cross_in.astype(jnp.bfloat16)
        grad_cmix = dot_nt(cross_low, w_cross[0]).astype(jnp.bfloat16)
        cross_grads = attn_bwd(
            cross_q, cross_pair, cross_pair, 0, 0, 6, grad_cmix, cross_probs, "crossb"
        )
        pair = jnp.concatenate([cross_grads[1], cross_grads[2]], 1)
        returned = partner_of(dot_nt(pair, w_keyval[0]).astype(jnp.bfloat16))
        back_two, gain_two, shift_two = norm_back(
            dot_nt(cross_grads[0], w_query[0]) + returned.astype(jnp.float32),
            unit_two,
            inverse_two,
            scales[1],
        )
        self_low = (grad_cross_in + back_two).astype(jnp.bfloat16)
        moved_low = jnp.concatenate([self_low[half:], lax.ppermute(self_low[:half], both, forth)])
        grad_smix = dot_nt(moved_low, w_out[0]).astype(jnp.bfloat16)
        self_grads = attn_bwd(packed, packed, packed, 0, 6, 12, grad_smix, self_probs, "selfb")
        packed_grad = jnp.concatenate([self_grads[0], self_grads[1], self_grads[2]], 1)
        back_one, gain_one, shift_one = norm_back(
            dot_nt(packed_grad, w_qkv[0]), unit_one, inverse_one, scales[0]
        )
        moved_grad = (moved_low.astype(jnp.float32) + back_one).astype(jnp.bfloat16)
        input_grad = jnp.concatenate([lax.ppermute(moved_grad[half:], both, back), moved_grad[:half]])

        def summed(grad):
            return lax.psum_scatter(grad, "page", scatter_dimension=0, tiled=True)

        def scattered(left, right):
            return summed(
                lax.dot_general(
                    left, right, (((0,), (0,)), ((), ())), preferred_element_type=jnp.float32
                )
            )

        grad_down = scattered(hidden, dy)
        grad_up = scattered(third, pre_low)
        grad_cross = scattered(cross_mixed, cross_low)
        grad_query = scattered(second, cross_grads[0])
        grad_keyval = scattered(partner, pair)
        grad_out = scattered(jnp.concatenate([back_mixed, near]), self_low)
        grad_qkv = scattered(first, packed_grad)
        gains = summed(jnp.stack([gain_one, gain_two, gain_three], 1)).T
        biases = summed(jnp.stack([shift_one, shift_two, shift_three], 1)).T
        down_bias = summed(jnp.sum(upstream, axis=0))
        up_bias = summed(jnp.sum(pre_low.astype(jnp.float32), axis=0))
    return (
        output[None],
        input_grad[None],
        gains.T[None],
        biases.T[None],
        grad_qkv[None],
        grad_out[None],
        grad_query[None],
        grad_keyval[None],
        grad_cross[None],
        grad_up[None],
        up_bias[None],
        grad_down[None],
        down_bias[None],
    )


def solution(mesh):
    tokens = P("stream", "page", None)
    whole = P("stream", None, None)
    placed = (tokens, tokens) + (whole,) * 8 + (P("stream", None), whole, P("stream", None))
    return jax.shard_map(
        on_device,
        mesh=mesh,
        in_specs=placed + (P(), P("page")),
        out_specs=(tokens,) * 10 + (P("stream", "page"), tokens, P("stream", "page")),
        check_vma=False,
    )
```

```python
import functools

import jax
import jax.numpy as jnp
from jax import lax
from jax.experimental import pallas as pl
from jax.experimental.pallas import tpu as pltpu
from jax.sharding import PartitionSpec as P

HEADS = 12
HEAD = 64
WIN = 12
SHIFT = 6
NORM_EPS = 1e-05
MASKED = -1e30


def dot_nt(a,b):
    return lax.dot_general(a,b,(((1,),(1,)),((),())),preferred_element_type=jnp.float32)
def dot_nn(a,b):
    return lax.dot_general(a,b,(((1,),(0,)),((),())),preferred_element_type=jnp.float32)

def fill_self_bias(info, bias, first=0):
    tokens, count = bias.shape
    half=tokens//2
    cols=tokens//12
    def codes(shape,dim,start):
        t=lax.broadcasted_iota(jnp.int32,shape,dim)+start
        row=jnp.zeros(shape,jnp.int32)
        page=jnp.full(shape,info[2],jnp.int32)
        for r in range(1,12):
            inside=t>=r*cols
            row=jnp.where(inside,r,row)
            page=jnp.where(inside,info[2+r],page)
        c=t-row*cols
        win=jnp.zeros(shape,jnp.int32)
        for w in range(1,cols//12):
            win=jnp.where((c>=6+12*(w-1))&(c<6+12*w),w,win)
        win=jnp.where(c>=cols-6,cols//12+1,win)
        slot=jnp.where(t<half,t+half,t-half)
        return page*16+win,slot
    ck,sk=codes((tokens,1),0,0)
    cq,sq=codes((1,count),1,first)
    length=info[1]
    @pl.when(info[0]==1)
    def _():
        ok=(sk<=sq)&(sk<length)
        bias[...]=jnp.where(ok,0.0,MASKED)
    @pl.when(info[0]==0)
    def _():
        bias[...]=jnp.where(ck==cq,0.0,MASKED)

def fill_cross_bias(info,bias,first=0):
    tokens=bias.shape[0]
    t=lax.broadcasted_iota(jnp.int32,bias.shape,0)
    bias[...]=jnp.where((t<info[1])|(info[0]==1),0.0,MASKED)

def lane_pick(e,scale):
    lane=lax.broadcasted_iota(jnp.int32,(1,2*HEAD),1)
    return jnp.where((lane>=HEAD)==bool(e),scale,0.0).astype(jnp.bfloat16)

def fwd_kernel(fill, info, q_ref, k_ref, v_ref, o_ref, p_ref, bias):
    @pl.when(pl.program_id(0) == 0)
    def _():
        fill(info, bias)

    q, k = q_ref[...], k_ref[...]
    vt = v_ref[...].T
    scores = [dot_nt(k, q * lane_pick(e, HEAD**-0.5)) + bias[...] for e in range(2)]
    outs = []
    for e in range(2):
        weights = jnp.exp(scores[e] - jnp.max(scores[e], axis=0, keepdims=True))
        inverse = 1.0 / jnp.sum(weights, axis=0, keepdims=True)
        probs = (weights * inverse).astype(jnp.bfloat16)
        p_ref[e] = probs
        outs.append(dot_nn(vt[e * HEAD : (e + 1) * HEAD], probs))
    o_ref[...] = jnp.concatenate(outs, 0).T.astype(jnp.bfloat16)


NOTHING = pl.CostEstimate(flops=1000, bytes_accessed=1000, transcendentals=0)


def attn_fwd(info, q, k, v, qo, ko, vo, fill, name):
    tokens = q.shape[0]
    spec = lambda off: pl.BlockSpec((tokens, 128), lambda j, info: (0, off + j))
    return pl.pallas_call(
        functools.partial(fwd_kernel, fill),
        grid_spec=pltpu.PrefetchScalarGridSpec(
            num_scalar_prefetch=1,
            grid=(HEADS // 2,),
            in_specs=[spec(qo), spec(ko), spec(vo)],
            out_specs=[spec(0), pl.BlockSpec((2, tokens, tokens), lambda j, info: (j, 0, 0))],
            scratch_shapes=[pltpu.VMEM((tokens, tokens), jnp.float32)],
        ),
        out_shape=[
            jax.ShapeDtypeStruct((tokens, HEADS * HEAD), jnp.bfloat16),
            pltpu.HBM((HEADS, tokens, tokens), jnp.bfloat16),
        ],
        compiler_params=pltpu.CompilerParams(vmem_limit_bytes=24 * 2**20),
        cost_estimate=NOTHING,
        name=name,
    )(info, q, k, v)


def bwd_kernel(q_ref, k_ref, v_ref, do_ref, p_ref, d_ref):
    grads = backward_heads(q_ref[...], k_ref[...], v_ref[...], do_ref[...], p_ref)
    for i in range(3):
        d_ref[i] = grads[i]


def attn_bwd(q, k, v, qo, ko, vo, do, probs, name):
    tokens = q.shape[0]
    spec = lambda off: pl.BlockSpec((tokens, 128), lambda j: (0, off + j))
    return pl.pallas_call(
        bwd_kernel,
        grid=(HEADS // 2,),
        in_specs=[spec(qo), spec(ko), spec(vo), spec(0)]
        + [pl.BlockSpec((2, tokens, tokens), lambda j: (j, 0, 0))],
        out_specs=pl.BlockSpec((3, tokens, 128), lambda j: (0, 0, j)),
        out_shape=jax.ShapeDtypeStruct((3, tokens, HEADS * HEAD), jnp.bfloat16),
        compiler_params=pltpu.CompilerParams(vmem_limit_bytes=24 * 2**20),
        cost_estimate=NOTHING,
        name=name,
    )(q, k, v, do, pltpu.with_memory_space_constraint(probs, pltpu.HBM))


def layer_norm(inputs, scales, shifts):
    average = jnp.mean(inputs, axis=1, keepdims=True)
    centred = inputs - average
    spread = jnp.mean(centred * centred, axis=1, keepdims=True)
    inverse = lax.rsqrt(spread + NORM_EPS)
    unit = centred * inverse
    return (unit * scales + shifts).astype(jnp.bfloat16), unit, inverse


def norm_back(upstream, unit, inverse, scales):
    scaled = upstream * scales
    inner = (
        scaled
        - jnp.mean(scaled, axis=1, keepdims=True)
        - unit * jnp.mean(scaled * unit, axis=1, keepdims=True)
    )
    return (inverse * inner, jnp.sum(upstream * unit, axis=0), jnp.sum(upstream, axis=0))


def matmul(left, right):
    return jnp.dot(left, right, preferred_element_type=jnp.float32)


def gelu_pair(pre):
    root = 0.7978845608028654
    square = pre * pre
    gate = 0.5 + 0.5 * jnp.tanh(pre * (root + root * 0.044715 * square))
    value = pre * gate
    return value, gate + value * (1.0 - gate) * (2 * root + 6 * root * 0.044715 * square)


def layer_parts(v):
    average = jnp.mean(v, axis=1, keepdims=True)
    centred = v - average
    inverse = lax.rsqrt(jnp.mean(centred * centred, axis=1, keepdims=True) + NORM_EPS)
    return centred * inverse, inverse


def layer_back(grad, unit, inverse, scale):
    scaled = grad * scale
    return inverse * (
        scaled
        - jnp.mean(scaled, axis=1, keepdims=True)
        - unit * jnp.mean(scaled * unit, axis=1, keepdims=True)
    )


def column_sums(*values):
    rows = [jnp.sum(v, axis=0, keepdims=True) for v in values]
    rows.append(jnp.zeros((8 - len(rows), rows[0].shape[1]), jnp.float32))
    return jnp.concatenate(rows)


def sort_rows(order, x, across, sorted_rows):
    rows = sorted_rows.shape[0] // 16
    across[...] = x.T
    for n in range(16):
        start = pl.multiple_of(order[n] * rows, 16)
        sorted_rows[n * rows : (n + 1) * rows, :] = across[pl.ds(start, rows), :]


def feed_kernel(
    order, after_ref, mixed_ref, dy_ref, scales_ref, shifts_ref, cross_ref, down_bias_ref,
    up_ref, up_bias_ref, down_ref,
    out_ref, grad_ref, kept_ref, bias_ref,
    down_send, down_keep, up_send, up_keep,
    third_rows, across, sorted_rows, after, total, grad_total,
):
    step = pl.program_id(0)
    rows = dy_ref.shape[1] // 16
    half = 8 * rows

    @pl.when(step == 0)
    def _():
        after[...] = after_ref[...] + dot_nn(mixed_ref[...], cross_ref[0])
        unit = layer_parts(after[...])[0]
        third_rows[...] = (unit * scales_ref[2:3, :] + shifts_ref[2:3, :]).astype(jnp.bfloat16)
        sort_rows(order, third_rows[...], across, sorted_rows)
        total[...] = after[...] + down_bias_ref[...]
        grad_total[...] = jnp.zeros_like(grad_total)

    dy, third = dy_ref[...], third_rows[...]
    tile = up_ref.shape[2] // 2
    deep = tile // 2
    parts = [slice(0, tile), slice(tile, 2 * tile)]
    pre = [dot_nn(third, up_ref[0, :, p]) + up_bias_ref[:, p] for p in parts]
    grad_hidden = [dot_nt(dy, down_ref[0, p, :]) for p in parts]
    out = grad_third = 0.0
    grads = []
    for i, p in enumerate(parts):
        value, slope = gelu_pair(pre[i])
        hidden = value.astype(jnp.bfloat16)
        low = (grad_hidden[i] * slope).astype(jnp.bfloat16)
        bias_ref[0, :, p] = jnp.sum(low.astype(jnp.float32), axis=0, keepdims=True)
        grad = dot_nn(sorted_rows[...], low).astype(jnp.bfloat16)
        up_send[:, :, p] = grad[:half].reshape(8, rows, tile)
        up_keep[:, :, p] = grad[half:].reshape(8, rows, tile)
        grads.append(dot_nn(hidden.T, dy).astype(jnp.bfloat16))
        out += dot_nn(hidden, down_ref[0, p, :])
        grad_third += dot_nt(low, up_ref[0, :, p])
    total[...] += out
    grad_total[...] += grad_third
    for odd in range(2):
        for far in range(2):

            @pl.when((order[15] % 2 == odd) & (order[15] // 2 % 2 == far))
            def _():
                for n in range(2):
                    both = grads[n ^ far ^ 1]
                    down_send[n] = both[deep * (1 - odd) : deep * (2 - odd)]
                    down_keep[n] = both[deep * odd : deep * (odd + 1)]

    @pl.when(step == pl.num_programs(0) - 1)
    def _():
        out_ref[...] = total[...].astype(jnp.bfloat16)
        grad_ref[...] = grad_total[...]
        kept_ref[...] = after[...]


def third_kernel(third_ref, after_ref, dy_ref, scales_ref, cross_ref, grad_ref, low_ref, mix_ref, sums_ref):
    upstream = dy_ref[...].astype(jnp.float32)
    unit, inverse = layer_parts(after_ref[...])
    grad = third_ref[...]
    sums_ref[...] = column_sums(grad * unit, grad, upstream)
    grad_ref[...] = upstream + layer_back(grad, unit, inverse, scales_ref[2:3, :])
    low_ref[...] = grad_ref[...].astype(jnp.bfloat16)
    mix_ref[...] = dot_nt(low_ref[...], cross_ref[0]).astype(jnp.bfloat16)


def third_back(grad, after, dy, scales, w_cross):
    full = jax.ShapeDtypeStruct(after.shape, jnp.float32)
    low = jax.ShapeDtypeStruct(after.shape, jnp.bfloat16)
    return pl.pallas_call(
        third_kernel,
        out_shape=[full, low, low, jax.ShapeDtypeStruct((8, after.shape[1]), jnp.float32)],
        compiler_params=pltpu.CompilerParams(vmem_limit_bytes=32 * 2**20),
        cost_estimate=NOTHING,
        name="third",
    )(grad, after, dy, scales, w_cross)


def feed_forward(order, after, mixed, dy, scales, shifts, w_cross, w_up, b_up, w_down, b_down):
    tokens, width = dy.shape
    deep = w_up.shape[2]
    tile = deep // 4
    rows = width // 16
    whole = lambda *shape: pl.BlockSpec(shape, lambda j, order: (0,) * len(shape))
    where = lambda j, order: order[8 + j] // 4
    token = whole(tokens, width)
    down_half = jax.ShapeDtypeStruct((8, deep // 16, width), jnp.bfloat16)
    up_half = jax.ShapeDtypeStruct((8, 4 * rows, tile), jnp.bfloat16)
    down_piece = pl.BlockSpec((2, deep // 16, width), lambda j, order: (j, 0, 0))
    up_piece = pl.BlockSpec((8, rows, tile), lambda j, order: (0, where(j, order), 0))
    low = jax.ShapeDtypeStruct((tokens, width), jnp.bfloat16)
    full = jax.ShapeDtypeStruct((tokens, width), jnp.float32)
    out = pl.pallas_call(
        feed_kernel,
        grid_spec=pltpu.PrefetchScalarGridSpec(
            num_scalar_prefetch=1,
            grid=(4,),
            in_specs=[
                token,
                token,
                token,
                whole(3, width),
                whole(3, width),
                whole(1, width, width),
                whole(1, width),
                pl.BlockSpec((1, width, tile), lambda j, order: (0, 0, where(j, order))),
                pl.BlockSpec((1, tile), lambda j, order: (0, where(j, order))),
                pl.BlockSpec((1, tile, width), lambda j, order: (0, where(j, order), 0)),
            ],
            out_specs=[
                token,
                token,
                token,
                pl.BlockSpec((1, 1, tile), lambda j, order: (where(j, order), 0, 0)),
                down_piece,
                down_piece,
                up_piece,
                up_piece,
            ],
            scratch_shapes=[pltpu.VMEM((tokens, width), jnp.bfloat16)]
            + [pltpu.VMEM((width, tokens), jnp.bfloat16)] * 2
            + [pltpu.VMEM((tokens, width), jnp.float32)] * 3,
        ),
        out_shape=[
            low,
            full,
            full,
            jax.ShapeDtypeStruct((4, 1, tile), jnp.float32),
            down_half,
            down_half,
            up_half,
            up_half,
        ],
        compiler_params=pltpu.CompilerParams(vmem_limit_bytes=48 * 2**20),
        cost_estimate=NOTHING,
        name="feed",
    )(order, after, mixed, dy, scales, shifts, w_cross, b_down, w_up, b_up, w_down)
    return (*out[:4], (out[4], out[5]), (out[6], out[7]))


def backward_heads(q, k, v, do, p_ref):
    kt = k.T
    queries = []
    keys = values = 0.0
    picked = [do * lane_pick(e, 1.0) for e in range(2)]
    grads = [dot_nt(v, picked[e]) for e in range(2)]
    for e in range(2):
        probs = p_ref[e]
        wide = probs.astype(jnp.float32)
        part = wide * grads[e]
        total = jnp.sum(part, axis=0, keepdims=True)
        ds = (part - wide * total).astype(jnp.bfloat16)
        values += dot_nn(probs, picked[e])
        keys += dot_nn(ds, q * lane_pick(e, HEAD**-0.5))
        queries.append(dot_nn(kt[e * HEAD : (e + 1) * HEAD], ds) * HEAD**-0.5)
    queries = jnp.concatenate(queries, 0).T
    return [g.astype(jnp.bfloat16) for g in (queries, keys, values)]


def self_back_kernel(q_ref, k_ref, v_ref, near_ref, far_ref, out_ref, p_ref, d_ref):
    low = jnp.concatenate([near_ref[...], far_ref[...]])
    do = dot_nt(low, out_ref[0]).astype(jnp.bfloat16)
    grads = backward_heads(q_ref[...], k_ref[...], v_ref[...], do, p_ref)
    for i in range(3):
        d_ref[i] = grads[i]


def self_back(packed, near, far, w_out, probs):
    tokens, width = packed.shape[0], near.shape[1]
    spec = lambda off: pl.BlockSpec((tokens, 128), lambda j: (0, off + j))
    rows = pl.BlockSpec(near.shape, lambda j: (0, 0))
    return pl.pallas_call(
        self_back_kernel,
        grid=(HEADS // 2,),
        in_specs=[spec(0), spec(6), spec(12), rows, rows]
        + [pl.BlockSpec((1, 128, width), lambda j: (0, j, 0))]
        + [pl.BlockSpec((2, tokens, tokens), lambda j: (j, 0, 0))],
        out_specs=pl.BlockSpec((3, tokens, 128), lambda j: (0, 0, j)),
        out_shape=jax.ShapeDtypeStruct((3, tokens, width), jnp.bfloat16),
        compiler_params=pltpu.CompilerParams(vmem_limit_bytes=24 * 2**20),
        cost_estimate=NOTHING,
        name="selfb",
    )(packed, packed, packed, near, far, w_out, pltpu.with_memory_space_constraint(probs, pltpu.HBM))


def second_kernel(back_ref, returned_ref, after_ref, grad_ref, scales_ref, low_ref, sums_ref):
    unit, inverse = layer_parts(after_ref[...])
    grad = back_ref[...] + returned_ref[...].astype(jnp.float32)
    sums_ref[...] = column_sums(grad * unit, grad)
    back = layer_back(grad, unit, inverse, scales_ref[1:2, :])
    low_ref[...] = (grad_ref[...] + back).astype(jnp.bfloat16)


def second_back(which, back, returned, after, grad, scales):
    half, width = returned.shape
    rows = pl.BlockSpec((half, width), lambda j: (which, 0))
    first = pl.BlockSpec((half, width), lambda j: (0, 0))
    return pl.pallas_call(
        second_kernel,
        grid=(1,),
        in_specs=[rows, first, rows, rows, pl.BlockSpec((3, width), lambda j: (0, 0))],
        out_specs=[first, pl.BlockSpec((8, width), lambda j: (0, 0))],
        out_shape=[
            jax.ShapeDtypeStruct((half, width), jnp.bfloat16),
            jax.ShapeDtypeStruct((8, width), jnp.float32),
        ],
        compiler_params=pltpu.CompilerParams(vmem_limit_bytes=24 * 2**20),
        cost_estimate=NOTHING,
        name="second",
    )(back, returned, after, grad, scales)


def tail_kernel(
    order, d_ref, w_ref, first_ref, top_ref, bottom_ref, moved_ref, near_ref, far_ref, scales_ref, swapped_ref,
    *refs,
):
    step = pl.program_id(0)
    stay_ref, gone_ref, sums_ref = refs[8:11]
    across, sorted_rows, total = refs[11:]
    half = sorted_rows.shape[0] // 2

    @pl.when(step == 0)
    def _():
        sort_rows(order, first_ref[...], across, sorted_rows)

    for i in range(3):

        @pl.when(step == i)
        def _():
            part = dot_nt(d_ref[0], w_ref[0])
            grad = dot_nn(sorted_rows[...], d_ref[0]).astype(jnp.bfloat16)
            refs[2 * i][...] = grad[:half].reshape(refs[0].shape)
            refs[2 * i + 1][...] = grad[half:].reshape(refs[0].shape)
            if i == 0:
                total[...] = part
            else:
                total[...] += part

    @pl.when(step == 3)
    def _():
        mixed = jnp.concatenate([top_ref[...], bottom_ref[...]])
        sort_rows(order, mixed, across, sorted_rows)
        low = jnp.concatenate([swapped_ref[...], near_ref[...]])
        grad = dot_nn(sorted_rows[...], low).astype(jnp.bfloat16)
        refs[6][...] = grad[:half].reshape(refs[0].shape)
        refs[7][...] = grad[half:].reshape(refs[0].shape)
        rows = stay_ref.shape[0]
        unit, inverse = layer_parts(moved_ref[...].astype(jnp.float32))
        grad = total[...]
        sums_ref[...] = column_sums(grad * unit, grad)
        back = layer_back(grad, unit, inverse, scales_ref[0:1, :])
        stay_ref[...] = (near_ref[...].astype(jnp.float32) + back[:rows]).astype(jnp.bfloat16)
        gone_ref[...] = (far_ref[...].astype(jnp.float32) + back[rows:]).astype(jnp.bfloat16)


def tail_grads(order, grads, w_qkv, first, top, bottom, moved, near, far, scales, swapped):
    tokens, width = moved.shape
    half = tokens // 2
    whole = lambda *shape: pl.BlockSpec(shape, lambda j, order: (0,) * len(shape))
    rows = jax.ShapeDtypeStruct((half, width), jnp.bfloat16)
    piece = (8, width // 16, width)
    last = lambda j: jnp.minimum(j, 2)
    outs = pl.pallas_call(
        tail_kernel,
        grid_spec=pltpu.PrefetchScalarGridSpec(
            num_scalar_prefetch=1,
            grid=(4,),
            in_specs=[
                pl.BlockSpec((1, tokens, width), lambda j, order: (last(j), 0, 0)),
                pl.BlockSpec((1, width, width), lambda j, order: (0, 0, last(j))),
                whole(tokens, width),
                whole(half, width),
                whole(half, width),
                whole(tokens, width),
                whole(half, width),
                whole(half, width),
                whole(3, width),
                whole(half, width),
            ],
            out_specs=[whole(*piece)] * 8 + [whole(half, width)] * 2 + [whole(8, width)],
            scratch_shapes=[pltpu.VMEM((width, tokens), jnp.bfloat16)] * 2
            + [pltpu.VMEM((tokens, width), jnp.float32)],
        ),
        out_shape=[jax.ShapeDtypeStruct(piece, jnp.bfloat16)] * 8
        + [rows, rows, jax.ShapeDtypeStruct((8, width), jnp.float32)],
        compiler_params=pltpu.CompilerParams(vmem_limit_bytes=40 * 2**20),
        cost_estimate=NOTHING,
        name="tail",
    )(order, grads, w_qkv, first, top, bottom, moved, near, far, scales, swapped)
    return [(outs[i], outs[i + 1]) for i in range(0, 8, 2)], *outs[8:]


def group_kernel(plan, halves, pieces, order, *refs):
    refs = list(refs)
    groups = [[refs.pop(0) for _ in range(n)] for n in halves]
    joined = lambda group: jnp.concatenate([r[...] for r in group]) if len(group) > 1 else group[0][...]
    outs, (across, sorted_rows) = refs[:-2], refs[-2:]
    half = sorted_rows.shape[0] // 2
    before = None
    for i, (x, dy, lead, target) in enumerate(plan):
        turn = x != before
        before = x

        @pl.when(pl.program_id(0) == i)
        def _():
            if turn:
                sort_rows(order, joined(groups[x]), across, sorted_rows)
            right = joined(groups[dy]) if lead is None else groups[dy][0][0]
            grad = dot_nn(sorted_rows[...], right).astype(jnp.bfloat16)
            send_ref, keep_ref = outs[2 * target], outs[2 * target + 1]
            send_ref[...] = grad[:half].reshape(send_ref.shape)
            keep_ref[...] = grad[half:].reshape(keep_ref.shape)


def grad_group(order, operands, plan, name):
    width = operands[0][0].shape[-1]
    rows = width // 16
    tokens = sum(a.shape[-2] for a in operands[0])
    in_specs = []
    for n, group in enumerate(operands):
        for a in group:
            if a.ndim == 2:
                in_specs.append(pl.BlockSpec(a.shape, lambda j, order: (0, 0)))
            else:
                first = min(i for i, p in enumerate(plan) if p[1] == n)
                in_specs.append(
                    pl.BlockSpec(
                        (1, *a.shape[1:]),
                        lambda j, order, first=first, last=a.shape[0] - 1: (
                            jnp.clip(j - first, 0, last),
                            0,
                            0,
                        ),
                    )
                )
    out_specs, out_shape = [], []
    for target in range(1 + max(p[3] for p in plan)):
        steps = [i for i, p in enumerate(plan) if p[3] == target]
        spec = pl.BlockSpec(
            (8, rows, width),
            lambda j, order, first=steps[0], last=len(steps) - 1: (
                0,
                jnp.clip(j - first, 0, last),
                0,
            ),
        )
        out_specs += [spec, spec]
        out_shape += [jax.ShapeDtypeStruct((8, rows * len(steps), width), jnp.bfloat16)] * 2
    outs = pl.pallas_call(
        functools.partial(group_kernel, plan, [len(g) for g in operands], len(out_specs)),
        grid_spec=pltpu.PrefetchScalarGridSpec(
            num_scalar_prefetch=1,
            grid=(len(plan),),
            in_specs=in_specs,
            out_specs=out_specs,
            scratch_shapes=[pltpu.VMEM((width, tokens), jnp.bfloat16)] * 2,
        ),
        out_shape=out_shape,
        compiler_params=pltpu.CompilerParams(vmem_limit_bytes=32 * 2**20),
        cost_estimate=NOTHING,
        name=name,
    )(order, *[a for group in operands for a in group])
    return [(outs[i], outs[i + 1]) for i in range(0, len(outs), 2)]


def add_kernel(count, *refs):
    at = 0
    for n in range(count):
        keep, arrived = refs[2 * n], refs[2 * n + 1]
        rows = keep.shape[-2]
        for i, out in enumerate(refs[2 * count :]):
            out[0, at : at + rows, :] = keep[i, 0] + arrived[i, 0]
        at += rows


def add_halves(keeps, arrivals, name="add"):
    pairs = keeps[0].shape[0] // 2
    width = keeps[0].shape[2]
    rows = sum(k.shape[1] for k in keeps)
    operands = []
    for keep, arrived in zip(keeps, arrivals):
        operands += [a.reshape(2, pairs, *a.shape[1:]) for a in (keep, arrived)]
    out = pl.BlockSpec((1, rows, width), lambda j: (j, 0, 0))
    return pl.pallas_call(
        functools.partial(add_kernel, len(keeps)),
        grid=(pairs,),
        in_specs=[
            pl.BlockSpec((2, 1, *a.shape[2:]), lambda j: (0, j, 0, 0)) for a in operands
        ],
        out_specs=[out, out],
        out_shape=[jax.ShapeDtypeStruct((pairs, rows, width), jnp.bfloat16)] * 2,
        compiler_params=pltpu.CompilerParams(vmem_limit_bytes=16 * 2**20),
        cost_estimate=NOTHING,
        name=name,
    )(*operands)


def last_kernel(keep_ref, arrived_ref, *outs):
    total = keep_ref[0].astype(jnp.float32) + arrived_ref[0].astype(jnp.float32)
    width = total.shape[1]
    at = 0
    for out in outs:
        rows, columns = out.shape
        for n in range(columns // width):
            out[:, n * width : (n + 1) * width] = total[at : at + rows]
            at += rows


def last_sum(keep, arrived, shapes):
    return pl.pallas_call(
        last_kernel,
        out_shape=[jax.ShapeDtypeStruct(s, jnp.float32) for s in shapes],
        compiler_params=pltpu.CompilerParams(vmem_limit_bytes=16 * 2**20),
        cost_estimate=NOTHING,
        name="last",
    )(keep, arrived)


def swap(x, bit):
    return lax.ppermute(x, "page", [(i, i ^ bit) for i in range(16)])


pin = lax.optimization_barrier


def on_device(
    block_input,
    cotangent,
    norm_gain,
    norm_bias,
    w_qkv,
    w_out,
    w_query,
    w_keyval,
    w_cross,
    w_up,
    b_up,
    w_down,
    b_down,
    row_page,
    lengths,
):
    x = block_input[0]
    dy = cotangent[0]
    tokens, width = x.shape
    half = tokens // 2
    pages = lax.axis_size("page")
    device = lax.axis_index("page")
    stream = lax.axis_index("stream")
    scales = norm_gain[0].T
    shifts = norm_bias[0].T
    share = width // pages
    padded = jnp.concatenate([row_page, row_page[:SHIFT]])
    info = jnp.concatenate(
        [
            stream.astype(jnp.int32)[None],
            lengths,
            lax.dynamic_slice_in_dim(padded, device * WIN + SHIFT, WIN),
        ]
    )
    stay = [(pages + i, pages + i) for i in range(pages)]
    both = ("stream", "page")
    forth = [((i + 1) % pages, i) for i in range(pages)] + stay
    back = [(i, (i + 1) % pages) for i in range(pages)] + stay

    def partner_of(rows):
        return lax.ppermute(rows, "stream", [(0, 1), (1, 0)])

    moved = jnp.concatenate([x[half:], lax.ppermute(x[:half], both, forth)])
    first, unit_one, inverse_one = layer_norm(moved.astype(jnp.float32), scales[0], shifts[0])
    packed = matmul(first, w_qkv[0]).astype(jnp.bfloat16)
    moved_mixed, self_probs = attn_fwd(
        info, packed, packed, packed, 0, 6, 12, fill_self_bias, "selff"
    )
    gone, near = moved_mixed[half:], moved_mixed[:half]
    after_gone = moved[half:].astype(jnp.float32) + matmul(gone, w_out[0])
    second_gone = layer_norm(after_gone, scales[1], shifts[1])[0]
    partner_top = lax.ppermute(
        second_gone,
        both,
        [(i, pages + (i + 1) % pages) for i in range(pages)]
        + [(pages + i, i) for i in range(pages)],
    )
    back_mixed = lax.ppermute(gone, both, back)
    after_low = moved[:half].astype(jnp.float32) + matmul(near, w_out[0])
    second_low = layer_norm(after_low, scales[1], shifts[1])[0]
    partner_low = partner_of(second_low)
    back_mixed, second_low, partner_top = pin((back_mixed, second_low, partner_top))
    after_top = x[:half].astype(jnp.float32) + matmul(back_mixed, w_out[0])
    second_top = layer_norm(after_top, scales[1], shifts[1])[0]
    after_self = jnp.concatenate([after_top, after_low])
    second = jnp.concatenate([second_top, second_low])
    cross_q = matmul(second, w_query[0]).astype(jnp.bfloat16)
    cross_q, after_self, partner_top, partner_low = pin(
        (cross_q, after_self, partner_top, partner_low)
    )
    partner = jnp.concatenate([partner_top, partner_low])
    cross_pair = matmul(partner, w_keyval[0]).astype(jnp.bfloat16)
    cross_mixed, cross_probs = attn_fwd(
        info, cross_q, cross_pair, cross_pair, 0, 0, 6, fill_cross_bias, "crossf"
    )
    if pages == 16:
        ordinal = jnp.arange(16, dtype=jnp.int32)
        turned = 15 - ordinal
        turned = (turned & 1) << 3 | (turned & 2) << 1 | (turned & 4) >> 1 | (turned & 8) >> 3
        order = device.astype(jnp.int32) ^ turned
        output, grad_third, after_cross, up_bias, down, up = feed_forward(
            order, after_self, cross_mixed, dy, scales, shifts, w_cross, w_up, b_up, w_down, b_down
        )
        grad_cross_in, cross_low, grad_cmix, sums_three = third_back(
            grad_third, after_cross, dy, scales, w_cross
        )

        def onward(keeps, sends, bit):
            return add_halves(keeps, [swap(s, bit) for s in sends])

        grad_cmix, down_keep, up_keep = pin((grad_cmix, down[1], up[1]))
        down = onward([down_keep], [down[0]], 1)
        up = onward([up_keep], [up[0]], 1)
        grad_cmix, down, up = pin((grad_cmix, down, up))
        cross_grads = attn_bwd(
            cross_q, cross_pair, cross_pair, 0, 0, 6, grad_cmix, cross_probs, "crossb"
        )

        def given(rows):
            keys = dot_nt(cross_grads[1, rows], w_keyval[0][:, :width])
            return (keys + dot_nt(cross_grads[2, rows], w_keyval[0][:, width:])).astype(jnp.bfloat16)

        returned_top = partner_of(given(slice(0, half)))
        returned_low = partner_of(given(slice(half, tokens)))
        query_back = dot_nt(cross_grads[0], w_query[0])
        (cross_part,) = grad_group(
            order,
            (
                (cross_mixed,),
                (second_top, second_low),
                (partner_top, partner_low),
                (cross_low,),
                (cross_grads,),
            ),
            ((0, 3, None, 0), (1, 4, 0, 0), (2, 4, 1, 0), (2, 4, 2, 0)),
            "gcross",
        )
        down = onward([down[1]], [down[0]], 4)
        up = onward([up[1]], [up[0]], 2)
        returned_top, cross_part, down, up = pin((returned_top, cross_part, down, up))
        low_top, sums_top = second_back(
            0, query_back, returned_top, after_self, grad_cross_in, scales
        )
        arrived_low = lax.ppermute(low_top, both, forth)
        low_top, cross_keep = pin((low_top, cross_part[1]))
        cross_part = onward([cross_keep], [cross_part[0]], 1)
        returned_low, arrived_low, cross_part, down, up = pin(
            (returned_low, arrived_low, cross_part, down, up)
        )
        low_low, sums_low = second_back(
            1, query_back, returned_low, after_self, grad_cross_in, scales
        )
        self_grads = self_back(packed, low_low, arrived_low, w_out, self_probs)
        self_grads, up_keep = pin((self_grads, up[1]))
        up = onward([up_keep], [up[0]], 4)
        self_grads, up = pin((self_grads, up))
        parts, input_stay, input_gone, sums_one = tail_grads(
            order, self_grads, w_qkv, first, back_mixed, near, moved, low_low, arrived_low, scales,
            low_top,
        )
        parts = [parts[1], parts[2], parts[0], parts[3]]
        parts, cross_keep, down_keep, up_keep = pin((parts, cross_part[1], down[1], up[1]))
        (grad_up,) = last_sum(up_keep, swap(up[0], 8), [(48, 4 * width)])
        down = onward([down_keep], [down[0]], 8)
        cross_part = onward([cross_keep], [cross_part[0]], 2)
        sends, keeps = [p[0] for p in parts], [p[1] for p in parts]
        cross_part, keeps, down, grad_up = pin((cross_part, keeps, down, grad_up))
        pair_part = onward(keeps[:2], sends[:2], 1)
        rest_part = onward(keeps[2:], sends[2:], 1)
        pair_part, rest_part, input_gone, sums_one = pin(
            (pair_part, rest_part, input_gone, sums_one)
        )
        input_top = lax.ppermute(input_gone, both, back)
        sums = jnp.concatenate(
            [sums_one[:2], sums_top[:2] + sums_low[:2], sums_three[:3], up_bias.reshape(4, width)]
        )
        sums = sums + swap(sums, 1)
        pair_keep, sums = pin((pair_part[1], sums))
        pair_part = onward([pair_keep], [pair_part[0]], 2)
        cross_keep, pair_part = pin((cross_part[1], pair_part))
        cross_part = onward([cross_keep], [cross_part[0]], 4)
        cross_part, pair_keep = pin((cross_part, pair_part[1]))
        pair_part = onward([pair_keep], [pair_part[0]], 4)
        pair_part, cross_keep = pin((pair_part, cross_part[1]))
        grad_cross, grad_query, grad_keyval = last_sum(
            cross_keep,
            swap(cross_part[0], 8),
            [(48, width), (48, width), (48, 2 * width)],
        )
        rest_keep, grad_cross, grad_query, grad_keyval = pin(
            (rest_part[1], grad_cross, grad_query, grad_keyval)
        )
        rest_part = onward([rest_keep], [rest_part[0]], 2)
        sums = sums + swap(sums, 2)
        rest_keep, pair_keep, sums = pin((rest_part[1], pair_part[1], sums))
        rest_part = onward([rest_keep], [rest_part[0]], 4)
        (grad_pair,) = last_sum(pair_keep, swap(pair_part[0], 8), [(48, 2 * width)])
        (grad_down,) = last_sum(down[1], swap(down[0], 2), [(192, width)])
        sums = sums + swap(sums, 4)
        rest_part, sums, grad_pair, grad_down = pin((rest_part, sums, grad_pair, grad_down))
        grad_first, grad_out = last_sum(
            rest_part[1], swap(rest_part[0], 8), [(48, width), (48, width)]
        )
        sums = sums + swap(sums, 8)
        grad_qkv = jnp.concatenate([grad_first, grad_pair], 1)
        mine = lax.dynamic_slice_in_dim(sums[:7], device * share, share, 1)
        gains, biases = mine[0:6:2], mine[1:6:2]
        down_bias = mine[6]
        up_bias = lax.dynamic_slice_in_dim(sums[7:].reshape(-1), device * 192, 192)
        input_grad = jnp.concatenate([input_top, input_stay])
    else:
        _, unit_two, inverse_two = layer_norm(after_self, scales[1], shifts[1])
        after_cross = after_self + matmul(cross_mixed, w_cross[0])
        third, unit_three, inverse_three = layer_norm(after_cross, scales[2], shifts[2])
        value, slope = gelu_pair(matmul(third, w_up[0]) + b_up[0])
        hidden = value.astype(jnp.bfloat16)
        output = (after_cross + matmul(hidden, w_down[0]) + b_down[0]).astype(jnp.bfloat16)
        upstream = dy.astype(jnp.float32)
        pre_low = (dot_nt(dy, w_down[0]) * slope).astype(jnp.bfloat16)
        back_three, gain_three, shift_three = norm_back(
            dot_nt(pre_low, w_up[0]), unit_three, inverse_three, scales[2]
        )
        grad_cross_in = upstream + back_three
        cross_low = grad_cross_in.astype(jnp.bfloat16)
        grad_cmix = dot_nt(cross_low, w_cross[0]).astype(jnp.bfloat16)
        cross_grads = attn_bwd(
            cross_q, cross_pair, cross_pair, 0, 0, 6, grad_cmix, cross_probs, "crossb"
        )
        pair = jnp.concatenate([cross_grads[1], cross_grads[2]], 1)
        returned = partner_of(dot_nt(pair, w_keyval[0]).astype(jnp.bfloat16))
        back_two, gain_two, shift_two = norm_back(
            dot_nt(cross_grads[0], w_query[0]) + returned.astype(jnp.float32),
            unit_two,
            inverse_two,
            scales[1],
        )
        self_low = (grad_cross_in + back_two).astype(jnp.bfloat16)
        moved_low = jnp.concatenate([self_low[half:], lax.ppermute(self_low[:half], both, forth)])
        grad_smix = dot_nt(moved_low, w_out[0]).astype(jnp.bfloat16)
        self_grads = attn_bwd(packed, packed, packed, 0, 6, 12, grad_smix, self_probs, "selfb")
        packed_grad = jnp.concatenate([self_grads[0], self_grads[1], self_grads[2]], 1)
        back_one, gain_one, shift_one = norm_back(
            dot_nt(packed_grad, w_qkv[0]), unit_one, inverse_one, scales[0]
        )
        moved_grad = (moved_low.astype(jnp.float32) + back_one).astype(jnp.bfloat16)
        input_grad = jnp.concatenate([lax.ppermute(moved_grad[half:], both, back), moved_grad[:half]])

        def summed(grad):
            return lax.psum_scatter(grad, "page", scatter_dimension=0, tiled=True)

        def scattered(left, right):
            return summed(
                lax.dot_general(
                    left, right, (((0,), (0,)), ((), ())), preferred_element_type=jnp.float32
                )
            )

        grad_down = scattered(hidden, dy)
        grad_up = scattered(third, pre_low)
        grad_cross = scattered(cross_mixed, cross_low)
        grad_query = scattered(second, cross_grads[0])
        grad_keyval = scattered(partner, pair)
        grad_out = scattered(jnp.concatenate([back_mixed, near]), self_low)
        grad_qkv = scattered(first, packed_grad)
        gains = summed(jnp.stack([gain_one, gain_two, gain_three], 1)).T
        biases = summed(jnp.stack([shift_one, shift_two, shift_three], 1)).T
        down_bias = summed(jnp.sum(upstream, axis=0))
        up_bias = summed(jnp.sum(pre_low.astype(jnp.float32), axis=0))
    return (
        output[None],
        input_grad[None],
        gains.T[None],
        biases.T[None],
        grad_qkv[None],
        grad_out[None],
        grad_query[None],
        grad_keyval[None],
        grad_cross[None],
        grad_up[None],
        up_bias[None],
        grad_down[None],
        down_bias[None],
    )


def solution(mesh):
    tokens = P("stream", "page", None)
    whole = P("stream", None, None)
    placed = (tokens, tokens) + (whole,) * 8 + (P("stream", None), whole, P("stream", None))
    return jax.shard_map(
        on_device,
        mesh=mesh,
        in_specs=placed + (P(), P("page")),
        out_specs=(tokens,) * 10 + (P("stream", "page"), tokens, P("stream", "page")),
        check_vma=False,
    )
```

```python
import functools

import jax
import jax.numpy as jnp
from jax import lax
from jax.experimental import pallas as pl
from jax.experimental.pallas import tpu as pltpu
from jax.sharding import PartitionSpec as P

HEADS = 12
HEAD = 64
WIN = 12
SHIFT = 6
NORM_EPS = 1e-05
MASKED = -1e30


def dot_nt(a,b):
    return lax.dot_general(a,b,(((1,),(1,)),((),())),preferred_element_type=jnp.float32)
def dot_nn(a,b):
    return lax.dot_general(a,b,(((1,),(0,)),((),())),preferred_element_type=jnp.float32)

def fill_self_bias(info, bias, first=0):
    tokens, count = bias.shape
    half=tokens//2
    cols=tokens//12
    def codes(shape,dim,start):
        t=lax.broadcasted_iota(jnp.int32,shape,dim)+start
        row=jnp.zeros(shape,jnp.int32)
        page=jnp.full(shape,info[2],jnp.int32)
        for r in range(1,12):
            inside=t>=r*cols
            row=jnp.where(inside,r,row)
            page=jnp.where(inside,info[2+r],page)
        c=t-row*cols
        win=jnp.zeros(shape,jnp.int32)
        for w in range(1,cols//12):
            win=jnp.where((c>=6+12*(w-1))&(c<6+12*w),w,win)
        win=jnp.where(c>=cols-6,cols//12+1,win)
        slot=jnp.where(t<half,t+half,t-half)
        return page*16+win,slot
    ck,sk=codes((tokens,1),0,0)
    cq,sq=codes((1,count),1,first)
    length=info[1]
    @pl.when(info[0]==1)
    def _():
        ok=(sk<=sq)&(sk<length)
        bias[...]=jnp.where(ok,0.0,MASKED)
    @pl.when(info[0]==0)
    def _():
        bias[...]=jnp.where(ck==cq,0.0,MASKED)

def fill_cross_bias(info,bias,first=0):
    tokens=bias.shape[0]
    t=lax.broadcasted_iota(jnp.int32,bias.shape,0)
    bias[...]=jnp.where((t<info[1])|(info[0]==1),0.0,MASKED)

def lane_pick(e,scale):
    lane=lax.broadcasted_iota(jnp.int32,(1,2*HEAD),1)
    return jnp.where((lane>=HEAD)==bool(e),scale,0.0).astype(jnp.bfloat16)

def fwd_kernel(fill, info, q_ref, k_ref, v_ref, o_ref, p_ref, bias):
    @pl.when(pl.program_id(0) == 0)
    def _():
        fill(info, bias)

    q, k = q_ref[...], k_ref[...]
    vt = v_ref[...].T
    scores = [dot_nt(k, q * lane_pick(e, HEAD**-0.5)) + bias[...] for e in range(2)]
    outs = []
    for e in range(2):
        weights = jnp.exp(scores[e] - jnp.max(scores[e], axis=0, keepdims=True))
        inverse = 1.0 / jnp.sum(weights, axis=0, keepdims=True)
        probs = (weights * inverse).astype(jnp.bfloat16)
        p_ref[e] = probs
        outs.append(dot_nn(vt[e * HEAD : (e + 1) * HEAD], probs))
    o_ref[...] = jnp.concatenate(outs, 0).T.astype(jnp.bfloat16)


NOTHING = pl.CostEstimate(flops=1000, bytes_accessed=1000, transcendentals=0)


def attn_fwd(info, q, k, v, qo, ko, vo, fill, name):
    tokens = q.shape[0]
    spec = lambda off: pl.BlockSpec((tokens, 128), lambda j, info: (0, off + j))
    return pl.pallas_call(
        functools.partial(fwd_kernel, fill),
        grid_spec=pltpu.PrefetchScalarGridSpec(
            num_scalar_prefetch=1,
            grid=(HEADS // 2,),
            in_specs=[spec(qo), spec(ko), spec(vo)],
            out_specs=[spec(0), pl.BlockSpec((2, tokens, tokens), lambda j, info: (j, 0, 0))],
            scratch_shapes=[pltpu.VMEM((tokens, tokens), jnp.float32)],
        ),
        out_shape=[
            jax.ShapeDtypeStruct((tokens, HEADS * HEAD), jnp.bfloat16),
            pltpu.HBM((HEADS, tokens, tokens), jnp.bfloat16),
        ],
        compiler_params=pltpu.CompilerParams(vmem_limit_bytes=24 * 2**20),
        cost_estimate=NOTHING,
        name=name,
    )(info, q, k, v)


def bwd_kernel(q_ref, k_ref, v_ref, do_ref, p_ref, d_ref):
    grads = backward_heads(q_ref[...], k_ref[...], v_ref[...], do_ref[...], p_ref)
    for i in range(3):
        d_ref[i] = grads[i]


def attn_bwd(q, k, v, qo, ko, vo, do, probs, name):
    tokens = q.shape[0]
    spec = lambda off: pl.BlockSpec((tokens, 128), lambda j: (0, off + j))
    return pl.pallas_call(
        bwd_kernel,
        grid=(HEADS // 2,),
        in_specs=[spec(qo), spec(ko), spec(vo), spec(0)]
        + [pl.BlockSpec((2, tokens, tokens), lambda j: (j, 0, 0))],
        out_specs=pl.BlockSpec((3, tokens, 128), lambda j: (0, 0, j)),
        out_shape=jax.ShapeDtypeStruct((3, tokens, HEADS * HEAD), jnp.bfloat16),
        compiler_params=pltpu.CompilerParams(vmem_limit_bytes=24 * 2**20),
        cost_estimate=NOTHING,
        name=name,
    )(q, k, v, do, pltpu.with_memory_space_constraint(probs, pltpu.HBM))


def layer_norm(inputs, scales, shifts):
    average = jnp.mean(inputs, axis=1, keepdims=True)
    centred = inputs - average
    spread = jnp.mean(centred * centred, axis=1, keepdims=True)
    inverse = lax.rsqrt(spread + NORM_EPS)
    unit = centred * inverse
    return (unit * scales + shifts).astype(jnp.bfloat16), unit, inverse


def norm_back(upstream, unit, inverse, scales):
    scaled = upstream * scales
    inner = (
        scaled
        - jnp.mean(scaled, axis=1, keepdims=True)
        - unit * jnp.mean(scaled * unit, axis=1, keepdims=True)
    )
    return (inverse * inner, jnp.sum(upstream * unit, axis=0), jnp.sum(upstream, axis=0))


def matmul(left, right):
    return jnp.dot(left, right, preferred_element_type=jnp.float32)


def gelu_pair(pre):
    root = 0.7978845608028654
    square = pre * pre
    gate = 0.5 + 0.5 * jnp.tanh(pre * (root + root * 0.044715 * square))
    value = pre * gate
    return value, gate + value * (1.0 - gate) * (2 * root + 6 * root * 0.044715 * square)


def layer_parts(v):
    average = jnp.mean(v, axis=1, keepdims=True)
    centred = v - average
    inverse = lax.rsqrt(jnp.mean(centred * centred, axis=1, keepdims=True) + NORM_EPS)
    return centred * inverse, inverse


def layer_back(grad, unit, inverse, scale):
    scaled = grad * scale
    return inverse * (
        scaled
        - jnp.mean(scaled, axis=1, keepdims=True)
        - unit * jnp.mean(scaled * unit, axis=1, keepdims=True)
    )


def column_sums(*values):
    rows = [jnp.sum(v, axis=0, keepdims=True) for v in values]
    rows.append(jnp.zeros((8 - len(rows), rows[0].shape[1]), jnp.float32))
    return jnp.concatenate(rows)


def sort_rows(order, x, across, sorted_rows):
    rows = sorted_rows.shape[0] // 16
    across[...] = x.T
    for n in range(16):
        start = pl.multiple_of(order[n] * rows, 16)
        sorted_rows[n * rows : (n + 1) * rows, :] = across[pl.ds(start, rows), :]


def feed_kernel(
    order, after_ref, mixed_ref, dy_ref, scales_ref, shifts_ref, cross_ref, down_bias_ref,
    up_ref, up_bias_ref, down_ref,
    out_ref, grad_ref, kept_ref, bias_ref,
    down_send, down_keep, up_send, up_keep,
    third_rows, across, sorted_rows, after, total, grad_total,
):
    step = pl.program_id(0)
    rows = dy_ref.shape[1] // 16
    half = 8 * rows

    @pl.when(step == 0)
    def _():
        after[...] = after_ref[...] + dot_nn(mixed_ref[...], cross_ref[0])
        unit = layer_parts(after[...])[0]
        third_rows[...] = (unit * scales_ref[2:3, :] + shifts_ref[2:3, :]).astype(jnp.bfloat16)
        sort_rows(order, third_rows[...], across, sorted_rows)
        total[...] = after[...] + down_bias_ref[...]
        grad_total[...] = jnp.zeros_like(grad_total)

    dy, third = dy_ref[...], third_rows[...]
    tile = up_ref.shape[2] // 2
    deep = tile // 2
    parts = [slice(0, tile), slice(tile, 2 * tile)]
    pre = [dot_nn(third, up_ref[0, :, p]) + up_bias_ref[:, p] for p in parts]
    grad_hidden = [dot_nt(dy, down_ref[0, p, :]) for p in parts]
    out = grad_third = 0.0
    grads = []
    for i, p in enumerate(parts):
        value, slope = gelu_pair(pre[i])
        hidden = value.astype(jnp.bfloat16)
        low = (grad_hidden[i] * slope).astype(jnp.bfloat16)
        bias_ref[0, :, p] = jnp.sum(low.astype(jnp.float32), axis=0, keepdims=True)
        grad = dot_nn(sorted_rows[...], low).astype(jnp.bfloat16)
        up_send[:, :, p] = grad[:half].reshape(8, rows, tile)
        up_keep[:, :, p] = grad[half:].reshape(8, rows, tile)
        grads.append(dot_nn(hidden.T, dy).astype(jnp.bfloat16))
        out += dot_nn(hidden, down_ref[0, p, :])
        grad_third += dot_nt(low, up_ref[0, :, p])
    total[...] += out
    grad_total[...] += grad_third
    for odd in range(2):
        for far in range(2):

            @pl.when((order[15] % 2 == odd) & (order[15] // 2 % 2 == far))
            def _():
                for n in range(2):
                    both = grads[n ^ far ^ 1]
                    down_send[n] = both[deep * (1 - odd) : deep * (2 - odd)]
                    down_keep[n] = both[deep * odd : deep * (odd + 1)]

    @pl.when(step == pl.num_programs(0) - 1)
    def _():
        out_ref[...] = total[...].astype(jnp.bfloat16)
        grad_ref[...] = grad_total[...]
        kept_ref[...] = after[...]


def third_kernel(third_ref, after_ref, dy_ref, scales_ref, cross_ref, grad_ref, low_ref, mix_ref, sums_ref):
    upstream = dy_ref[...].astype(jnp.float32)
    unit, inverse = layer_parts(after_ref[...])
    grad = third_ref[...]
    sums_ref[...] = column_sums(grad * unit, grad, upstream)
    grad_ref[...] = upstream + layer_back(grad, unit, inverse, scales_ref[2:3, :])
    low_ref[...] = grad_ref[...].astype(jnp.bfloat16)
    mix_ref[...] = dot_nt(low_ref[...], cross_ref[0]).astype(jnp.bfloat16)


def third_back(grad, after, dy, scales, w_cross):
    full = jax.ShapeDtypeStruct(after.shape, jnp.float32)
    low = jax.ShapeDtypeStruct(after.shape, jnp.bfloat16)
    return pl.pallas_call(
        third_kernel,
        out_shape=[full, low, low, jax.ShapeDtypeStruct((8, after.shape[1]), jnp.float32)],
        compiler_params=pltpu.CompilerParams(vmem_limit_bytes=32 * 2**20),
        cost_estimate=NOTHING,
        name="third",
    )(grad, after, dy, scales, w_cross)


def feed_forward(order, after, mixed, dy, scales, shifts, w_cross, w_up, b_up, w_down, b_down):
    tokens, width = dy.shape
    deep = w_up.shape[2]
    tile = deep // 4
    rows = width // 16
    whole = lambda *shape: pl.BlockSpec(shape, lambda j, order: (0,) * len(shape))
    where = lambda j, order: order[8 + j] // 4
    once = lambda *shape: pl.BlockSpec(
        shape, lambda j, order: (0,) * len(shape), pipeline_mode=pl.Buffered(1)
    )
    token = once(tokens, width)
    down_half = jax.ShapeDtypeStruct((8, deep // 16, width), jnp.bfloat16)
    up_half = jax.ShapeDtypeStruct((8, 4 * rows, tile), jnp.bfloat16)
    down_piece = pl.BlockSpec((2, deep // 16, width), lambda j, order: (j, 0, 0))
    up_piece = pl.BlockSpec((8, rows, tile), lambda j, order: (0, where(j, order), 0))
    low = jax.ShapeDtypeStruct((tokens, width), jnp.bfloat16)
    full = jax.ShapeDtypeStruct((tokens, width), jnp.float32)
    out = pl.pallas_call(
        feed_kernel,
        grid_spec=pltpu.PrefetchScalarGridSpec(
            num_scalar_prefetch=1,
            grid=(4,),
            in_specs=[
                token,
                token,
                token,
                whole(3, width),
                whole(3, width),
                once(1, width, width),
                whole(1, width),
                pl.BlockSpec((1, width, tile), lambda j, order: (0, 0, where(j, order))),
                pl.BlockSpec((1, tile), lambda j, order: (0, where(j, order))),
                pl.BlockSpec((1, tile, width), lambda j, order: (0, where(j, order), 0)),
            ],
            out_specs=[
                token,
                token,
                token,
                pl.BlockSpec((1, 1, tile), lambda j, order: (where(j, order), 0, 0)),
                down_piece,
                down_piece,
                up_piece,
                up_piece,
            ],
            scratch_shapes=[pltpu.VMEM((tokens, width), jnp.bfloat16)]
            + [pltpu.VMEM((width, tokens), jnp.bfloat16)] * 2
            + [pltpu.VMEM((tokens, width), jnp.float32)] * 3,
        ),
        out_shape=[
            low,
            full,
            full,
            jax.ShapeDtypeStruct((4, 1, tile), jnp.float32),
            down_half,
            down_half,
            up_half,
            up_half,
        ],
        compiler_params=pltpu.CompilerParams(vmem_limit_bytes=36 * 2**20),
        cost_estimate=NOTHING,
        name="feed",
    )(order, after, mixed, dy, scales, shifts, w_cross, b_down, w_up, b_up, w_down)
    return (*out[:4], (out[4], out[5]), (out[6], out[7]))


def backward_heads(q, k, v, do, p_ref):
    kt = k.T
    queries = []
    keys = values = 0.0
    picked = [do * lane_pick(e, 1.0) for e in range(2)]
    grads = [dot_nt(v, picked[e]) for e in range(2)]
    for e in range(2):
        probs = p_ref[e]
        wide = probs.astype(jnp.float32)
        part = wide * grads[e]
        total = jnp.sum(part, axis=0, keepdims=True)
        ds = (part - wide * total).astype(jnp.bfloat16)
        values += dot_nn(probs, picked[e])
        keys += dot_nn(ds, q * lane_pick(e, HEAD**-0.5))
        queries.append(dot_nn(kt[e * HEAD : (e + 1) * HEAD], ds) * HEAD**-0.5)
    queries = jnp.concatenate(queries, 0).T
    return [g.astype(jnp.bfloat16) for g in (queries, keys, values)]


def self_back_kernel(q_ref, k_ref, v_ref, near_ref, far_ref, out_ref, p_ref, d_ref):
    low = jnp.concatenate([near_ref[...], far_ref[...]])
    do = dot_nt(low, out_ref[0]).astype(jnp.bfloat16)
    grads = backward_heads(q_ref[...], k_ref[...], v_ref[...], do, p_ref)
    for i in range(3):
        d_ref[i] = grads[i]


def self_back(packed, near, far, w_out, probs):
    tokens, width = packed.shape[0], near.shape[1]
    spec = lambda off: pl.BlockSpec((tokens, 128), lambda j: (0, off + j))
    rows = pl.BlockSpec(near.shape, lambda j: (0, 0))
    return pl.pallas_call(
        self_back_kernel,
        grid=(HEADS // 2,),
        in_specs=[spec(0), spec(6), spec(12), rows, rows]
        + [pl.BlockSpec((1, 128, width), lambda j: (0, j, 0))]
        + [pl.BlockSpec((2, tokens, tokens), lambda j: (j, 0, 0))],
        out_specs=pl.BlockSpec((3, tokens, 128), lambda j: (0, 0, j)),
        out_shape=jax.ShapeDtypeStruct((3, tokens, width), jnp.bfloat16),
        compiler_params=pltpu.CompilerParams(vmem_limit_bytes=24 * 2**20),
        cost_estimate=NOTHING,
        name="selfb",
    )(packed, packed, packed, near, far, w_out, pltpu.with_memory_space_constraint(probs, pltpu.HBM))


def second_kernel(
    near_back_ref, far_back_ref, near_given_ref, far_given_ref, near_after_ref, far_after_ref,
    near_grad_ref, far_grad_ref, scales_ref, near_ref, far_ref, sums_ref,
):
    sums = 0.0
    for back, given, after, grad, out in (
        (near_back_ref, near_given_ref, near_after_ref, near_grad_ref, near_ref),
        (far_back_ref, far_given_ref, far_after_ref, far_grad_ref, far_ref),
    ):
        unit, inverse = layer_parts(after[...])
        upstream = back[...].astype(jnp.float32) + given[...].astype(jnp.float32)
        sums += column_sums(upstream * unit, upstream)
        below = layer_back(upstream, unit, inverse, scales_ref[1:2, :])
        out[...] = (grad[...].astype(jnp.float32) + below).astype(jnp.bfloat16)
    sums_ref[...] = sums


def second_back(back, far_back, near_given, far_given, after, far_after, grad, far_grad, scales):
    half, width = near_given.shape
    low = pl.BlockSpec((half, width), lambda j: (1, 0))
    rows = pl.BlockSpec((half, width), lambda j: (0, 0))
    out = jax.ShapeDtypeStruct((half, width), jnp.bfloat16)
    return pl.pallas_call(
        second_kernel,
        grid=(1,),
        in_specs=[low, rows, rows, rows, low, rows, low, rows]
        + [pl.BlockSpec((3, width), lambda j: (0, 0))],
        out_specs=[rows, rows, pl.BlockSpec((8, width), lambda j: (0, 0))],
        out_shape=[out, out, jax.ShapeDtypeStruct((8, width), jnp.float32)],
        compiler_params=pltpu.CompilerParams(vmem_limit_bytes=24 * 2**20),
        cost_estimate=NOTHING,
        name="second",
    )(back, far_back, near_given, far_given, after, far_after, grad, far_grad, scales)


def tail_kernel(
    order, d_ref, w_ref, first_ref, mixed_ref, moved_ref, near_ref, far_ref, scales_ref, *refs,
):
    step = pl.program_id(0)
    stay_ref, gone_ref, sums_ref = refs[8:11]
    across, sorted_rows, total = refs[11:]
    half = sorted_rows.shape[0] // 2

    @pl.when(step == 0)
    def _():
        sort_rows(order, first_ref[...], across, sorted_rows)

    for i in range(3):

        @pl.when(step == i)
        def _():
            part = dot_nt(d_ref[0], w_ref[0])
            grad = dot_nn(sorted_rows[...], d_ref[0]).astype(jnp.bfloat16)
            refs[2 * i][...] = grad[:half].reshape(refs[0].shape)
            refs[2 * i + 1][...] = grad[half:].reshape(refs[0].shape)
            if i == 0:
                total[...] = part
            else:
                total[...] += part

    @pl.when(step == 3)
    def _():
        sort_rows(order, mixed_ref[...], across, sorted_rows)
        low = jnp.concatenate([near_ref[...], far_ref[...]])
        grad = dot_nn(sorted_rows[...], low).astype(jnp.bfloat16)
        refs[6][...] = grad[:half].reshape(refs[0].shape)
        refs[7][...] = grad[half:].reshape(refs[0].shape)
        rows = stay_ref.shape[0]
        unit, inverse = layer_parts(moved_ref[...].astype(jnp.float32))
        grad = total[...]
        sums_ref[...] = column_sums(grad * unit, grad)
        back = layer_back(grad, unit, inverse, scales_ref[0:1, :])
        stay_ref[...] = (near_ref[...].astype(jnp.float32) + back[:rows]).astype(jnp.bfloat16)
        gone_ref[...] = (far_ref[...].astype(jnp.float32) + back[rows:]).astype(jnp.bfloat16)


def tail_grads(order, grads, w_qkv, first, mixed, moved, near, far, scales):
    tokens, width = moved.shape
    half = tokens // 2
    whole = lambda *shape: pl.BlockSpec(shape, lambda j, order: (0,) * len(shape))
    rows = jax.ShapeDtypeStruct((half, width), jnp.bfloat16)
    piece = (8, width // 16, width)
    last = lambda j: jnp.minimum(j, 2)
    outs = pl.pallas_call(
        tail_kernel,
        grid_spec=pltpu.PrefetchScalarGridSpec(
            num_scalar_prefetch=1,
            grid=(4,),
            in_specs=[
                pl.BlockSpec((1, tokens, width), lambda j, order: (last(j), 0, 0)),
                pl.BlockSpec((1, width, width), lambda j, order: (0, 0, last(j))),
                whole(tokens, width),
                whole(tokens, width),
                whole(tokens, width),
                whole(half, width),
                whole(half, width),
                whole(3, width),
            ],
            out_specs=[whole(*piece)] * 8 + [whole(half, width)] * 2 + [whole(8, width)],
            scratch_shapes=[pltpu.VMEM((width, tokens), jnp.bfloat16)] * 2
            + [pltpu.VMEM((tokens, width), jnp.float32)],
        ),
        out_shape=[jax.ShapeDtypeStruct(piece, jnp.bfloat16)] * 8
        + [rows, rows, jax.ShapeDtypeStruct((8, width), jnp.float32)],
        compiler_params=pltpu.CompilerParams(vmem_limit_bytes=40 * 2**20),
        cost_estimate=NOTHING,
        name="tail",
    )(order, grads, w_qkv, first, mixed, moved, near, far, scales)
    return [(outs[i], outs[i + 1]) for i in range(0, 8, 2)], *outs[8:]


def group_kernel(plan, halves, pieces, order, *refs):
    refs = list(refs)
    groups = [[refs.pop(0) for _ in range(n)] for n in halves]
    joined = lambda group: jnp.concatenate([r[...] for r in group]) if len(group) > 1 else group[0][...]
    outs, (across, sorted_rows) = refs[:-2], refs[-2:]
    half = sorted_rows.shape[0] // 2
    before = None
    for i, (x, dy, lead, target) in enumerate(plan):
        turn = x != before
        before = x

        @pl.when(pl.program_id(0) == i)
        def _():
            if turn:
                sort_rows(order, joined(groups[x]), across, sorted_rows)
            right = joined(groups[dy]) if lead is None else groups[dy][0][0]
            grad = dot_nn(sorted_rows[...], right).astype(jnp.bfloat16)
            send_ref, keep_ref = outs[2 * target], outs[2 * target + 1]
            send_ref[...] = grad[:half].reshape(send_ref.shape)
            keep_ref[...] = grad[half:].reshape(keep_ref.shape)


def grad_group(order, operands, plan, name):
    width = operands[0][0].shape[-1]
    rows = width // 16
    tokens = sum(a.shape[-2] for a in operands[0])
    in_specs = []
    for n, group in enumerate(operands):
        for a in group:
            if a.ndim == 2:
                in_specs.append(pl.BlockSpec(a.shape, lambda j, order: (0, 0)))
            else:
                first = min(i for i, p in enumerate(plan) if p[1] == n)
                in_specs.append(
                    pl.BlockSpec(
                        (1, *a.shape[1:]),
                        lambda j, order, first=first, last=a.shape[0] - 1: (
                            jnp.clip(j - first, 0, last),
                            0,
                            0,
                        ),
                    )
                )
    out_specs, out_shape = [], []
    for target in range(1 + max(p[3] for p in plan)):
        steps = [i for i, p in enumerate(plan) if p[3] == target]
        spec = pl.BlockSpec(
            (8, rows, width),
            lambda j, order, first=steps[0], last=len(steps) - 1: (
                0,
                jnp.clip(j - first, 0, last),
                0,
            ),
        )
        out_specs += [spec, spec]
        out_shape += [jax.ShapeDtypeStruct((8, rows * len(steps), width), jnp.bfloat16)] * 2
    outs = pl.pallas_call(
        functools.partial(group_kernel, plan, [len(g) for g in operands], len(out_specs)),
        grid_spec=pltpu.PrefetchScalarGridSpec(
            num_scalar_prefetch=1,
            grid=(len(plan),),
            in_specs=in_specs,
            out_specs=out_specs,
            scratch_shapes=[pltpu.VMEM((width, tokens), jnp.bfloat16)] * 2,
        ),
        out_shape=out_shape,
        compiler_params=pltpu.CompilerParams(vmem_limit_bytes=32 * 2**20),
        cost_estimate=NOTHING,
        name=name,
    )(order, *[a for group in operands for a in group])
    return [(outs[i], outs[i + 1]) for i in range(0, len(outs), 2)]


def add_kernel(count, *refs):
    at = 0
    for n in range(count):
        keep, arrived = refs[2 * n], refs[2 * n + 1]
        rows = keep.shape[-2]
        for i, out in enumerate(refs[2 * count :]):
            out[0, at : at + rows, :] = keep[i, 0] + arrived[i, 0]
        at += rows


def add_halves(keeps, arrivals, name="add"):
    pairs = keeps[0].shape[0] // 2
    width = keeps[0].shape[2]
    rows = sum(k.shape[1] for k in keeps)
    operands = []
    for keep, arrived in zip(keeps, arrivals):
        operands += [a.reshape(2, pairs, *a.shape[1:]) for a in (keep, arrived)]
    out = pl.BlockSpec((1, rows, width), lambda j: (j, 0, 0))
    return pl.pallas_call(
        functools.partial(add_kernel, len(keeps)),
        grid=(pairs,),
        in_specs=[
            pl.BlockSpec((2, 1, *a.shape[2:]), lambda j: (0, j, 0, 0)) for a in operands
        ],
        out_specs=[out, out],
        out_shape=[jax.ShapeDtypeStruct((pairs, rows, width), jnp.bfloat16)] * 2,
        compiler_params=pltpu.CompilerParams(vmem_limit_bytes=16 * 2**20),
        cost_estimate=NOTHING,
        name=name,
    )(*operands)


def last_kernel(keep_ref, arrived_ref, *outs):
    total = keep_ref[0].astype(jnp.float32) + arrived_ref[0].astype(jnp.float32)
    width = total.shape[1]
    at = 0
    for out in outs:
        rows, columns = out.shape
        for n in range(columns // width):
            out[:, n * width : (n + 1) * width] = total[at : at + rows]
            at += rows


def last_sum(keep, arrived, shapes):
    return pl.pallas_call(
        last_kernel,
        out_shape=[jax.ShapeDtypeStruct(s, jnp.float32) for s in shapes],
        compiler_params=pltpu.CompilerParams(vmem_limit_bytes=16 * 2**20),
        cost_estimate=NOTHING,
        name="last",
    )(keep, arrived)


def swap(x, bit):
    return lax.ppermute(x, "page", [(i, i ^ bit) for i in range(16)])


pin = lax.optimization_barrier


def on_device(
    block_input,
    cotangent,
    norm_gain,
    norm_bias,
    w_qkv,
    w_out,
    w_query,
    w_keyval,
    w_cross,
    w_up,
    b_up,
    w_down,
    b_down,
    row_page,
    lengths,
):
    x = block_input[0]
    dy = cotangent[0]
    tokens, width = x.shape
    half = tokens // 2
    pages = lax.axis_size("page")
    device = lax.axis_index("page")
    stream = lax.axis_index("stream")
    scales = norm_gain[0].T
    shifts = norm_bias[0].T
    share = width // pages
    padded = jnp.concatenate([row_page, row_page[:SHIFT]])
    info = jnp.concatenate(
        [
            stream.astype(jnp.int32)[None],
            lengths,
            lax.dynamic_slice_in_dim(padded, device * WIN + SHIFT, WIN),
        ]
    )
    stay = [(pages + i, pages + i) for i in range(pages)]
    both = ("stream", "page")
    forth = [((i + 1) % pages, i) for i in range(pages)] + stay
    back = [(i, (i + 1) % pages) for i in range(pages)] + stay

    def partner_of(rows):
        return lax.ppermute(rows, "stream", [(0, 1), (1, 0)])

    moved = jnp.concatenate([x[half:], lax.ppermute(x[:half], both, forth)])
    first, unit_one, inverse_one = layer_norm(moved.astype(jnp.float32), scales[0], shifts[0])
    packed = matmul(first, w_qkv[0]).astype(jnp.bfloat16)
    moved_mixed, self_probs = attn_fwd(
        info, packed, packed, packed, 0, 6, 12, fill_self_bias, "selff"
    )
    gone, near = moved_mixed[half:], moved_mixed[:half]
    after_gone = moved[half:].astype(jnp.float32) + matmul(gone, w_out[0])
    second_gone = layer_norm(after_gone, scales[1], shifts[1])[0]
    partner_top = lax.ppermute(
        second_gone,
        both,
        [(i, pages + (i + 1) % pages) for i in range(pages)]
        + [(pages + i, i) for i in range(pages)],
    )
    back_mixed = lax.ppermute(gone, both, back)
    after_low = moved[:half].astype(jnp.float32) + matmul(near, w_out[0])
    second_low = layer_norm(after_low, scales[1], shifts[1])[0]
    partner_low = partner_of(second_low)
    back_mixed, second_low, partner_top = pin((back_mixed, second_low, partner_top))
    after_top = x[:half].astype(jnp.float32) + matmul(back_mixed, w_out[0])
    second_top = layer_norm(after_top, scales[1], shifts[1])[0]
    after_self = jnp.concatenate([after_top, after_low])
    second = jnp.concatenate([second_top, second_low])
    cross_q = matmul(second, w_query[0]).astype(jnp.bfloat16)
    cross_q, after_self, partner_top, partner_low = pin(
        (cross_q, after_self, partner_top, partner_low)
    )
    partner = jnp.concatenate([partner_top, partner_low])
    cross_pair = matmul(partner, w_keyval[0]).astype(jnp.bfloat16)
    cross_mixed, cross_probs = attn_fwd(
        info, cross_q, cross_pair, cross_pair, 0, 0, 6, fill_cross_bias, "crossf"
    )
    if pages == 16:
        ordinal = jnp.arange(16, dtype=jnp.int32)
        turned = 15 - ordinal
        turned = (turned & 1) << 3 | (turned & 2) << 1 | (turned & 4) >> 1 | (turned & 8) >> 3
        order = device.astype(jnp.int32) ^ turned
        output, grad_third, after_cross, up_bias, down, up = feed_forward(
            order, after_self, cross_mixed, dy, scales, shifts, w_cross, w_up, b_up, w_down, b_down
        )
        grad_cross_in, cross_low, grad_cmix, sums_three = third_back(
            grad_third, after_cross, dy, scales, w_cross
        )

        def onward(keeps, sends, bit):
            return add_halves(keeps, [swap(s, bit) for s in sends])

        grad_cmix, down_keep, up_keep = pin((grad_cmix, down[1], up[1]))
        down = onward([down_keep], [down[0]], 1)
        up = onward([up_keep], [up[0]], 1)
        grad_cmix, down, up = pin((grad_cmix, down, up))
        cross_grads = attn_bwd(
            cross_q, cross_pair, cross_pair, 0, 0, 6, grad_cmix, cross_probs, "crossb"
        )

        def given(rows):
            keys = dot_nt(cross_grads[1, rows], w_keyval[0][:, :width])
            return (keys + dot_nt(cross_grads[2, rows], w_keyval[0][:, width:])).astype(jnp.bfloat16)

        returned_top = lax.ppermute(
            given(slice(0, half)),
            both,
            [(i, pages + i) for i in range(pages)]
            + [(pages + (i + 1) % pages, i) for i in range(pages)],
        )
        returned_low = partner_of(given(slice(half, tokens)))
        query_back = dot_nt(cross_grads[0], w_query[0])
        far_back = lax.ppermute(query_back[:half].astype(jnp.bfloat16), both, forth)
        far_grad = lax.ppermute(cross_low[:half], both, forth)
        (cross_part,) = grad_group(
            order,
            (
                (cross_mixed,),
                (second_top, second_low),
                (partner_top, partner_low),
                (cross_low,),
                (cross_grads,),
            ),
            ((0, 3, None, 0), (1, 4, 0, 0), (2, 4, 1, 0), (2, 4, 2, 0)),
            "gcross",
        )
        down = onward([down[1]], [down[0]], 4)
        up = onward([up[1]], [up[0]], 2)
        returned_top, returned_low, far_back, far_grad, cross_part, down, up = pin(
            (returned_top, returned_low, far_back, far_grad, cross_part, down, up)
        )
        low_near, low_far, sums_two = second_back(
            query_back, far_back, returned_low, returned_top, after_self, after_gone,
            grad_cross_in, far_grad, scales,
        )
        low_near, cross_keep = pin((low_near, cross_part[1]))
        cross_part = onward([cross_keep], [cross_part[0]], 1)
        low_near, cross_part = pin((low_near, cross_part))
        self_grads = self_back(packed, low_near, low_far, w_out, self_probs)
        self_grads, up_keep = pin((self_grads, up[1]))
        up = onward([up_keep], [up[0]], 4)
        self_grads, up = pin((self_grads, up))
        parts, input_stay, input_gone, sums_one = tail_grads(
            order, self_grads, w_qkv, first, moved_mixed, moved, low_near, low_far, scales
        )
        parts = [parts[1], parts[2], parts[0], parts[3]]
        parts, cross_keep, down_keep, up_keep = pin((parts, cross_part[1], down[1], up[1]))
        (grad_up,) = last_sum(up_keep, swap(up[0], 8), [(48, 4 * width)])
        down = onward([down_keep], [down[0]], 8)
        cross_part = onward([cross_keep], [cross_part[0]], 2)
        sends, keeps = [p[0] for p in parts], [p[1] for p in parts]
        cross_part, keeps, down, grad_up = pin((cross_part, keeps, down, grad_up))
        pair_part = onward(keeps[:2], sends[:2], 1)
        rest_part = onward(keeps[2:], sends[2:], 1)
        pair_part, rest_part, input_gone, sums_one = pin(
            (pair_part, rest_part, input_gone, sums_one)
        )
        input_top = lax.ppermute(input_gone, both, back)
        sums = jnp.concatenate(
            [sums_one[:2], sums_two[:2], sums_three[:3], up_bias.reshape(4, width)]
        )
        sums = sums + swap(sums, 1)
        pair_keep, sums = pin((pair_part[1], sums))
        pair_part = onward([pair_keep], [pair_part[0]], 2)
        cross_keep, pair_part = pin((cross_part[1], pair_part))
        cross_part = onward([cross_keep], [cross_part[0]], 4)
        cross_part, pair_keep = pin((cross_part, pair_part[1]))
        pair_part = onward([pair_keep], [pair_part[0]], 4)
        pair_part, cross_keep = pin((pair_part, cross_part[1]))
        grad_cross, grad_query, grad_keyval = last_sum(
            cross_keep,
            swap(cross_part[0], 8),
            [(48, width), (48, width), (48, 2 * width)],
        )
        rest_keep, grad_cross, grad_query, grad_keyval = pin(
            (rest_part[1], grad_cross, grad_query, grad_keyval)
        )
        rest_part = onward([rest_keep], [rest_part[0]], 2)
        sums = sums + swap(sums, 2)
        rest_keep, pair_keep, sums = pin((rest_part[1], pair_part[1], sums))
        rest_part = onward([rest_keep], [rest_part[0]], 4)
        (grad_pair,) = last_sum(pair_keep, swap(pair_part[0], 8), [(48, 2 * width)])
        (grad_down,) = last_sum(down[1], swap(down[0], 2), [(192, width)])
        sums = sums + swap(sums, 4)
        rest_part, sums, grad_pair, grad_down = pin((rest_part, sums, grad_pair, grad_down))
        grad_first, grad_out = last_sum(
            rest_part[1], swap(rest_part[0], 8), [(48, width), (48, width)]
        )
        sums = sums + swap(sums, 8)
        grad_qkv = jnp.concatenate([grad_first, grad_pair], 1)
        mine = lax.dynamic_slice_in_dim(sums[:7], device * share, share, 1)
        gains, biases = mine[0:6:2], mine[1:6:2]
        down_bias = mine[6]
        up_bias = lax.dynamic_slice_in_dim(sums[7:].reshape(-1), device * 192, 192)
        input_grad = jnp.concatenate([input_top, input_stay])
    else:
        _, unit_two, inverse_two = layer_norm(after_self, scales[1], shifts[1])
        after_cross = after_self + matmul(cross_mixed, w_cross[0])
        third, unit_three, inverse_three = layer_norm(after_cross, scales[2], shifts[2])
        value, slope = gelu_pair(matmul(third, w_up[0]) + b_up[0])
        hidden = value.astype(jnp.bfloat16)
        output = (after_cross + matmul(hidden, w_down[0]) + b_down[0]).astype(jnp.bfloat16)
        upstream = dy.astype(jnp.float32)
        pre_low = (dot_nt(dy, w_down[0]) * slope).astype(jnp.bfloat16)
        back_three, gain_three, shift_three = norm_back(
            dot_nt(pre_low, w_up[0]), unit_three, inverse_three, scales[2]
        )
        grad_cross_in = upstream + back_three
        cross_low = grad_cross_in.astype(jnp.bfloat16)
        grad_cmix = dot_nt(cross_low, w_cross[0]).astype(jnp.bfloat16)
        cross_grads = attn_bwd(
            cross_q, cross_pair, cross_pair, 0, 0, 6, grad_cmix, cross_probs, "crossb"
        )
        pair = jnp.concatenate([cross_grads[1], cross_grads[2]], 1)
        returned = partner_of(dot_nt(pair, w_keyval[0]).astype(jnp.bfloat16))
        back_two, gain_two, shift_two = norm_back(
            dot_nt(cross_grads[0], w_query[0]) + returned.astype(jnp.float32),
            unit_two,
            inverse_two,
            scales[1],
        )
        self_low = (grad_cross_in + back_two).astype(jnp.bfloat16)
        moved_low = jnp.concatenate([self_low[half:], lax.ppermute(self_low[:half], both, forth)])
        grad_smix = dot_nt(moved_low, w_out[0]).astype(jnp.bfloat16)
        self_grads = attn_bwd(packed, packed, packed, 0, 6, 12, grad_smix, self_probs, "selfb")
        packed_grad = jnp.concatenate([self_grads[0], self_grads[1], self_grads[2]], 1)
        back_one, gain_one, shift_one = norm_back(
            dot_nt(packed_grad, w_qkv[0]), unit_one, inverse_one, scales[0]
        )
        moved_grad = (moved_low.astype(jnp.float32) + back_one).astype(jnp.bfloat16)
        input_grad = jnp.concatenate([lax.ppermute(moved_grad[half:], both, back), moved_grad[:half]])

        def summed(grad):
            return lax.psum_scatter(grad, "page", scatter_dimension=0, tiled=True)

        def scattered(left, right):
            return summed(
                lax.dot_general(
                    left, right, (((0,), (0,)), ((), ())), preferred_element_type=jnp.float32
                )
            )

        grad_down = scattered(hidden, dy)
        grad_up = scattered(third, pre_low)
        grad_cross = scattered(cross_mixed, cross_low)
        grad_query = scattered(second, cross_grads[0])
        grad_keyval = scattered(partner, pair)
        grad_out = scattered(jnp.concatenate([back_mixed, near]), self_low)
        grad_qkv = scattered(first, packed_grad)
        gains = summed(jnp.stack([gain_one, gain_two, gain_three], 1)).T
        biases = summed(jnp.stack([shift_one, shift_two, shift_three], 1)).T
        down_bias = summed(jnp.sum(upstream, axis=0))
        up_bias = summed(jnp.sum(pre_low.astype(jnp.float32), axis=0))
    return (
        output[None],
        input_grad[None],
        gains.T[None],
        biases.T[None],
        grad_qkv[None],
        grad_out[None],
        grad_query[None],
        grad_keyval[None],
        grad_cross[None],
        grad_up[None],
        up_bias[None],
        grad_down[None],
        down_bias[None],
    )


def solution(mesh):
    tokens = P("stream", "page", None)
    whole = P("stream", None, None)
    placed = (tokens, tokens) + (whole,) * 8 + (P("stream", None), whole, P("stream", None))
    return jax.shard_map(
        on_device,
        mesh=mesh,
        in_specs=placed + (P(), P("page")),
        out_specs=(tokens,) * 10 + (P("stream", "page"), tokens, P("stream", "page")),
        check_vma=False,
    )
```

```python
import functools

import jax
import jax.numpy as jnp
from jax import lax
from jax.experimental import pallas as pl
from jax.experimental.pallas import tpu as pltpu
from jax.sharding import PartitionSpec as P

HEADS = 12
HEAD = 64
WIN = 12
SHIFT = 6
NORM_EPS = 1e-05
MASKED = -1e30


def dot_nt(a,b):
    return lax.dot_general(a,b,(((1,),(1,)),((),())),preferred_element_type=jnp.float32)
def dot_nn(a,b):
    return lax.dot_general(a,b,(((1,),(0,)),((),())),preferred_element_type=jnp.float32)

def fill_self_bias(info, bias, first=0):
    tokens, count = bias.shape
    half=tokens//2
    cols=tokens//12
    def codes(shape,dim,start):
        t=lax.broadcasted_iota(jnp.int32,shape,dim)+start
        row=jnp.zeros(shape,jnp.int32)
        page=jnp.full(shape,info[2],jnp.int32)
        for r in range(1,12):
            inside=t>=r*cols
            row=jnp.where(inside,r,row)
            page=jnp.where(inside,info[2+r],page)
        c=t-row*cols
        win=jnp.zeros(shape,jnp.int32)
        for w in range(1,cols//12):
            win=jnp.where((c>=6+12*(w-1))&(c<6+12*w),w,win)
        win=jnp.where(c>=cols-6,cols//12+1,win)
        slot=jnp.where(t<half,t+half,t-half)
        return page*16+win,slot
    ck,sk=codes((tokens,1),0,0)
    cq,sq=codes((1,count),1,first)
    length=info[1]
    @pl.when(info[0]==1)
    def _():
        ok=(sk<=sq)&(sk<length)
        bias[...]=jnp.where(ok,0.0,MASKED)
    @pl.when(info[0]==0)
    def _():
        bias[...]=jnp.where(ck==cq,0.0,MASKED)

def fill_cross_bias(info,bias,first=0):
    tokens=bias.shape[0]
    t=lax.broadcasted_iota(jnp.int32,bias.shape,0)
    bias[...]=jnp.where((t<info[1])|(info[0]==1),0.0,MASKED)

def lane_pick(e,scale):
    lane=lax.broadcasted_iota(jnp.int32,(1,2*HEAD),1)
    return jnp.where((lane>=HEAD)==bool(e),scale,0.0).astype(jnp.bfloat16)

def fwd_kernel(fill, info, q_ref, k_ref, v_ref, o_ref, p_ref, bias):
    @pl.when(pl.program_id(0) == 0)
    def _():
        fill(info, bias)

    q, k = q_ref[...], k_ref[...]
    vt = v_ref[...].T
    scores = [dot_nt(k, q * lane_pick(e, HEAD**-0.5)) + bias[...] for e in range(2)]
    outs = []
    for e in range(2):
        weights = jnp.exp(scores[e] - jnp.max(scores[e], axis=0, keepdims=True))
        inverse = 1.0 / jnp.sum(weights, axis=0, keepdims=True)
        probs = (weights * inverse).astype(jnp.bfloat16)
        p_ref[e] = probs
        outs.append(dot_nn(vt[e * HEAD : (e + 1) * HEAD], probs))
    o_ref[...] = jnp.concatenate(outs, 0).T.astype(jnp.bfloat16)


NOTHING = pl.CostEstimate(flops=1000, bytes_accessed=1000, transcendentals=0)


def attn_fwd(info, q, k, v, qo, ko, vo, fill, name):
    tokens = q.shape[0]
    spec = lambda off: pl.BlockSpec((tokens, 128), lambda j, info: (0, off + j))
    return pl.pallas_call(
        functools.partial(fwd_kernel, fill),
        grid_spec=pltpu.PrefetchScalarGridSpec(
            num_scalar_prefetch=1,
            grid=(HEADS // 2,),
            in_specs=[spec(qo), spec(ko), spec(vo)],
            out_specs=[spec(0), pl.BlockSpec((2, tokens, tokens), lambda j, info: (j, 0, 0))],
            scratch_shapes=[pltpu.VMEM((tokens, tokens), jnp.float32)],
        ),
        out_shape=[
            jax.ShapeDtypeStruct((tokens, HEADS * HEAD), jnp.bfloat16),
            pltpu.HBM((HEADS, tokens, tokens), jnp.bfloat16),
        ],
        compiler_params=pltpu.CompilerParams(vmem_limit_bytes=24 * 2**20),
        cost_estimate=NOTHING,
        name=name,
    )(info, q, k, v)


def bwd_kernel(q_ref, k_ref, v_ref, do_ref, p_ref, d_ref):
    grads = backward_heads(q_ref[...], k_ref[...], v_ref[...], do_ref[...], p_ref)
    for i in range(3):
        d_ref[i] = grads[i]


def attn_bwd(q, k, v, qo, ko, vo, do, probs, name):
    tokens = q.shape[0]
    spec = lambda off: pl.BlockSpec((tokens, 128), lambda j: (0, off + j))
    return pl.pallas_call(
        bwd_kernel,
        grid=(HEADS // 2,),
        in_specs=[spec(qo), spec(ko), spec(vo), spec(0)]
        + [pl.BlockSpec((2, tokens, tokens), lambda j: (j, 0, 0))],
        out_specs=pl.BlockSpec((3, tokens, 128), lambda j: (0, 0, j)),
        out_shape=jax.ShapeDtypeStruct((3, tokens, HEADS * HEAD), jnp.bfloat16),
        compiler_params=pltpu.CompilerParams(vmem_limit_bytes=24 * 2**20),
        cost_estimate=NOTHING,
        name=name,
    )(q, k, v, do, pltpu.with_memory_space_constraint(probs, pltpu.HBM))


def layer_norm(inputs, scales, shifts):
    average = jnp.mean(inputs, axis=1, keepdims=True)
    centred = inputs - average
    spread = jnp.mean(centred * centred, axis=1, keepdims=True)
    inverse = lax.rsqrt(spread + NORM_EPS)
    unit = centred * inverse
    return (unit * scales + shifts).astype(jnp.bfloat16), unit, inverse


def norm_back(upstream, unit, inverse, scales):
    scaled = upstream * scales
    inner = (
        scaled
        - jnp.mean(scaled, axis=1, keepdims=True)
        - unit * jnp.mean(scaled * unit, axis=1, keepdims=True)
    )
    return (inverse * inner, jnp.sum(upstream * unit, axis=0), jnp.sum(upstream, axis=0))


def matmul(left, right):
    return jnp.dot(left, right, preferred_element_type=jnp.float32)


def gelu_pair(pre):
    root = 0.7978845608028654
    square = pre * pre
    gate = 0.5 + 0.5 * jnp.tanh(pre * (root + root * 0.044715 * square))
    value = pre * gate
    return value, gate + value * (1.0 - gate) * (2 * root + 6 * root * 0.044715 * square)


def layer_parts(v):
    average = jnp.mean(v, axis=1, keepdims=True)
    centred = v - average
    inverse = lax.rsqrt(jnp.mean(centred * centred, axis=1, keepdims=True) + NORM_EPS)
    return centred * inverse, inverse


def layer_back(grad, unit, inverse, scale):
    scaled = grad * scale
    return inverse * (
        scaled
        - jnp.mean(scaled, axis=1, keepdims=True)
        - unit * jnp.mean(scaled * unit, axis=1, keepdims=True)
    )


def column_sums(*values):
    rows = [jnp.sum(v, axis=0, keepdims=True) for v in values]
    rows.append(jnp.zeros((8 - len(rows), rows[0].shape[1]), jnp.float32))
    return jnp.concatenate(rows)


def sort_rows(order, x, across, sorted_rows):
    rows = sorted_rows.shape[0] // 16
    across[...] = x.T
    for n in range(16):
        start = pl.multiple_of(order[n] * rows, 16)
        sorted_rows[n * rows : (n + 1) * rows, :] = across[pl.ds(start, rows), :]


def feed_kernel(
    order, after_ref, mixed_ref, dy_ref, scales_ref, shifts_ref, cross_ref, down_bias_ref,
    up_ref, up_bias_ref, down_ref,
    out_ref, grad_ref, kept_ref, bias_ref,
    down_send, down_keep, up_send, up_keep,
    third_rows, across, sorted_rows, after, total, grad_total,
):
    step = pl.program_id(0)
    rows = dy_ref.shape[1] // 16
    half = 8 * rows

    @pl.when(step == 0)
    def _():
        after[...] = after_ref[...] + dot_nn(mixed_ref[...], cross_ref[0])
        unit = layer_parts(after[...])[0]
        third_rows[...] = (unit * scales_ref[2:3, :] + shifts_ref[2:3, :]).astype(jnp.bfloat16)
        sort_rows(order, third_rows[...], across, sorted_rows)
        total[...] = after[...] + down_bias_ref[...]
        grad_total[...] = jnp.zeros_like(grad_total)

    dy, third = dy_ref[...], third_rows[...]
    tile = up_ref.shape[2] // 2
    deep = tile // 2
    parts = [slice(0, tile), slice(tile, 2 * tile)]
    pre = [dot_nn(third, up_ref[0, :, p]) + up_bias_ref[:, p] for p in parts]
    grad_hidden = [dot_nt(dy, down_ref[0, p, :]) for p in parts]
    out = grad_third = 0.0
    grads = []
    for i, p in enumerate(parts):
        value, slope = gelu_pair(pre[i])
        hidden = value.astype(jnp.bfloat16)
        low = (grad_hidden[i] * slope).astype(jnp.bfloat16)
        bias_ref[0, :, p] = jnp.sum(low.astype(jnp.float32), axis=0, keepdims=True)
        grad = dot_nn(sorted_rows[...], low).astype(jnp.bfloat16)
        up_send[:, :, p] = grad[:half].reshape(8, rows, tile)
        up_keep[:, :, p] = grad[half:].reshape(8, rows, tile)
        grads.append(dot_nn(hidden.T, dy).astype(jnp.bfloat16))
        out += dot_nn(hidden, down_ref[0, p, :])
        grad_third += dot_nt(low, up_ref[0, :, p])
    total[...] += out
    grad_total[...] += grad_third
    for odd in range(2):
        for far in range(2):

            @pl.when((order[15] % 2 == odd) & (order[15] // 2 % 2 == far))
            def _():
                for n in range(2):
                    both = grads[n ^ far ^ 1]
                    down_send[n] = both[deep * (1 - odd) : deep * (2 - odd)]
                    down_keep[n] = both[deep * odd : deep * (odd + 1)]

    @pl.when(step == pl.num_programs(0) - 1)
    def _():
        out_ref[...] = total[...].astype(jnp.bfloat16)
        grad_ref[...] = grad_total[...]
        kept_ref[...] = after[...]


def third_kernel(third_ref, after_ref, dy_ref, scales_ref, cross_ref, grad_ref, low_ref, mix_ref, sums_ref):
    upstream = dy_ref[...].astype(jnp.float32)
    unit, inverse = layer_parts(after_ref[...])
    grad = third_ref[...]
    sums_ref[...] = column_sums(grad * unit, grad, upstream)
    grad_ref[...] = upstream + layer_back(grad, unit, inverse, scales_ref[2:3, :])
    low_ref[...] = grad_ref[...].astype(jnp.bfloat16)
    mix_ref[...] = dot_nt(low_ref[...], cross_ref[0]).astype(jnp.bfloat16)


def third_back(grad, after, dy, scales, w_cross):
    full = jax.ShapeDtypeStruct(after.shape, jnp.float32)
    low = jax.ShapeDtypeStruct(after.shape, jnp.bfloat16)
    return pl.pallas_call(
        third_kernel,
        out_shape=[full, low, low, jax.ShapeDtypeStruct((8, after.shape[1]), jnp.float32)],
        compiler_params=pltpu.CompilerParams(vmem_limit_bytes=32 * 2**20),
        cost_estimate=NOTHING,
        name="third",
    )(grad, after, dy, scales, w_cross)


def feed_forward(order, after, mixed, dy, scales, shifts, w_cross, w_up, b_up, w_down, b_down):
    tokens, width = dy.shape
    deep = w_up.shape[2]
    tile = deep // 4
    rows = width // 16
    whole = lambda *shape: pl.BlockSpec(shape, lambda j, order: (0,) * len(shape))
    where = lambda j, order: order[8 + j] // 4
    once = lambda *shape: pl.BlockSpec(
        shape, lambda j, order: (0,) * len(shape), pipeline_mode=pl.Buffered(1)
    )
    token = once(tokens, width)
    down_half = jax.ShapeDtypeStruct((8, deep // 16, width), jnp.bfloat16)
    up_half = jax.ShapeDtypeStruct((8, 4 * rows, tile), jnp.bfloat16)
    down_piece = pl.BlockSpec((2, deep // 16, width), lambda j, order: (j, 0, 0))
    up_piece = pl.BlockSpec((8, rows, tile), lambda j, order: (0, where(j, order), 0))
    low = jax.ShapeDtypeStruct((tokens, width), jnp.bfloat16)
    full = jax.ShapeDtypeStruct((tokens, width), jnp.float32)
    out = pl.pallas_call(
        feed_kernel,
        grid_spec=pltpu.PrefetchScalarGridSpec(
            num_scalar_prefetch=1,
            grid=(4,),
            in_specs=[
                token,
                token,
                token,
                whole(3, width),
                whole(3, width),
                once(1, width, width),
                whole(1, width),
                pl.BlockSpec((1, width, tile), lambda j, order: (0, 0, where(j, order))),
                pl.BlockSpec((1, tile), lambda j, order: (0, where(j, order))),
                pl.BlockSpec((1, tile, width), lambda j, order: (0, where(j, order), 0)),
            ],
            out_specs=[
                token,
                token,
                token,
                pl.BlockSpec((1, 1, tile), lambda j, order: (where(j, order), 0, 0)),
                down_piece,
                down_piece,
                up_piece,
                up_piece,
            ],
            scratch_shapes=[pltpu.VMEM((tokens, width), jnp.bfloat16)]
            + [pltpu.VMEM((width, tokens), jnp.bfloat16)] * 2
            + [pltpu.VMEM((tokens, width), jnp.float32)] * 3,
        ),
        out_shape=[
            low,
            full,
            full,
            jax.ShapeDtypeStruct((4, 1, tile), jnp.float32),
            down_half,
            down_half,
            up_half,
            up_half,
        ],
        compiler_params=pltpu.CompilerParams(vmem_limit_bytes=36 * 2**20),
        cost_estimate=NOTHING,
        name="feed",
    )(order, after, mixed, dy, scales, shifts, w_cross, b_down, w_up, b_up, w_down)
    return (*out[:4], (out[4], out[5]), (out[6], out[7]))


def backward_heads(q, k, v, do, p_ref):
    kt = k.T
    queries = []
    keys = values = 0.0
    picked = [do * lane_pick(e, 1.0) for e in range(2)]
    grads = [dot_nt(v, picked[e]) for e in range(2)]
    for e in range(2):
        probs = p_ref[e]
        wide = probs.astype(jnp.float32)
        part = wide * grads[e]
        total = jnp.sum(part, axis=0, keepdims=True)
        ds = (part - wide * total).astype(jnp.bfloat16)
        values += dot_nn(probs, picked[e])
        keys += dot_nn(ds, q * lane_pick(e, HEAD**-0.5))
        queries.append(dot_nn(kt[e * HEAD : (e + 1) * HEAD], ds) * HEAD**-0.5)
    queries = jnp.concatenate(queries, 0).T
    return [g.astype(jnp.bfloat16) for g in (queries, keys, values)]


def self_back_kernel(q_ref, k_ref, v_ref, near_ref, far_ref, out_ref, p_ref, d_ref):
    low = jnp.concatenate([near_ref[...], far_ref[...]])
    do = dot_nt(low, out_ref[0]).astype(jnp.bfloat16)
    grads = backward_heads(q_ref[...], k_ref[...], v_ref[...], do, p_ref)
    for i in range(3):
        d_ref[i] = grads[i]


def self_back(packed, near, far, w_out, probs):
    tokens, width = packed.shape[0], near.shape[1]
    spec = lambda off: pl.BlockSpec((tokens, 128), lambda j: (0, off + j))
    rows = pl.BlockSpec(near.shape, lambda j: (0, 0))
    return pl.pallas_call(
        self_back_kernel,
        grid=(HEADS // 2,),
        in_specs=[spec(0), spec(6), spec(12), rows, rows]
        + [pl.BlockSpec((1, 128, width), lambda j: (0, j, 0))]
        + [pl.BlockSpec((2, tokens, tokens), lambda j: (j, 0, 0))],
        out_specs=pl.BlockSpec((3, tokens, 128), lambda j: (0, 0, j)),
        out_shape=jax.ShapeDtypeStruct((3, tokens, width), jnp.bfloat16),
        compiler_params=pltpu.CompilerParams(vmem_limit_bytes=24 * 2**20),
        cost_estimate=NOTHING,
        name="selfb",
    )(packed, packed, packed, near, far, w_out, pltpu.with_memory_space_constraint(probs, pltpu.HBM))


def second_kernel(
    near_back_ref, far_back_ref, near_given_ref, far_given_ref, near_after_ref, far_after_ref,
    near_grad_ref, far_grad_ref, scales_ref, near_ref, far_ref, sums_ref,
):
    sums = 0.0
    for back, given, after, grad, out in (
        (near_back_ref, near_given_ref, near_after_ref, near_grad_ref, near_ref),
        (far_back_ref, far_given_ref, far_after_ref, far_grad_ref, far_ref),
    ):
        unit, inverse = layer_parts(after[...])
        upstream = back[...].astype(jnp.float32) + given[...].astype(jnp.float32)
        sums += column_sums(upstream * unit, upstream)
        below = layer_back(upstream, unit, inverse, scales_ref[1:2, :])
        out[...] = (grad[...].astype(jnp.float32) + below).astype(jnp.bfloat16)
    sums_ref[...] = sums


def second_back(back, far_back, near_given, far_given, after, far_after, grad, far_grad, scales):
    half, width = near_given.shape
    low = pl.BlockSpec((half, width), lambda j: (1, 0))
    rows = pl.BlockSpec((half, width), lambda j: (0, 0))
    out = jax.ShapeDtypeStruct((half, width), jnp.bfloat16)
    return pl.pallas_call(
        second_kernel,
        grid=(1,),
        in_specs=[low, rows, rows, rows, low, rows, low, rows]
        + [pl.BlockSpec((3, width), lambda j: (0, 0))],
        out_specs=[rows, rows, pl.BlockSpec((8, width), lambda j: (0, 0))],
        out_shape=[out, out, jax.ShapeDtypeStruct((8, width), jnp.float32)],
        compiler_params=pltpu.CompilerParams(vmem_limit_bytes=24 * 2**20),
        cost_estimate=NOTHING,
        name="second",
    )(back, far_back, near_given, far_given, after, far_after, grad, far_grad, scales)


def tail_kernel(
    order, d_ref, w_ref, first_ref, mixed_ref, moved_ref, near_ref, far_ref, scales_ref, *refs,
):
    step = pl.program_id(0)
    stay_ref, gone_ref, sums_ref = refs[8:11]
    across, sorted_rows, total = refs[11:]
    half = sorted_rows.shape[0] // 2

    @pl.when(step == 0)
    def _():
        sort_rows(order, first_ref[...], across, sorted_rows)

    for i in range(3):

        @pl.when(step == i)
        def _():
            part = dot_nt(d_ref[0], w_ref[0])
            grad = dot_nn(sorted_rows[...], d_ref[0]).astype(jnp.bfloat16)
            refs[2 * i][...] = grad[:half].reshape(refs[0].shape)
            refs[2 * i + 1][...] = grad[half:].reshape(refs[0].shape)
            if i == 0:
                total[...] = part
            else:
                total[...] += part

    @pl.when(step == 3)
    def _():
        sort_rows(order, mixed_ref[...], across, sorted_rows)
        low = jnp.concatenate([near_ref[...], far_ref[...]])
        grad = dot_nn(sorted_rows[...], low).astype(jnp.bfloat16)
        refs[6][...] = grad[:half].reshape(refs[0].shape)
        refs[7][...] = grad[half:].reshape(refs[0].shape)
        rows = stay_ref.shape[0]
        unit, inverse = layer_parts(moved_ref[...].astype(jnp.float32))
        grad = total[...]
        sums_ref[...] = column_sums(grad * unit, grad)
        back = layer_back(grad, unit, inverse, scales_ref[0:1, :])
        stay_ref[...] = (near_ref[...].astype(jnp.float32) + back[:rows]).astype(jnp.bfloat16)
        gone_ref[...] = (far_ref[...].astype(jnp.float32) + back[rows:]).astype(jnp.bfloat16)


def tail_grads(order, grads, w_qkv, first, mixed, moved, near, far, scales):
    tokens, width = moved.shape
    half = tokens // 2
    whole = lambda *shape: pl.BlockSpec(shape, lambda j, order: (0,) * len(shape))
    rows = jax.ShapeDtypeStruct((half, width), jnp.bfloat16)
    piece = (8, width // 16, width)
    last = lambda j: jnp.minimum(j, 2)
    outs = pl.pallas_call(
        tail_kernel,
        grid_spec=pltpu.PrefetchScalarGridSpec(
            num_scalar_prefetch=1,
            grid=(4,),
            in_specs=[
                pl.BlockSpec((1, tokens, width), lambda j, order: (last(j), 0, 0)),
                pl.BlockSpec((1, width, width), lambda j, order: (0, 0, last(j))),
                whole(tokens, width),
                whole(tokens, width),
                whole(tokens, width),
                whole(half, width),
                whole(half, width),
                whole(3, width),
            ],
            out_specs=[whole(*piece)] * 8 + [whole(half, width)] * 2 + [whole(8, width)],
            scratch_shapes=[pltpu.VMEM((width, tokens), jnp.bfloat16)] * 2
            + [pltpu.VMEM((tokens, width), jnp.float32)],
        ),
        out_shape=[jax.ShapeDtypeStruct(piece, jnp.bfloat16)] * 8
        + [rows, rows, jax.ShapeDtypeStruct((8, width), jnp.float32)],
        compiler_params=pltpu.CompilerParams(vmem_limit_bytes=40 * 2**20),
        cost_estimate=NOTHING,
        name="tail",
    )(order, grads, w_qkv, first, mixed, moved, near, far, scales)
    return [(outs[i], outs[i + 1]) for i in range(0, 8, 2)], *outs[8:]


def group_kernel(plan, halves, pieces, order, *refs):
    refs = list(refs)
    groups = [[refs.pop(0) for _ in range(n)] for n in halves]
    joined = lambda group: jnp.concatenate([r[...] for r in group]) if len(group) > 1 else group[0][...]
    outs, (across, sorted_rows) = refs[:-2], refs[-2:]
    half = sorted_rows.shape[0] // 2
    before = None
    for i, (x, dy, lead, target) in enumerate(plan):
        turn = x != before
        before = x

        @pl.when(pl.program_id(0) == i)
        def _():
            if turn:
                sort_rows(order, joined(groups[x]), across, sorted_rows)
            right = joined(groups[dy]) if lead is None else groups[dy][0][0]
            grad = dot_nn(sorted_rows[...], right).astype(jnp.bfloat16)
            send_ref, keep_ref = outs[2 * target], outs[2 * target + 1]
            send_ref[...] = grad[:half].reshape(send_ref.shape)
            keep_ref[...] = grad[half:].reshape(keep_ref.shape)


def grad_group(order, operands, plan, name):
    width = operands[0][0].shape[-1]
    rows = width // 16
    tokens = sum(a.shape[-2] for a in operands[0])
    in_specs = []
    for n, group in enumerate(operands):
        for a in group:
            if a.ndim == 2:
                in_specs.append(pl.BlockSpec(a.shape, lambda j, order: (0, 0)))
            else:
                first = min(i for i, p in enumerate(plan) if p[1] == n)
                in_specs.append(
                    pl.BlockSpec(
                        (1, *a.shape[1:]),
                        lambda j, order, first=first, last=a.shape[0] - 1: (
                            jnp.clip(j - first, 0, last),
                            0,
                            0,
                        ),
                    )
                )
    out_specs, out_shape = [], []
    for target in range(1 + max(p[3] for p in plan)):
        steps = [i for i, p in enumerate(plan) if p[3] == target]
        spec = pl.BlockSpec(
            (8, rows, width),
            lambda j, order, first=steps[0], last=len(steps) - 1: (
                0,
                jnp.clip(j - first, 0, last),
                0,
            ),
        )
        out_specs += [spec, spec]
        out_shape += [jax.ShapeDtypeStruct((8, rows * len(steps), width), jnp.bfloat16)] * 2
    outs = pl.pallas_call(
        functools.partial(group_kernel, plan, [len(g) for g in operands], len(out_specs)),
        grid_spec=pltpu.PrefetchScalarGridSpec(
            num_scalar_prefetch=1,
            grid=(len(plan),),
            in_specs=in_specs,
            out_specs=out_specs,
            scratch_shapes=[pltpu.VMEM((width, tokens), jnp.bfloat16)] * 2,
        ),
        out_shape=out_shape,
        compiler_params=pltpu.CompilerParams(vmem_limit_bytes=32 * 2**20),
        cost_estimate=NOTHING,
        name=name,
    )(order, *[a for group in operands for a in group])
    return [(outs[i], outs[i + 1]) for i in range(0, len(outs), 2)]


def add_kernel(count, *refs):
    at = 0
    for n in range(count):
        keep, arrived = refs[2 * n], refs[2 * n + 1]
        rows = keep.shape[-2]
        for i, out in enumerate(refs[2 * count :]):
            out[0, at : at + rows, :] = keep[i, 0] + arrived[i, 0]
        at += rows


def add_halves(keeps, arrivals, name="add"):
    pairs = keeps[0].shape[0] // 2
    width = keeps[0].shape[2]
    rows = sum(k.shape[1] for k in keeps)
    operands = []
    for keep, arrived in zip(keeps, arrivals):
        operands += [a.reshape(2, pairs, *a.shape[1:]) for a in (keep, arrived)]
    out = pl.BlockSpec((1, rows, width), lambda j: (j, 0, 0))
    return pl.pallas_call(
        functools.partial(add_kernel, len(keeps)),
        grid=(pairs,),
        in_specs=[
            pl.BlockSpec((2, 1, *a.shape[2:]), lambda j: (0, j, 0, 0)) for a in operands
        ],
        out_specs=[out, out],
        out_shape=[jax.ShapeDtypeStruct((pairs, rows, width), jnp.bfloat16)] * 2,
        compiler_params=pltpu.CompilerParams(vmem_limit_bytes=16 * 2**20),
        cost_estimate=NOTHING,
        name=name,
    )(*operands)


def last_kernel(keep_ref, arrived_ref, *outs):
    total = keep_ref[0].astype(jnp.float32) + arrived_ref[0].astype(jnp.float32)
    width = total.shape[1]
    at = 0
    for out in outs:
        rows, columns = out.shape
        for n in range(columns // width):
            out[:, n * width : (n + 1) * width] = total[at : at + rows]
            at += rows


def last_sum(keep, arrived, shapes):
    return pl.pallas_call(
        last_kernel,
        out_shape=[jax.ShapeDtypeStruct(s, jnp.float32) for s in shapes],
        compiler_params=pltpu.CompilerParams(vmem_limit_bytes=16 * 2**20),
        cost_estimate=NOTHING,
        name="last",
    )(keep, arrived)


def swap(x, bit):
    return lax.ppermute(x, "page", [(i, i ^ bit) for i in range(16)])


pin = lax.optimization_barrier


def on_device(
    block_input,
    cotangent,
    norm_gain,
    norm_bias,
    w_qkv,
    w_out,
    w_query,
    w_keyval,
    w_cross,
    w_up,
    b_up,
    w_down,
    b_down,
    row_page,
    lengths,
):
    x = block_input[0]
    dy = cotangent[0]
    tokens, width = x.shape
    half = tokens // 2
    pages = lax.axis_size("page")
    device = lax.axis_index("page")
    stream = lax.axis_index("stream")
    scales = norm_gain[0].T
    shifts = norm_bias[0].T
    share = width // pages
    padded = jnp.concatenate([row_page, row_page[:SHIFT]])
    info = jnp.concatenate(
        [
            stream.astype(jnp.int32)[None],
            lengths,
            lax.dynamic_slice_in_dim(padded, device * WIN + SHIFT, WIN),
        ]
    )
    stay = [(pages + i, pages + i) for i in range(pages)]
    both = ("stream", "page")
    forth = [((i + 1) % pages, i) for i in range(pages)] + stay
    back = [(i, (i + 1) % pages) for i in range(pages)] + stay

    def partner_of(rows):
        return lax.ppermute(rows, "stream", [(0, 1), (1, 0)])

    moved = jnp.concatenate([x[half:], lax.ppermute(x[:half], both, forth)])
    first, unit_one, inverse_one = layer_norm(moved.astype(jnp.float32), scales[0], shifts[0])
    packed = matmul(first, w_qkv[0]).astype(jnp.bfloat16)
    moved_mixed, self_probs = attn_fwd(
        info, packed, packed, packed, 0, 6, 12, fill_self_bias, "selff"
    )
    gone, near = moved_mixed[half:], moved_mixed[:half]
    after_gone = moved[half:].astype(jnp.float32) + matmul(gone, w_out[0])
    second_gone = layer_norm(after_gone, scales[1], shifts[1])[0]
    partner_top = lax.ppermute(
        second_gone,
        both,
        [(i, pages + (i + 1) % pages) for i in range(pages)]
        + [(pages + i, i) for i in range(pages)],
    )
    back_mixed = lax.ppermute(gone, both, back)
    after_low = moved[:half].astype(jnp.float32) + matmul(near, w_out[0])
    second_low = layer_norm(after_low, scales[1], shifts[1])[0]
    partner_low = partner_of(second_low)
    back_mixed, second_low, partner_top = pin((back_mixed, second_low, partner_top))
    after_top = x[:half].astype(jnp.float32) + matmul(back_mixed, w_out[0])
    second_top = layer_norm(after_top, scales[1], shifts[1])[0]
    after_self = jnp.concatenate([after_top, after_low])
    second = jnp.concatenate([second_top, second_low])
    cross_q = matmul(second, w_query[0]).astype(jnp.bfloat16)
    cross_q, after_self, partner_top, partner_low = pin(
        (cross_q, after_self, partner_top, partner_low)
    )
    partner = jnp.concatenate([partner_top, partner_low])
    cross_pair = matmul(partner, w_keyval[0]).astype(jnp.bfloat16)
    cross_mixed, cross_probs = attn_fwd(
        info, cross_q, cross_pair, cross_pair, 0, 0, 6, fill_cross_bias, "crossf"
    )
    if pages == 16:
        ordinal = jnp.arange(16, dtype=jnp.int32)
        turned = 15 - ordinal
        turned = (turned & 1) << 3 | (turned & 2) << 1 | (turned & 4) >> 1 | (turned & 8) >> 3
        order = device.astype(jnp.int32) ^ turned
        output, grad_third, after_cross, up_bias, down, up = feed_forward(
            order, after_self, cross_mixed, dy, scales, shifts, w_cross, w_up, b_up, w_down, b_down
        )
        grad_cross_in, cross_low, grad_cmix, sums_three = third_back(
            grad_third, after_cross, dy, scales, w_cross
        )

        def onward(keeps, sends, bit):
            return add_halves(keeps, [swap(s, bit) for s in sends])

        grad_cmix, down_keep, up_keep = pin((grad_cmix, down[1], up[1]))
        down = onward([down_keep], [down[0]], 1)
        up = onward([up_keep], [up[0]], 1)
        grad_cmix, down, up = pin((grad_cmix, down, up))
        cross_grads = attn_bwd(
            cross_q, cross_pair, cross_pair, 0, 0, 6, grad_cmix, cross_probs, "crossb"
        )

        def given(rows):
            keys = dot_nt(cross_grads[1, rows], w_keyval[0][:, :width])
            return (keys + dot_nt(cross_grads[2, rows], w_keyval[0][:, width:])).astype(jnp.bfloat16)

        returned_top = lax.ppermute(
            given(slice(0, half)),
            both,
            [(i, pages + i) for i in range(pages)]
            + [(pages + (i + 1) % pages, i) for i in range(pages)],
        )
        returned_low = partner_of(given(slice(half, tokens)))
        query_back = dot_nt(cross_grads[0], w_query[0])
        far_back = lax.ppermute(query_back[:half].astype(jnp.bfloat16), both, forth)
        far_grad = lax.ppermute(cross_low[:half], both, forth)
        (cross_part,) = grad_group(
            order,
            (
                (cross_mixed,),
                (second_top, second_low),
                (partner_top, partner_low),
                (cross_low,),
                (cross_grads,),
            ),
            ((0, 3, None, 0), (1, 4, 0, 0), (2, 4, 1, 0), (2, 4, 2, 0)),
            "gcross",
        )
        down = onward([down[1]], [down[0]], 4)
        up = onward([up[1]], [up[0]], 2)
        returned_top, returned_low, far_back, far_grad, cross_part, down, up = pin(
            (returned_top, returned_low, far_back, far_grad, cross_part, down, up)
        )
        low_near, low_far, sums_two = second_back(
            query_back, far_back, returned_low, returned_top, after_self, after_gone,
            grad_cross_in, far_grad, scales,
        )
        low_near, cross_keep = pin((low_near, cross_part[1]))
        cross_part = onward([cross_keep], [cross_part[0]], 1)
        low_near, cross_part = pin((low_near, cross_part))
        self_grads = self_back(packed, low_near, low_far, w_out, self_probs)
        self_grads, up_keep = pin((self_grads, up[1]))
        up = onward([up_keep], [up[0]], 4)
        self_grads, up = pin((self_grads, up))
        parts, input_stay, input_gone, sums_one = tail_grads(
            order, self_grads, w_qkv, first, moved_mixed, moved, low_near, low_far, scales
        )
        parts = [parts[1], parts[2], parts[0], parts[3]]
        parts, cross_keep, down_keep = pin((parts, cross_part[1], down[1]))
        down = onward([down_keep], [down[0]], 8)
        cross_part = onward([cross_keep], [cross_part[0]], 2)
        sends, keeps = [p[0] for p in parts], [p[1] for p in parts]
        cross_part, keeps, down = pin((cross_part, keeps, down))
        pair_part = onward(keeps[:2], sends[:2], 1)
        rest_part = onward(keeps[2:], sends[2:], 1)
        pair_part, rest_part, input_gone, up, sums_one = pin(
            (pair_part, rest_part, input_gone, up, sums_one)
        )
        input_top = lax.ppermute(input_gone, both, back)
        sums = jnp.concatenate(
            [sums_one[:2], sums_two[:2], sums_three[:3], up_bias.reshape(4, width)]
        )
        sums = sums + swap(sums, 1)
        pair_keep, sums = pin((pair_part[1], sums))
        pair_part = onward([pair_keep], [pair_part[0]], 2)
        cross_keep, up_keep, pair_part = pin((cross_part[1], up[1], pair_part))
        (grad_up,) = last_sum(up_keep, swap(up[0], 8), [(48, 4 * width)])
        cross_part = onward([cross_keep], [cross_part[0]], 4)
        cross_part, rest_keep, grad_up = pin((cross_part, rest_part[1], grad_up))
        rest_part = onward([rest_keep], [rest_part[0]], 2)
        rest_part, pair_keep, cross_keep = pin((rest_part, pair_part[1], cross_part[1]))
        pair_part = onward([pair_keep], [pair_part[0]], 4)
        grad_cross, grad_query, grad_keyval = last_sum(
            cross_keep,
            swap(cross_part[0], 8),
            [(48, width), (48, width), (48, 2 * width)],
        )
        rest_keep, pair_part, grad_cross, grad_query, grad_keyval, sums = pin(
            (rest_part[1], pair_part, grad_cross, grad_query, grad_keyval, sums)
        )
        rest_part = onward([rest_keep], [rest_part[0]], 4)
        sums = sums + swap(sums, 2)
        rest_part, pair_keep, sums = pin((rest_part, pair_part[1], sums))
        (grad_pair,) = last_sum(pair_keep, swap(pair_part[0], 8), [(48, 2 * width)])
        sums = sums + swap(sums, 4)
        rest_keep, grad_pair, sums = pin((rest_part[1], grad_pair, sums))
        (grad_down,) = last_sum(down[1], swap(down[0], 2), [(192, width)])
        grad_first, grad_out = last_sum(
            rest_keep, swap(rest_part[0], 8), [(48, width), (48, width)]
        )
        sums = sums + swap(sums, 8)
        grad_qkv = jnp.concatenate([grad_first, grad_pair], 1)
        mine = lax.dynamic_slice_in_dim(sums[:7], device * share, share, 1)
        gains, biases = mine[0:6:2], mine[1:6:2]
        down_bias = mine[6]
        up_bias = lax.dynamic_slice_in_dim(sums[7:].reshape(-1), device * 192, 192)
        input_grad = jnp.concatenate([input_top, input_stay])
    else:
        _, unit_two, inverse_two = layer_norm(after_self, scales[1], shifts[1])
        after_cross = after_self + matmul(cross_mixed, w_cross[0])
        third, unit_three, inverse_three = layer_norm(after_cross, scales[2], shifts[2])
        value, slope = gelu_pair(matmul(third, w_up[0]) + b_up[0])
        hidden = value.astype(jnp.bfloat16)
        output = (after_cross + matmul(hidden, w_down[0]) + b_down[0]).astype(jnp.bfloat16)
        upstream = dy.astype(jnp.float32)
        pre_low = (dot_nt(dy, w_down[0]) * slope).astype(jnp.bfloat16)
        back_three, gain_three, shift_three = norm_back(
            dot_nt(pre_low, w_up[0]), unit_three, inverse_three, scales[2]
        )
        grad_cross_in = upstream + back_three
        cross_low = grad_cross_in.astype(jnp.bfloat16)
        grad_cmix = dot_nt(cross_low, w_cross[0]).astype(jnp.bfloat16)
        cross_grads = attn_bwd(
            cross_q, cross_pair, cross_pair, 0, 0, 6, grad_cmix, cross_probs, "crossb"
        )
        pair = jnp.concatenate([cross_grads[1], cross_grads[2]], 1)
        returned = partner_of(dot_nt(pair, w_keyval[0]).astype(jnp.bfloat16))
        back_two, gain_two, shift_two = norm_back(
            dot_nt(cross_grads[0], w_query[0]) + returned.astype(jnp.float32),
            unit_two,
            inverse_two,
            scales[1],
        )
        self_low = (grad_cross_in + back_two).astype(jnp.bfloat16)
        moved_low = jnp.concatenate([self_low[half:], lax.ppermute(self_low[:half], both, forth)])
        grad_smix = dot_nt(moved_low, w_out[0]).astype(jnp.bfloat16)
        self_grads = attn_bwd(packed, packed, packed, 0, 6, 12, grad_smix, self_probs, "selfb")
        packed_grad = jnp.concatenate([self_grads[0], self_grads[1], self_grads[2]], 1)
        back_one, gain_one, shift_one = norm_back(
            dot_nt(packed_grad, w_qkv[0]), unit_one, inverse_one, scales[0]
        )
        moved_grad = (moved_low.astype(jnp.float32) + back_one).astype(jnp.bfloat16)
        input_grad = jnp.concatenate([lax.ppermute(moved_grad[half:], both, back), moved_grad[:half]])

        def summed(grad):
            return lax.psum_scatter(grad, "page", scatter_dimension=0, tiled=True)

        def scattered(left, right):
            return summed(
                lax.dot_general(
                    left, right, (((0,), (0,)), ((), ())), preferred_element_type=jnp.float32
                )
            )

        grad_down = scattered(hidden, dy)
        grad_up = scattered(third, pre_low)
        grad_cross = scattered(cross_mixed, cross_low)
        grad_query = scattered(second, cross_grads[0])
        grad_keyval = scattered(partner, pair)
        grad_out = scattered(jnp.concatenate([back_mixed, near]), self_low)
        grad_qkv = scattered(first, packed_grad)
        gains = summed(jnp.stack([gain_one, gain_two, gain_three], 1)).T
        biases = summed(jnp.stack([shift_one, shift_two, shift_three], 1)).T
        down_bias = summed(jnp.sum(upstream, axis=0))
        up_bias = summed(jnp.sum(pre_low.astype(jnp.float32), axis=0))
    return (
        output[None],
        input_grad[None],
        gains.T[None],
        biases.T[None],
        grad_qkv[None],
        grad_out[None],
        grad_query[None],
        grad_keyval[None],
        grad_cross[None],
        grad_up[None],
        up_bias[None],
        grad_down[None],
        down_bias[None],
    )


def solution(mesh):
    tokens = P("stream", "page", None)
    whole = P("stream", None, None)
    placed = (tokens, tokens) + (whole,) * 8 + (P("stream", None), whole, P("stream", None))
    return jax.shard_map(
        on_device,
        mesh=mesh,
        in_specs=placed + (P(), P("page")),
        out_specs=(tokens,) * 10 + (P("stream", "page"), tokens, P("stream", "page")),
        check_vma=False,
    )
```

```python
import functools

import jax
import jax.numpy as jnp
from jax import lax
from jax.experimental import pallas as pl
from jax.experimental.pallas import tpu as pltpu
from jax.sharding import PartitionSpec as P

HEADS = 12
HEAD = 64
WIN = 12
SHIFT = 6
NORM_EPS = 1e-05
MASKED = -1e30


def dot_nt(a,b):
    return lax.dot_general(a,b,(((1,),(1,)),((),())),preferred_element_type=jnp.float32)
def dot_nn(a,b):
    return lax.dot_general(a,b,(((1,),(0,)),((),())),preferred_element_type=jnp.float32)

def fill_self_bias(info, bias, first=0):
    tokens, count = bias.shape
    half=tokens//2
    cols=tokens//12
    def codes(shape,dim,start):
        t=lax.broadcasted_iota(jnp.int32,shape,dim)+start
        row=jnp.zeros(shape,jnp.int32)
        page=jnp.full(shape,info[2],jnp.int32)
        for r in range(1,12):
            inside=t>=r*cols
            row=jnp.where(inside,r,row)
            page=jnp.where(inside,info[2+r],page)
        c=t-row*cols
        win=jnp.zeros(shape,jnp.int32)
        for w in range(1,cols//12):
            win=jnp.where((c>=6+12*(w-1))&(c<6+12*w),w,win)
        win=jnp.where(c>=cols-6,cols//12+1,win)
        slot=jnp.where(t<half,t+half,t-half)
        return page*16+win,slot
    ck,sk=codes((tokens,1),0,0)
    cq,sq=codes((1,count),1,first)
    length=info[1]
    @pl.when(info[0]==1)
    def _():
        ok=(sk<=sq)&(sk<length)
        bias[...]=jnp.where(ok,0.0,MASKED)
    @pl.when(info[0]==0)
    def _():
        bias[...]=jnp.where(ck==cq,0.0,MASKED)

def fill_cross_bias(info,bias,first=0):
    tokens=bias.shape[0]
    t=lax.broadcasted_iota(jnp.int32,bias.shape,0)
    bias[...]=jnp.where((t<info[1])|(info[0]==1),0.0,MASKED)

def lane_pick(e,scale):
    lane=lax.broadcasted_iota(jnp.int32,(1,2*HEAD),1)
    return jnp.where((lane>=HEAD)==bool(e),scale,0.0).astype(jnp.bfloat16)

def fwd_kernel(fill, info, q_ref, k_ref, v_ref, o_ref, p_ref, bias):
    @pl.when(pl.program_id(0) == 0)
    def _():
        fill(info, bias)

    q, k = q_ref[...], k_ref[...]
    vt = v_ref[...].T
    scores = [dot_nt(k, q * lane_pick(e, HEAD**-0.5)) + bias[...] for e in range(2)]
    outs = []
    for e in range(2):
        weights = jnp.exp(scores[e] - jnp.max(scores[e], axis=0, keepdims=True))
        inverse = 1.0 / jnp.sum(weights, axis=0, keepdims=True)
        probs = (weights * inverse).astype(jnp.bfloat16)
        p_ref[e] = probs
        outs.append(dot_nn(vt[e * HEAD : (e + 1) * HEAD], probs))
    o_ref[...] = jnp.concatenate(outs, 0).T.astype(jnp.bfloat16)


NOTHING = pl.CostEstimate(flops=1000, bytes_accessed=1000, transcendentals=0)


def attn_fwd(info, q, k, v, qo, ko, vo, fill, name):
    tokens = q.shape[0]
    spec = lambda off: pl.BlockSpec((tokens, 128), lambda j, info: (0, off + j))
    return pl.pallas_call(
        functools.partial(fwd_kernel, fill),
        grid_spec=pltpu.PrefetchScalarGridSpec(
            num_scalar_prefetch=1,
            grid=(HEADS // 2,),
            in_specs=[spec(qo), spec(ko), spec(vo)],
            out_specs=[spec(0), pl.BlockSpec((2, tokens, tokens), lambda j, info: (j, 0, 0))],
            scratch_shapes=[pltpu.VMEM((tokens, tokens), jnp.float32)],
        ),
        out_shape=[
            jax.ShapeDtypeStruct((tokens, HEADS * HEAD), jnp.bfloat16),
            pltpu.HBM((HEADS, tokens, tokens), jnp.bfloat16),
        ],
        compiler_params=pltpu.CompilerParams(vmem_limit_bytes=24 * 2**20),
        cost_estimate=NOTHING,
        name=name,
    )(info, q, k, v)


def bwd_kernel(q_ref, k_ref, v_ref, do_ref, p_ref, d_ref):
    grads = backward_heads(q_ref[...], k_ref[...], v_ref[...], do_ref[...], p_ref)
    for i in range(3):
        d_ref[i] = grads[i]


def attn_bwd(q, k, v, qo, ko, vo, do, probs, name):
    tokens = q.shape[0]
    spec = lambda off: pl.BlockSpec((tokens, 128), lambda j: (0, off + j))
    return pl.pallas_call(
        bwd_kernel,
        grid=(HEADS // 2,),
        in_specs=[spec(qo), spec(ko), spec(vo), spec(0)]
        + [pl.BlockSpec((2, tokens, tokens), lambda j: (j, 0, 0))],
        out_specs=pl.BlockSpec((3, tokens, 128), lambda j: (0, 0, j)),
        out_shape=jax.ShapeDtypeStruct((3, tokens, HEADS * HEAD), jnp.bfloat16),
        compiler_params=pltpu.CompilerParams(vmem_limit_bytes=24 * 2**20),
        cost_estimate=NOTHING,
        name=name,
    )(q, k, v, do, pltpu.with_memory_space_constraint(probs, pltpu.HBM))


def layer_norm(inputs, scales, shifts):
    average = jnp.mean(inputs, axis=1, keepdims=True)
    centred = inputs - average
    spread = jnp.mean(centred * centred, axis=1, keepdims=True)
    inverse = lax.rsqrt(spread + NORM_EPS)
    unit = centred * inverse
    return (unit * scales + shifts).astype(jnp.bfloat16), unit, inverse


def norm_back(upstream, unit, inverse, scales):
    scaled = upstream * scales
    inner = (
        scaled
        - jnp.mean(scaled, axis=1, keepdims=True)
        - unit * jnp.mean(scaled * unit, axis=1, keepdims=True)
    )
    return (inverse * inner, jnp.sum(upstream * unit, axis=0), jnp.sum(upstream, axis=0))


def matmul(left, right):
    return jnp.dot(left, right, preferred_element_type=jnp.float32)


def gelu_pair(pre):
    root = 0.7978845608028654
    square = pre * pre
    gate = 0.5 + 0.5 * jnp.tanh(pre * (root + root * 0.044715 * square))
    value = pre * gate
    return value, gate + value * (1.0 - gate) * (2 * root + 6 * root * 0.044715 * square)


def layer_parts(v):
    average = jnp.mean(v, axis=1, keepdims=True)
    centred = v - average
    inverse = lax.rsqrt(jnp.mean(centred * centred, axis=1, keepdims=True) + NORM_EPS)
    return centred * inverse, inverse


def layer_back(grad, unit, inverse, scale):
    scaled = grad * scale
    return inverse * (
        scaled
        - jnp.mean(scaled, axis=1, keepdims=True)
        - unit * jnp.mean(scaled * unit, axis=1, keepdims=True)
    )


def column_sums(*values):
    rows = [jnp.sum(v, axis=0, keepdims=True) for v in values]
    rows.append(jnp.zeros((8 - len(rows), rows[0].shape[1]), jnp.float32))
    return jnp.concatenate(rows)


def sort_rows(order, x, across, sorted_rows):
    rows = sorted_rows.shape[0] // 16
    across[...] = x.T
    for n in range(16):
        start = pl.multiple_of(order[n] * rows, 16)
        sorted_rows[n * rows : (n + 1) * rows, :] = across[pl.ds(start, rows), :]


def feed_kernel(
    order, after_ref, mixed_ref, dy_ref, scales_ref, shifts_ref, cross_ref, down_bias_ref,
    up_ref, up_bias_ref, down_ref,
    out_ref, grad_ref, kept_ref, bias_ref,
    down_send, down_keep, up_send, up_keep,
    third_rows, across, sorted_rows, after, total, grad_total,
):
    step = pl.program_id(0)
    rows = dy_ref.shape[1] // 16
    half = 8 * rows

    @pl.when(step == 0)
    def _():
        after[...] = after_ref[...] + dot_nn(mixed_ref[...], cross_ref[0])
        unit = layer_parts(after[...])[0]
        third_rows[...] = (unit * scales_ref[2:3, :] + shifts_ref[2:3, :]).astype(jnp.bfloat16)
        sort_rows(order, third_rows[...], across, sorted_rows)
        total[...] = after[...] + down_bias_ref[...]
        grad_total[...] = jnp.zeros_like(grad_total)

    dy, third = dy_ref[...], third_rows[...]
    tile = up_ref.shape[2] // 2
    deep = tile // 2
    parts = [slice(0, tile), slice(tile, 2 * tile)]
    pre = [dot_nn(third, up_ref[0, :, p]) + up_bias_ref[:, p] for p in parts]
    grad_hidden = [dot_nt(dy, down_ref[0, p, :]) for p in parts]
    out = grad_third = 0.0
    grads = []
    for i, p in enumerate(parts):
        value, slope = gelu_pair(pre[i])
        hidden = value.astype(jnp.bfloat16)
        low = (grad_hidden[i] * slope).astype(jnp.bfloat16)
        bias_ref[0, :, p] = jnp.sum(low.astype(jnp.float32), axis=0, keepdims=True)
        grad = dot_nn(sorted_rows[...], low).astype(jnp.bfloat16)
        up_send[:, :, p] = grad[:half].reshape(8, rows, tile)
        up_keep[:, :, p] = grad[half:].reshape(8, rows, tile)
        grads.append(dot_nn(hidden.T, dy).astype(jnp.bfloat16))
        out += dot_nn(hidden, down_ref[0, p, :])
        grad_third += dot_nt(low, up_ref[0, :, p])
    total[...] += out
    grad_total[...] += grad_third
    for odd in range(2):
        for far in range(2):

            @pl.when((order[15] % 2 == odd) & (order[15] // 2 % 2 == far))
            def _():
                for n in range(2):
                    both = grads[n ^ far ^ 1]
                    down_send[n] = both[deep * (1 - odd) : deep * (2 - odd)]
                    down_keep[n] = both[deep * odd : deep * (odd + 1)]

    @pl.when(step == pl.num_programs(0) - 1)
    def _():
        out_ref[...] = total[...].astype(jnp.bfloat16)
        grad_ref[...] = grad_total[...]
        kept_ref[...] = after[...]


def third_kernel(third_ref, after_ref, dy_ref, scales_ref, cross_ref, grad_ref, low_ref, mix_ref, sums_ref):
    upstream = dy_ref[...].astype(jnp.float32)
    unit, inverse = layer_parts(after_ref[...])
    grad = third_ref[...]
    sums_ref[...] = column_sums(grad * unit, grad, upstream)
    grad_ref[...] = upstream + layer_back(grad, unit, inverse, scales_ref[2:3, :])
    low_ref[...] = grad_ref[...].astype(jnp.bfloat16)
    mix_ref[...] = dot_nt(low_ref[...], cross_ref[0]).astype(jnp.bfloat16)


def third_back(grad, after, dy, scales, w_cross):
    full = jax.ShapeDtypeStruct(after.shape, jnp.float32)
    low = jax.ShapeDtypeStruct(after.shape, jnp.bfloat16)
    return pl.pallas_call(
        third_kernel,
        out_shape=[full, low, low, jax.ShapeDtypeStruct((8, after.shape[1]), jnp.float32)],
        compiler_params=pltpu.CompilerParams(vmem_limit_bytes=32 * 2**20),
        cost_estimate=NOTHING,
        name="third",
    )(grad, after, dy, scales, w_cross)


def feed_forward(order, after, mixed, dy, scales, shifts, w_cross, w_up, b_up, w_down, b_down):
    tokens, width = dy.shape
    deep = w_up.shape[2]
    tile = deep // 4
    rows = width // 16
    whole = lambda *shape: pl.BlockSpec(shape, lambda j, order: (0,) * len(shape))
    where = lambda j, order: order[8 + j] // 4
    once = lambda *shape: pl.BlockSpec(
        shape, lambda j, order: (0,) * len(shape), pipeline_mode=pl.Buffered(1)
    )
    token = once(tokens, width)
    down_half = jax.ShapeDtypeStruct((8, deep // 16, width), jnp.bfloat16)
    up_half = jax.ShapeDtypeStruct((8, 4 * rows, tile), jnp.bfloat16)
    down_piece = pl.BlockSpec((2, deep // 16, width), lambda j, order: (j, 0, 0))
    up_piece = pl.BlockSpec((8, rows, tile), lambda j, order: (0, where(j, order), 0))
    low = jax.ShapeDtypeStruct((tokens, width), jnp.bfloat16)
    full = jax.ShapeDtypeStruct((tokens, width), jnp.float32)
    out = pl.pallas_call(
        feed_kernel,
        grid_spec=pltpu.PrefetchScalarGridSpec(
            num_scalar_prefetch=1,
            grid=(4,),
            in_specs=[
                token,
                token,
                token,
                whole(3, width),
                whole(3, width),
                once(1, width, width),
                whole(1, width),
                pl.BlockSpec((1, width, tile), lambda j, order: (0, 0, where(j, order))),
                pl.BlockSpec((1, tile), lambda j, order: (0, where(j, order))),
                pl.BlockSpec((1, tile, width), lambda j, order: (0, where(j, order), 0)),
            ],
            out_specs=[
                token,
                token,
                token,
                pl.BlockSpec((1, 1, tile), lambda j, order: (where(j, order), 0, 0)),
                down_piece,
                down_piece,
                up_piece,
                up_piece,
            ],
            scratch_shapes=[pltpu.VMEM((tokens, width), jnp.bfloat16)]
            + [pltpu.VMEM((width, tokens), jnp.bfloat16)] * 2
            + [pltpu.VMEM((tokens, width), jnp.float32)] * 3,
        ),
        out_shape=[
            low,
            full,
            full,
            jax.ShapeDtypeStruct((4, 1, tile), jnp.float32),
            down_half,
            down_half,
            up_half,
            up_half,
        ],
        compiler_params=pltpu.CompilerParams(vmem_limit_bytes=36 * 2**20),
        cost_estimate=NOTHING,
        name="feed",
    )(order, after, mixed, dy, scales, shifts, w_cross, b_down, w_up, b_up, w_down)
    return (*out[:4], (out[4], out[5]), (out[6], out[7]))


def backward_heads(q, k, v, do, p_ref):
    kt = k.T
    queries = []
    keys = values = 0.0
    picked = [do * lane_pick(e, 1.0) for e in range(2)]
    grads = [dot_nt(v, picked[e]) for e in range(2)]
    for e in range(2):
        probs = p_ref[e]
        wide = probs.astype(jnp.float32)
        part = wide * grads[e]
        total = jnp.sum(part, axis=0, keepdims=True)
        ds = (part - wide * total).astype(jnp.bfloat16)
        values += dot_nn(probs, picked[e])
        keys += dot_nn(ds, q * lane_pick(e, HEAD**-0.5))
        queries.append(dot_nn(kt[e * HEAD : (e + 1) * HEAD], ds) * HEAD**-0.5)
    queries = jnp.concatenate(queries, 0).T
    return [g.astype(jnp.bfloat16) for g in (queries, keys, values)]


def self_back_kernel(q_ref, k_ref, v_ref, near_ref, far_ref, out_ref, p_ref, d_ref):
    low = jnp.concatenate([near_ref[...], far_ref[...]])
    do = dot_nt(low, out_ref[0]).astype(jnp.bfloat16)
    grads = backward_heads(q_ref[...], k_ref[...], v_ref[...], do, p_ref)
    for i in range(3):
        d_ref[i] = grads[i]


def self_back(packed, near, far, w_out, probs):
    tokens, width = packed.shape[0], near.shape[1]
    spec = lambda off: pl.BlockSpec((tokens, 128), lambda j: (0, off + j))
    rows = pl.BlockSpec(near.shape, lambda j: (0, 0))
    return pl.pallas_call(
        self_back_kernel,
        grid=(HEADS // 2,),
        in_specs=[spec(0), spec(6), spec(12), rows, rows]
        + [pl.BlockSpec((1, 128, width), lambda j: (0, j, 0))]
        + [pl.BlockSpec((2, tokens, tokens), lambda j: (j, 0, 0))],
        out_specs=pl.BlockSpec((3, tokens, 128), lambda j: (0, 0, j)),
        out_shape=jax.ShapeDtypeStruct((3, tokens, width), jnp.bfloat16),
        compiler_params=pltpu.CompilerParams(vmem_limit_bytes=24 * 2**20),
        cost_estimate=NOTHING,
        name="selfb",
    )(packed, packed, packed, near, far, w_out, pltpu.with_memory_space_constraint(probs, pltpu.HBM))


def second_kernel(
    near_back_ref, far_back_ref, near_given_ref, far_given_ref, near_after_ref, far_after_ref,
    near_grad_ref, far_grad_ref, scales_ref, near_ref, far_ref, sums_ref,
):
    sums = 0.0
    for back, given, after, grad, out in (
        (near_back_ref, near_given_ref, near_after_ref, near_grad_ref, near_ref),
        (far_back_ref, far_given_ref, far_after_ref, far_grad_ref, far_ref),
    ):
        unit, inverse = layer_parts(after[...])
        upstream = back[...].astype(jnp.float32) + given[...].astype(jnp.float32)
        sums += column_sums(upstream * unit, upstream)
        below = layer_back(upstream, unit, inverse, scales_ref[1:2, :])
        out[...] = (grad[...].astype(jnp.float32) + below).astype(jnp.bfloat16)
    sums_ref[...] = sums


def second_back(back, far_back, near_given, far_given, after, far_after, grad, far_grad, scales):
    half, width = near_given.shape
    low = pl.BlockSpec((half, width), lambda j: (1, 0))
    rows = pl.BlockSpec((half, width), lambda j: (0, 0))
    out = jax.ShapeDtypeStruct((half, width), jnp.bfloat16)
    return pl.pallas_call(
        second_kernel,
        grid=(1,),
        in_specs=[low, rows, rows, rows, low, rows, low, rows]
        + [pl.BlockSpec((3, width), lambda j: (0, 0))],
        out_specs=[rows, rows, pl.BlockSpec((8, width), lambda j: (0, 0))],
        out_shape=[out, out, jax.ShapeDtypeStruct((8, width), jnp.float32)],
        compiler_params=pltpu.CompilerParams(vmem_limit_bytes=24 * 2**20),
        cost_estimate=NOTHING,
        name="second",
    )(back, far_back, near_given, far_given, after, far_after, grad, far_grad, scales)


def tail_kernel(
    order, d_ref, w_ref, first_ref, mixed_ref, moved_ref, near_ref, far_ref, scales_ref, *refs,
):
    step = pl.program_id(0)
    stay_ref, gone_ref, sums_ref = refs[8:11]
    across, sorted_rows, total = refs[11:]
    half = sorted_rows.shape[0] // 2

    @pl.when(step == 0)
    def _():
        sort_rows(order, first_ref[...], across, sorted_rows)

    for i in range(3):

        @pl.when(step == i)
        def _():
            part = dot_nt(d_ref[0], w_ref[0])
            grad = dot_nn(sorted_rows[...], d_ref[0]).astype(jnp.bfloat16)
            refs[2 * i][...] = grad[:half].reshape(refs[0].shape)
            refs[2 * i + 1][...] = grad[half:].reshape(refs[0].shape)
            if i == 0:
                total[...] = part
            else:
                total[...] += part

    @pl.when(step == 3)
    def _():
        sort_rows(order, mixed_ref[...], across, sorted_rows)
        low = jnp.concatenate([near_ref[...], far_ref[...]])
        grad = dot_nn(sorted_rows[...], low).astype(jnp.bfloat16)
        refs[6][...] = grad[:half].reshape(refs[0].shape)
        refs[7][...] = grad[half:].reshape(refs[0].shape)
        rows = stay_ref.shape[0]
        unit, inverse = layer_parts(moved_ref[...].astype(jnp.float32))
        grad = total[...]
        sums_ref[...] = column_sums(grad * unit, grad)
        back = layer_back(grad, unit, inverse, scales_ref[0:1, :])
        stay_ref[...] = (near_ref[...].astype(jnp.float32) + back[:rows]).astype(jnp.bfloat16)
        gone_ref[...] = (far_ref[...].astype(jnp.float32) + back[rows:]).astype(jnp.bfloat16)


def tail_grads(order, grads, w_qkv, first, mixed, moved, near, far, scales):
    tokens, width = moved.shape
    half = tokens // 2
    whole = lambda *shape: pl.BlockSpec(shape, lambda j, order: (0,) * len(shape))
    rows = jax.ShapeDtypeStruct((half, width), jnp.bfloat16)
    piece = (8, width // 16, width)
    last = lambda j: jnp.minimum(j, 2)
    outs = pl.pallas_call(
        tail_kernel,
        grid_spec=pltpu.PrefetchScalarGridSpec(
            num_scalar_prefetch=1,
            grid=(4,),
            in_specs=[
                pl.BlockSpec((1, tokens, width), lambda j, order: (last(j), 0, 0)),
                pl.BlockSpec((1, width, width), lambda j, order: (0, 0, last(j))),
                whole(tokens, width),
                whole(tokens, width),
                whole(tokens, width),
                whole(half, width),
                whole(half, width),
                whole(3, width),
            ],
            out_specs=[whole(*piece)] * 8 + [whole(half, width)] * 2 + [whole(8, width)],
            scratch_shapes=[pltpu.VMEM((width, tokens), jnp.bfloat16)] * 2
            + [pltpu.VMEM((tokens, width), jnp.float32)],
        ),
        out_shape=[jax.ShapeDtypeStruct(piece, jnp.bfloat16)] * 8
        + [rows, rows, jax.ShapeDtypeStruct((8, width), jnp.float32)],
        compiler_params=pltpu.CompilerParams(vmem_limit_bytes=40 * 2**20),
        cost_estimate=NOTHING,
        name="tail",
    )(order, grads, w_qkv, first, mixed, moved, near, far, scales)
    return [(outs[i], outs[i + 1]) for i in range(0, 8, 2)], *outs[8:]


def group_kernel(plan, halves, pieces, order, *refs):
    refs = list(refs)
    groups = [[refs.pop(0) for _ in range(n)] for n in halves]
    joined = lambda group: jnp.concatenate([r[...] for r in group]) if len(group) > 1 else group[0][...]
    outs, (across, sorted_rows) = refs[:-2], refs[-2:]
    half = sorted_rows.shape[0] // 2
    before = None
    for i, (x, dy, lead, target) in enumerate(plan):
        turn = x != before
        before = x

        @pl.when(pl.program_id(0) == i)
        def _():
            if turn:
                sort_rows(order, joined(groups[x]), across, sorted_rows)
            right = joined(groups[dy]) if lead is None else groups[dy][0][0]
            grad = dot_nn(sorted_rows[...], right).astype(jnp.bfloat16)
            send_ref, keep_ref = outs[2 * target], outs[2 * target + 1]
            send_ref[...] = grad[:half].reshape(send_ref.shape)
            keep_ref[...] = grad[half:].reshape(keep_ref.shape)


def grad_group(order, operands, plan, name):
    width = operands[0][0].shape[-1]
    rows = width // 16
    tokens = sum(a.shape[-2] for a in operands[0])
    in_specs = []
    for n, group in enumerate(operands):
        for a in group:
            if a.ndim == 2:
                in_specs.append(pl.BlockSpec(a.shape, lambda j, order: (0, 0)))
            else:
                first = min(i for i, p in enumerate(plan) if p[1] == n)
                in_specs.append(
                    pl.BlockSpec(
                        (1, *a.shape[1:]),
                        lambda j, order, first=first, last=a.shape[0] - 1: (
                            jnp.clip(j - first, 0, last),
                            0,
                            0,
                        ),
                    )
                )
    out_specs, out_shape = [], []
    for target in range(1 + max(p[3] for p in plan)):
        steps = [i for i, p in enumerate(plan) if p[3] == target]
        spec = pl.BlockSpec(
            (8, rows, width),
            lambda j, order, first=steps[0], last=len(steps) - 1: (
                0,
                jnp.clip(j - first, 0, last),
                0,
            ),
        )
        out_specs += [spec, spec]
        out_shape += [jax.ShapeDtypeStruct((8, rows * len(steps), width), jnp.bfloat16)] * 2
    outs = pl.pallas_call(
        functools.partial(group_kernel, plan, [len(g) for g in operands], len(out_specs)),
        grid_spec=pltpu.PrefetchScalarGridSpec(
            num_scalar_prefetch=1,
            grid=(len(plan),),
            in_specs=in_specs,
            out_specs=out_specs,
            scratch_shapes=[pltpu.VMEM((width, tokens), jnp.bfloat16)] * 2,
        ),
        out_shape=out_shape,
        compiler_params=pltpu.CompilerParams(vmem_limit_bytes=32 * 2**20),
        cost_estimate=NOTHING,
        name=name,
    )(order, *[a for group in operands for a in group])
    return [(outs[i], outs[i + 1]) for i in range(0, len(outs), 2)]


def add_kernel(count, *refs):
    at = 0
    for n in range(count):
        keep, arrived = refs[2 * n], refs[2 * n + 1]
        rows = keep.shape[-2]
        for i, out in enumerate(refs[2 * count :]):
            out[0, at : at + rows, :] = keep[i, 0] + arrived[i, 0]
        at += rows


def add_halves(keeps, arrivals, name="add"):
    pairs = keeps[0].shape[0] // 2
    width = keeps[0].shape[2]
    rows = sum(k.shape[1] for k in keeps)
    operands = []
    for keep, arrived in zip(keeps, arrivals):
        operands += [a.reshape(2, pairs, *a.shape[1:]) for a in (keep, arrived)]
    out = pl.BlockSpec((1, rows, width), lambda j: (j, 0, 0))
    return pl.pallas_call(
        functools.partial(add_kernel, len(keeps)),
        grid=(pairs,),
        in_specs=[
            pl.BlockSpec((2, 1, *a.shape[2:]), lambda j: (0, j, 0, 0)) for a in operands
        ],
        out_specs=[out, out],
        out_shape=[jax.ShapeDtypeStruct((pairs, rows, width), jnp.bfloat16)] * 2,
        compiler_params=pltpu.CompilerParams(vmem_limit_bytes=16 * 2**20),
        cost_estimate=NOTHING,
        name=name,
    )(*operands)


def last_kernel(keep_ref, arrived_ref, *outs):
    total = keep_ref[0].astype(jnp.float32) + arrived_ref[0].astype(jnp.float32)
    width = total.shape[1]
    at = 0
    for out in outs:
        rows, columns = out.shape
        for n in range(columns // width):
            out[:, n * width : (n + 1) * width] = total[at : at + rows]
            at += rows


def last_sum(keep, arrived, shapes):
    return pl.pallas_call(
        last_kernel,
        out_shape=[jax.ShapeDtypeStruct(s, jnp.float32) for s in shapes],
        compiler_params=pltpu.CompilerParams(vmem_limit_bytes=16 * 2**20),
        cost_estimate=NOTHING,
        name="last",
    )(keep, arrived)


def swap(x, bit):
    return lax.ppermute(x, "page", [(i, i ^ bit) for i in range(16)])


pin = lax.optimization_barrier


def on_device(
    block_input,
    cotangent,
    norm_gain,
    norm_bias,
    w_qkv,
    w_out,
    w_query,
    w_keyval,
    w_cross,
    w_up,
    b_up,
    w_down,
    b_down,
    row_page,
    lengths,
):
    x = block_input[0]
    dy = cotangent[0]
    tokens, width = x.shape
    half = tokens // 2
    pages = lax.axis_size("page")
    device = lax.axis_index("page")
    stream = lax.axis_index("stream")
    scales = norm_gain[0].T
    shifts = norm_bias[0].T
    share = width // pages
    padded = jnp.concatenate([row_page, row_page[:SHIFT]])
    info = jnp.concatenate(
        [
            stream.astype(jnp.int32)[None],
            lengths,
            lax.dynamic_slice_in_dim(padded, device * WIN + SHIFT, WIN),
        ]
    )
    stay = [(pages + i, pages + i) for i in range(pages)]
    both = ("stream", "page")
    forth = [((i + 1) % pages, i) for i in range(pages)] + stay
    back = [(i, (i + 1) % pages) for i in range(pages)] + stay

    def partner_of(rows):
        return lax.ppermute(rows, "stream", [(0, 1), (1, 0)])

    moved = jnp.concatenate([x[half:], lax.ppermute(x[:half], both, forth)])
    first, unit_one, inverse_one = layer_norm(moved.astype(jnp.float32), scales[0], shifts[0])
    packed = matmul(first, w_qkv[0]).astype(jnp.bfloat16)
    moved_mixed, self_probs = attn_fwd(
        info, packed, packed, packed, 0, 6, 12, fill_self_bias, "selff"
    )
    gone, near = moved_mixed[half:], moved_mixed[:half]
    after_gone = moved[half:].astype(jnp.float32) + matmul(gone, w_out[0])
    second_gone = layer_norm(after_gone, scales[1], shifts[1])[0]
    partner_top = lax.ppermute(
        second_gone,
        both,
        [(i, pages + (i + 1) % pages) for i in range(pages)]
        + [(pages + i, i) for i in range(pages)],
    )
    back_mixed = lax.ppermute(gone, both, back)
    after_low = moved[:half].astype(jnp.float32) + matmul(near, w_out[0])
    second_low = layer_norm(after_low, scales[1], shifts[1])[0]
    partner_low = partner_of(second_low)
    back_mixed, second_low, partner_top = pin((back_mixed, second_low, partner_top))
    after_top = x[:half].astype(jnp.float32) + matmul(back_mixed, w_out[0])
    second_top = layer_norm(after_top, scales[1], shifts[1])[0]
    after_self = jnp.concatenate([after_top, after_low])
    second = jnp.concatenate([second_top, second_low])
    cross_q = matmul(second, w_query[0]).astype(jnp.bfloat16)
    cross_q, after_self, partner_top, partner_low = pin(
        (cross_q, after_self, partner_top, partner_low)
    )
    partner = jnp.concatenate([partner_top, partner_low])
    cross_pair = matmul(partner, w_keyval[0]).astype(jnp.bfloat16)
    cross_mixed, cross_probs = attn_fwd(
        info, cross_q, cross_pair, cross_pair, 0, 0, 6, fill_cross_bias, "crossf"
    )
    if pages == 16:
        ordinal = jnp.arange(16, dtype=jnp.int32)
        turned = 15 - ordinal
        turned = (turned & 1) << 3 | (turned & 2) << 1 | (turned & 4) >> 1 | (turned & 8) >> 3
        order = device.astype(jnp.int32) ^ turned
        output, grad_third, after_cross, up_bias, down, up = feed_forward(
            order, after_self, cross_mixed, dy, scales, shifts, w_cross, w_up, b_up, w_down, b_down
        )
        grad_cross_in, cross_low, grad_cmix, sums_three = third_back(
            grad_third, after_cross, dy, scales, w_cross
        )

        def onward(keeps, sends, bit):
            return add_halves(keeps, [swap(s, bit) for s in sends])

        grad_cmix, down_keep, up_keep = pin((grad_cmix, down[1], up[1]))
        down = onward([down_keep], [down[0]], 1)
        up = onward([up_keep], [up[0]], 1)
        grad_cmix, down, up = pin((grad_cmix, down, up))
        cross_grads = attn_bwd(
            cross_q, cross_pair, cross_pair, 0, 0, 6, grad_cmix, cross_probs, "crossb"
        )

        def given(rows):
            keys = dot_nt(cross_grads[1, rows], w_keyval[0][:, :width])
            return (keys + dot_nt(cross_grads[2, rows], w_keyval[0][:, width:])).astype(jnp.bfloat16)

        returned_top = lax.ppermute(
            given(slice(0, half)),
            both,
            [(i, pages + i) for i in range(pages)]
            + [(pages + (i + 1) % pages, i) for i in range(pages)],
        )
        returned_low = partner_of(given(slice(half, tokens)))
        query_back = dot_nt(cross_grads[0], w_query[0])
        far_back = lax.ppermute(query_back[:half].astype(jnp.bfloat16), both, forth)
        far_grad = lax.ppermute(cross_low[:half], both, forth)
        (cross_part,) = grad_group(
            order,
            (
                (cross_mixed,),
                (second_top, second_low),
                (partner_top, partner_low),
                (cross_low,),
                (cross_grads,),
            ),
            ((0, 3, None, 0), (1, 4, 0, 0), (2, 4, 1, 0), (2, 4, 2, 0)),
            "gcross",
        )
        down = onward([down[1]], [down[0]], 4)
        up = onward([up[1]], [up[0]], 2)
        returned_top, returned_low, far_back, far_grad, cross_part, down, up = pin(
            (returned_top, returned_low, far_back, far_grad, cross_part, down, up)
        )
        low_near, low_far, sums_two = second_back(
            query_back, far_back, returned_low, returned_top, after_self, after_gone,
            grad_cross_in, far_grad, scales,
        )
        low_near, cross_keep = pin((low_near, cross_part[1]))
        cross_part = onward([cross_keep], [cross_part[0]], 1)
        low_near, cross_part = pin((low_near, cross_part))
        self_grads = self_back(packed, low_near, low_far, w_out, self_probs)
        self_grads, up_keep = pin((self_grads, up[1]))
        up = onward([up_keep], [up[0]], 4)
        self_grads, up = pin((self_grads, up))
        parts, input_stay, input_gone, sums_one = tail_grads(
            order, self_grads, w_qkv, first, moved_mixed, moved, low_near, low_far, scales
        )
        parts = [parts[1], parts[2], parts[0], parts[3]]
        parts, cross_keep, down_keep = pin((parts, cross_part[1], down[1]))
        down = onward([down_keep], [down[0]], 8)
        cross_part = onward([cross_keep], [cross_part[0]], 2)
        sends, keeps = [p[0] for p in parts], [p[1] for p in parts]
        cross_part, keeps, down = pin((cross_part, keeps, down))
        pair_part = onward(keeps[:2], sends[:2], 1)
        rest_part = onward(keeps[2:], sends[2:], 1)
        pair_part, rest_part, input_gone, up, sums_one = pin(
            (pair_part, rest_part, input_gone, up, sums_one)
        )
        input_top = lax.ppermute(input_gone, both, back)
        sums = jnp.concatenate(
            [sums_one[:2], sums_two[:2], sums_three[:3], up_bias.reshape(4, width)]
        )
        sums = sums + swap(sums, 1)
        pair_keep, sums = pin((pair_part[1], sums))
        pair_part = onward([pair_keep], [pair_part[0]], 2)
        cross_keep, up_keep, pair_part = pin((cross_part[1], up[1], pair_part))
        (grad_up,) = last_sum(up_keep, swap(up[0], 8), [(48, 4 * width)])
        cross_part = onward([cross_keep], [cross_part[0]], 4)
        cross_part, rest_keep, grad_up = pin((cross_part, rest_part[1], grad_up))
        rest_part = onward([rest_keep], [rest_part[0]], 2)
        rest_part, pair_keep, cross_keep, sums = pin(
            (rest_part, pair_part[1], cross_part[1], sums)
        )
        pair_part = onward([pair_keep], [pair_part[0]], 4)
        sums = sums + swap(sums, 2)
        grad_cross, grad_query, grad_keyval = last_sum(
            cross_keep,
            swap(cross_part[0], 8),
            [(48, width), (48, width), (48, 2 * width)],
        )
        rest_keep, pair_part, grad_cross, grad_query, grad_keyval, sums = pin(
            (rest_part[1], pair_part, grad_cross, grad_query, grad_keyval, sums)
        )
        rest_part = onward([rest_keep], [rest_part[0]], 4)
        sums = sums + swap(sums, 4)
        rest_keep, pair_keep, sums = pin((rest_part[1], pair_part[1], sums))
        (grad_pair,) = last_sum(pair_keep, swap(pair_part[0], 8), [(48, 2 * width)])
        (grad_down,) = last_sum(down[1], swap(down[0], 2), [(192, width)])
        grad_first, grad_out = last_sum(
            rest_keep, swap(rest_part[0], 8), [(48, width), (48, width)]
        )
        sums = sums + swap(sums, 8)
        grad_qkv = jnp.concatenate([grad_first, grad_pair], 1)
        mine = lax.dynamic_slice_in_dim(sums[:7], device * share, share, 1)
        gains, biases = mine[0:6:2], mine[1:6:2]
        down_bias = mine[6]
        up_bias = lax.dynamic_slice_in_dim(sums[7:].reshape(-1), device * 192, 192)
        input_grad = jnp.concatenate([input_top, input_stay])
    else:
        _, unit_two, inverse_two = layer_norm(after_self, scales[1], shifts[1])
        after_cross = after_self + matmul(cross_mixed, w_cross[0])
        third, unit_three, inverse_three = layer_norm(after_cross, scales[2], shifts[2])
        value, slope = gelu_pair(matmul(third, w_up[0]) + b_up[0])
        hidden = value.astype(jnp.bfloat16)
        output = (after_cross + matmul(hidden, w_down[0]) + b_down[0]).astype(jnp.bfloat16)
        upstream = dy.astype(jnp.float32)
        pre_low = (dot_nt(dy, w_down[0]) * slope).astype(jnp.bfloat16)
        back_three, gain_three, shift_three = norm_back(
            dot_nt(pre_low, w_up[0]), unit_three, inverse_three, scales[2]
        )
        grad_cross_in = upstream + back_three
        cross_low = grad_cross_in.astype(jnp.bfloat16)
        grad_cmix = dot_nt(cross_low, w_cross[0]).astype(jnp.bfloat16)
        cross_grads = attn_bwd(
            cross_q, cross_pair, cross_pair, 0, 0, 6, grad_cmix, cross_probs, "crossb"
        )
        pair = jnp.concatenate([cross_grads[1], cross_grads[2]], 1)
        returned = partner_of(dot_nt(pair, w_keyval[0]).astype(jnp.bfloat16))
        back_two, gain_two, shift_two = norm_back(
            dot_nt(cross_grads[0], w_query[0]) + returned.astype(jnp.float32),
            unit_two,
            inverse_two,
            scales[1],
        )
        self_low = (grad_cross_in + back_two).astype(jnp.bfloat16)
        moved_low = jnp.concatenate([self_low[half:], lax.ppermute(self_low[:half], both, forth)])
        grad_smix = dot_nt(moved_low, w_out[0]).astype(jnp.bfloat16)
        self_grads = attn_bwd(packed, packed, packed, 0, 6, 12, grad_smix, self_probs, "selfb")
        packed_grad = jnp.concatenate([self_grads[0], self_grads[1], self_grads[2]], 1)
        back_one, gain_one, shift_one = norm_back(
            dot_nt(packed_grad, w_qkv[0]), unit_one, inverse_one, scales[0]
        )
        moved_grad = (moved_low.astype(jnp.float32) + back_one).astype(jnp.bfloat16)
        input_grad = jnp.concatenate([lax.ppermute(moved_grad[half:], both, back), moved_grad[:half]])

        def summed(grad):
            return lax.psum_scatter(grad, "page", scatter_dimension=0, tiled=True)

        def scattered(left, right):
            return summed(
                lax.dot_general(
                    left, right, (((0,), (0,)), ((), ())), preferred_element_type=jnp.float32
                )
            )

        grad_down = scattered(hidden, dy)
        grad_up = scattered(third, pre_low)
        grad_cross = scattered(cross_mixed, cross_low)
        grad_query = scattered(second, cross_grads[0])
        grad_keyval = scattered(partner, pair)
        grad_out = scattered(jnp.concatenate([back_mixed, near]), self_low)
        grad_qkv = scattered(first, packed_grad)
        gains = summed(jnp.stack([gain_one, gain_two, gain_three], 1)).T
        biases = summed(jnp.stack([shift_one, shift_two, shift_three], 1)).T
        down_bias = summed(jnp.sum(upstream, axis=0))
        up_bias = summed(jnp.sum(pre_low.astype(jnp.float32), axis=0))
    return (
        output[None],
        input_grad[None],
        gains.T[None],
        biases.T[None],
        grad_qkv[None],
        grad_out[None],
        grad_query[None],
        grad_keyval[None],
        grad_cross[None],
        grad_up[None],
        up_bias[None],
        grad_down[None],
        down_bias[None],
    )


def solution(mesh):
    tokens = P("stream", "page", None)
    whole = P("stream", None, None)
    placed = (tokens, tokens) + (whole,) * 8 + (P("stream", None), whole, P("stream", None))
    return jax.shard_map(
        on_device,
        mesh=mesh,
        in_specs=placed + (P(), P("page")),
        out_specs=(tokens,) * 10 + (P("stream", "page"), tokens, P("stream", "page")),
        check_vma=False,
    )
```

```python
import functools

import jax
import jax.numpy as jnp
from jax import lax
from jax.experimental import pallas as pl
from jax.experimental.pallas import tpu as pltpu
from jax.sharding import PartitionSpec as P

HEADS = 12
HEAD = 64
WIN = 12
SHIFT = 6
NORM_EPS = 1e-05
MASKED = -1e30


def dot_nt(a,b):
    return lax.dot_general(a,b,(((1,),(1,)),((),())),preferred_element_type=jnp.float32)
def dot_nn(a,b):
    return lax.dot_general(a,b,(((1,),(0,)),((),())),preferred_element_type=jnp.float32)

def fill_self_bias(info, bias, first=0):
    tokens, count = bias.shape
    half=tokens//2
    cols=tokens//12
    def codes(shape,dim,start):
        t=lax.broadcasted_iota(jnp.int32,shape,dim)+start
        row=jnp.zeros(shape,jnp.int32)
        page=jnp.full(shape,info[2],jnp.int32)
        for r in range(1,12):
            inside=t>=r*cols
            row=jnp.where(inside,r,row)
            page=jnp.where(inside,info[2+r],page)
        c=t-row*cols
        win=jnp.zeros(shape,jnp.int32)
        for w in range(1,cols//12):
            win=jnp.where((c>=6+12*(w-1))&(c<6+12*w),w,win)
        win=jnp.where(c>=cols-6,cols//12+1,win)
        slot=jnp.where(t<half,t+half,t-half)
        return page*16+win,slot
    ck,sk=codes((tokens,1),0,0)
    cq,sq=codes((1,count),1,first)
    length=info[1]
    @pl.when(info[0]==1)
    def _():
        ok=(sk<=sq)&(sk<length)
        bias[...]=jnp.where(ok,0.0,MASKED)
    @pl.when(info[0]==0)
    def _():
        bias[...]=jnp.where(ck==cq,0.0,MASKED)

def fill_cross_bias(info,bias,first=0):
    tokens=bias.shape[0]
    t=lax.broadcasted_iota(jnp.int32,bias.shape,0)
    bias[...]=jnp.where((t<info[1])|(info[0]==1),0.0,MASKED)

def lane_pick(e,scale):
    lane=lax.broadcasted_iota(jnp.int32,(1,2*HEAD),1)
    return jnp.where((lane>=HEAD)==bool(e),scale,0.0).astype(jnp.bfloat16)

def fwd_kernel(fill, info, q_ref, k_ref, v_ref, o_ref, p_ref, bias):
    @pl.when(pl.program_id(0) == 0)
    def _():
        fill(info, bias)

    q, k = q_ref[...], k_ref[...]
    vt = v_ref[...].T
    scores = [dot_nt(k, q * lane_pick(e, HEAD**-0.5)) + bias[...] for e in range(2)]
    outs = []
    for e in range(2):
        weights = jnp.exp(scores[e] - jnp.max(scores[e], axis=0, keepdims=True))
        inverse = 1.0 / jnp.sum(weights, axis=0, keepdims=True)
        probs = (weights * inverse).astype(jnp.bfloat16)
        p_ref[e] = probs
        outs.append(dot_nn(vt[e * HEAD : (e + 1) * HEAD], probs))
    o_ref[...] = jnp.concatenate(outs, 0).T.astype(jnp.bfloat16)


NOTHING = pl.CostEstimate(flops=1000, bytes_accessed=1000, transcendentals=0)


def attn_fwd(info, q, k, v, qo, ko, vo, fill, name):
    tokens = q.shape[0]
    spec = lambda off: pl.BlockSpec((tokens, 128), lambda j, info: (0, off + j))
    return pl.pallas_call(
        functools.partial(fwd_kernel, fill),
        grid_spec=pltpu.PrefetchScalarGridSpec(
            num_scalar_prefetch=1,
            grid=(HEADS // 2,),
            in_specs=[spec(qo), spec(ko), spec(vo)],
            out_specs=[spec(0), pl.BlockSpec((2, tokens, tokens), lambda j, info: (j, 0, 0))],
            scratch_shapes=[pltpu.VMEM((tokens, tokens), jnp.float32)],
        ),
        out_shape=[
            jax.ShapeDtypeStruct((tokens, HEADS * HEAD), jnp.bfloat16),
            pltpu.HBM((HEADS, tokens, tokens), jnp.bfloat16),
        ],
        compiler_params=pltpu.CompilerParams(vmem_limit_bytes=24 * 2**20),
        cost_estimate=NOTHING,
        name=name,
    )(info, q, k, v)


def bwd_kernel(q_ref, k_ref, v_ref, do_ref, p_ref, d_ref):
    grads = backward_heads(q_ref[...], k_ref[...], v_ref[...], do_ref[...], p_ref)
    for i in range(3):
        d_ref[i] = grads[i]


def attn_bwd(q, k, v, qo, ko, vo, do, probs, name):
    tokens = q.shape[0]
    spec = lambda off: pl.BlockSpec((tokens, 128), lambda j: (0, off + j))
    return pl.pallas_call(
        bwd_kernel,
        grid=(HEADS // 2,),
        in_specs=[spec(qo), spec(ko), spec(vo), spec(0)]
        + [pl.BlockSpec((2, tokens, tokens), lambda j: (j, 0, 0))],
        out_specs=pl.BlockSpec((3, tokens, 128), lambda j: (0, 0, j)),
        out_shape=jax.ShapeDtypeStruct((3, tokens, HEADS * HEAD), jnp.bfloat16),
        compiler_params=pltpu.CompilerParams(vmem_limit_bytes=24 * 2**20),
        cost_estimate=NOTHING,
        name=name,
    )(q, k, v, do, pltpu.with_memory_space_constraint(probs, pltpu.HBM))


def layer_norm(inputs, scales, shifts):
    average = jnp.mean(inputs, axis=1, keepdims=True)
    centred = inputs - average
    spread = jnp.mean(centred * centred, axis=1, keepdims=True)
    inverse = lax.rsqrt(spread + NORM_EPS)
    unit = centred * inverse
    return (unit * scales + shifts).astype(jnp.bfloat16), unit, inverse


def norm_back(upstream, unit, inverse, scales):
    scaled = upstream * scales
    inner = (
        scaled
        - jnp.mean(scaled, axis=1, keepdims=True)
        - unit * jnp.mean(scaled * unit, axis=1, keepdims=True)
    )
    return (inverse * inner, jnp.sum(upstream * unit, axis=0), jnp.sum(upstream, axis=0))


def matmul(left, right):
    return jnp.dot(left, right, preferred_element_type=jnp.float32)


def gelu_pair(pre):
    root = 0.7978845608028654
    square = pre * pre
    gate = 0.5 + 0.5 * jnp.tanh(pre * (root + root * 0.044715 * square))
    value = pre * gate
    return value, gate + value * (1.0 - gate) * (2 * root + 6 * root * 0.044715 * square)


def layer_parts(v):
    average = jnp.mean(v, axis=1, keepdims=True)
    centred = v - average
    inverse = lax.rsqrt(jnp.mean(centred * centred, axis=1, keepdims=True) + NORM_EPS)
    return centred * inverse, inverse


def layer_back(grad, unit, inverse, scale):
    scaled = grad * scale
    return inverse * (
        scaled
        - jnp.mean(scaled, axis=1, keepdims=True)
        - unit * jnp.mean(scaled * unit, axis=1, keepdims=True)
    )


def column_sums(*values):
    rows = [jnp.sum(v, axis=0, keepdims=True) for v in values]
    rows.append(jnp.zeros((8 - len(rows), rows[0].shape[1]), jnp.float32))
    return jnp.concatenate(rows)


def sort_rows(order, x, across, sorted_rows):
    rows = sorted_rows.shape[0] // 16
    across[...] = x.T
    for n in range(16):
        start = pl.multiple_of(order[n] * rows, 16)
        sorted_rows[n * rows : (n + 1) * rows, :] = across[pl.ds(start, rows), :]


def feed_kernel(
    order, after_ref, mixed_ref, dy_ref, scales_ref, shifts_ref, cross_ref, down_bias_ref,
    up_ref, up_bias_ref, down_ref,
    out_ref, grad_ref, kept_ref, bias_ref,
    down_send, down_keep, up_send, up_keep,
    third_rows, across, sorted_rows, after, total, grad_total,
):
    step = pl.program_id(0)
    rows = dy_ref.shape[1] // 16
    half = 8 * rows

    @pl.when(step == 0)
    def _():
        after[...] = after_ref[...] + dot_nn(mixed_ref[...], cross_ref[0])
        unit = layer_parts(after[...])[0]
        third_rows[...] = (unit * scales_ref[2:3, :] + shifts_ref[2:3, :]).astype(jnp.bfloat16)
        sort_rows(order, third_rows[...], across, sorted_rows)
        total[...] = after[...] + down_bias_ref[...]
        grad_total[...] = jnp.zeros_like(grad_total)

    dy, third = dy_ref[...], third_rows[...]
    tile = up_ref.shape[2] // 2
    deep = tile // 2
    parts = [slice(0, tile), slice(tile, 2 * tile)]
    pre = [dot_nn(third, up_ref[0, :, p]) + up_bias_ref[:, p] for p in parts]
    grad_hidden = [dot_nt(dy, down_ref[0, p, :]) for p in parts]
    out = grad_third = 0.0
    grads = []
    for i, p in enumerate(parts):
        value, slope = gelu_pair(pre[i])
        hidden = value.astype(jnp.bfloat16)
        low = (grad_hidden[i] * slope).astype(jnp.bfloat16)
        bias_ref[0, :, p] = jnp.sum(low.astype(jnp.float32), axis=0, keepdims=True)
        grad = dot_nn(sorted_rows[...], low).astype(jnp.bfloat16)
        up_send[:, :, p] = grad[:half].reshape(8, rows, tile)
        up_keep[:, :, p] = grad[half:].reshape(8, rows, tile)
        grads.append(dot_nn(hidden.T, dy).astype(jnp.bfloat16))
        out += dot_nn(hidden, down_ref[0, p, :])
        grad_third += dot_nt(low, up_ref[0, :, p])
    total[...] += out
    grad_total[...] += grad_third
    for odd in range(2):
        for far in range(2):

            @pl.when((order[15] % 2 == odd) & (order[15] // 2 % 2 == far))
            def _():
                for n in range(2):
                    both = grads[n ^ far ^ 1]
                    down_send[n] = both[deep * (1 - odd) : deep * (2 - odd)]
                    down_keep[n] = both[deep * odd : deep * (odd + 1)]

    @pl.when(step == pl.num_programs(0) - 1)
    def _():
        out_ref[...] = total[...].astype(jnp.bfloat16)
        grad_ref[...] = grad_total[...]
        kept_ref[...] = after[...]


def third_kernel(third_ref, after_ref, dy_ref, scales_ref, cross_ref, grad_ref, low_ref, mix_ref, sums_ref):
    upstream = dy_ref[...].astype(jnp.float32)
    unit, inverse = layer_parts(after_ref[...])
    grad = third_ref[...]
    sums_ref[...] = column_sums(grad * unit, grad, upstream)
    grad_ref[...] = upstream + layer_back(grad, unit, inverse, scales_ref[2:3, :])
    low_ref[...] = grad_ref[...].astype(jnp.bfloat16)
    mix_ref[...] = dot_nt(low_ref[...], cross_ref[0]).astype(jnp.bfloat16)


def third_back(grad, after, dy, scales, w_cross):
    full = jax.ShapeDtypeStruct(after.shape, jnp.float32)
    low = jax.ShapeDtypeStruct(after.shape, jnp.bfloat16)
    return pl.pallas_call(
        third_kernel,
        out_shape=[full, low, low, jax.ShapeDtypeStruct((8, after.shape[1]), jnp.float32)],
        compiler_params=pltpu.CompilerParams(vmem_limit_bytes=32 * 2**20),
        cost_estimate=NOTHING,
        name="third",
    )(grad, after, dy, scales, w_cross)


def feed_forward(order, after, mixed, dy, scales, shifts, w_cross, w_up, b_up, w_down, b_down):
    tokens, width = dy.shape
    deep = w_up.shape[2]
    tile = deep // 4
    rows = width // 16
    whole = lambda *shape: pl.BlockSpec(shape, lambda j, order: (0,) * len(shape))
    where = lambda j, order: order[8 + j] // 4
    once = lambda *shape: pl.BlockSpec(
        shape, lambda j, order: (0,) * len(shape), pipeline_mode=pl.Buffered(1)
    )
    token = once(tokens, width)
    down_half = jax.ShapeDtypeStruct((8, deep // 16, width), jnp.bfloat16)
    up_half = jax.ShapeDtypeStruct((8, 4 * rows, tile), jnp.bfloat16)
    down_piece = pl.BlockSpec((2, deep // 16, width), lambda j, order: (j, 0, 0))
    up_piece = pl.BlockSpec((8, rows, tile), lambda j, order: (0, where(j, order), 0))
    low = jax.ShapeDtypeStruct((tokens, width), jnp.bfloat16)
    full = jax.ShapeDtypeStruct((tokens, width), jnp.float32)
    out = pl.pallas_call(
        feed_kernel,
        grid_spec=pltpu.PrefetchScalarGridSpec(
            num_scalar_prefetch=1,
            grid=(4,),
            in_specs=[
                token,
                token,
                token,
                whole(3, width),
                whole(3, width),
                once(1, width, width),
                whole(1, width),
                pl.BlockSpec((1, width, tile), lambda j, order: (0, 0, where(j, order))),
                pl.BlockSpec((1, tile), lambda j, order: (0, where(j, order))),
                pl.BlockSpec((1, tile, width), lambda j, order: (0, where(j, order), 0)),
            ],
            out_specs=[
                token,
                token,
                token,
                pl.BlockSpec((1, 1, tile), lambda j, order: (where(j, order), 0, 0)),
                down_piece,
                down_piece,
                up_piece,
                up_piece,
            ],
            scratch_shapes=[pltpu.VMEM((tokens, width), jnp.bfloat16)]
            + [pltpu.VMEM((width, tokens), jnp.bfloat16)] * 2
            + [pltpu.VMEM((tokens, width), jnp.float32)] * 3,
        ),
        out_shape=[
            low,
            full,
            full,
            jax.ShapeDtypeStruct((4, 1, tile), jnp.float32),
            down_half,
            down_half,
            up_half,
            up_half,
        ],
        compiler_params=pltpu.CompilerParams(vmem_limit_bytes=36 * 2**20),
        cost_estimate=NOTHING,
        name="feed",
    )(order, after, mixed, dy, scales, shifts, w_cross, b_down, w_up, b_up, w_down)
    return (*out[:4], (out[4], out[5]), (out[6], out[7]))


def backward_heads(q, k, v, do, p_ref):
    kt = k.T
    queries = []
    keys = values = 0.0
    picked = [do * lane_pick(e, 1.0) for e in range(2)]
    grads = [dot_nt(v, picked[e]) for e in range(2)]
    for e in range(2):
        probs = p_ref[e]
        wide = probs.astype(jnp.float32)
        part = wide * grads[e]
        total = jnp.sum(part, axis=0, keepdims=True)
        ds = (part - wide * total).astype(jnp.bfloat16)
        values += dot_nn(probs, picked[e])
        keys += dot_nn(ds, q * lane_pick(e, HEAD**-0.5))
        queries.append(dot_nn(kt[e * HEAD : (e + 1) * HEAD], ds) * HEAD**-0.5)
    queries = jnp.concatenate(queries, 0).T
    return [g.astype(jnp.bfloat16) for g in (queries, keys, values)]


def self_back_kernel(q_ref, k_ref, v_ref, near_ref, far_ref, out_ref, p_ref, d_ref):
    low = jnp.concatenate([near_ref[...], far_ref[...]])
    do = dot_nt(low, out_ref[0]).astype(jnp.bfloat16)
    grads = backward_heads(q_ref[...], k_ref[...], v_ref[...], do, p_ref)
    for i in range(3):
        d_ref[i] = grads[i]


def self_back(packed, near, far, w_out, probs):
    tokens, width = packed.shape[0], near.shape[1]
    spec = lambda off: pl.BlockSpec((tokens, 128), lambda j: (0, off + j))
    rows = pl.BlockSpec(near.shape, lambda j: (0, 0))
    return pl.pallas_call(
        self_back_kernel,
        grid=(HEADS // 2,),
        in_specs=[spec(0), spec(6), spec(12), rows, rows]
        + [pl.BlockSpec((1, 128, width), lambda j: (0, j, 0))]
        + [pl.BlockSpec((2, tokens, tokens), lambda j: (j, 0, 0))],
        out_specs=pl.BlockSpec((3, tokens, 128), lambda j: (0, 0, j)),
        out_shape=jax.ShapeDtypeStruct((3, tokens, width), jnp.bfloat16),
        compiler_params=pltpu.CompilerParams(vmem_limit_bytes=24 * 2**20),
        cost_estimate=NOTHING,
        name="selfb",
    )(packed, packed, packed, near, far, w_out, pltpu.with_memory_space_constraint(probs, pltpu.HBM))


def second_kernel(
    near_back_ref, far_back_ref, near_given_ref, far_given_ref, near_after_ref, far_after_ref,
    near_grad_ref, far_grad_ref, scales_ref, near_ref, far_ref, sums_ref,
):
    sums = 0.0
    for back, given, after, grad, out in (
        (near_back_ref, near_given_ref, near_after_ref, near_grad_ref, near_ref),
        (far_back_ref, far_given_ref, far_after_ref, far_grad_ref, far_ref),
    ):
        unit, inverse = layer_parts(after[...])
        upstream = back[...].astype(jnp.float32) + given[...].astype(jnp.float32)
        sums += column_sums(upstream * unit, upstream)
        below = layer_back(upstream, unit, inverse, scales_ref[1:2, :])
        out[...] = (grad[...].astype(jnp.float32) + below).astype(jnp.bfloat16)
    sums_ref[...] = sums


def second_back(back, far_back, near_given, far_given, after, far_after, grad, far_grad, scales):
    half, width = near_given.shape
    low = pl.BlockSpec((half, width), lambda j: (1, 0))
    rows = pl.BlockSpec((half, width), lambda j: (0, 0))
    out = jax.ShapeDtypeStruct((half, width), jnp.bfloat16)
    return pl.pallas_call(
        second_kernel,
        grid=(1,),
        in_specs=[low, rows, rows, rows, low, rows, low, rows]
        + [pl.BlockSpec((3, width), lambda j: (0, 0))],
        out_specs=[rows, rows, pl.BlockSpec((8, width), lambda j: (0, 0))],
        out_shape=[out, out, jax.ShapeDtypeStruct((8, width), jnp.float32)],
        compiler_params=pltpu.CompilerParams(vmem_limit_bytes=24 * 2**20),
        cost_estimate=NOTHING,
        name="second",
    )(back, far_back, near_given, far_given, after, far_after, grad, far_grad, scales)


def tail_kernel(
    order, d_ref, w_ref, first_ref, mixed_ref, moved_ref, near_ref, far_ref, scales_ref, *refs,
):
    step = pl.program_id(0)
    stay_ref, gone_ref, sums_ref = refs[8:11]
    across, sorted_rows, total = refs[11:]
    half = sorted_rows.shape[0] // 2

    @pl.when(step == 0)
    def _():
        sort_rows(order, first_ref[...], across, sorted_rows)

    for i in range(3):

        @pl.when(step == i)
        def _():
            part = dot_nt(d_ref[0], w_ref[0])
            grad = dot_nn(sorted_rows[...], d_ref[0]).astype(jnp.bfloat16)
            refs[2 * i][...] = grad[:half].reshape(refs[0].shape)
            refs[2 * i + 1][...] = grad[half:].reshape(refs[0].shape)
            if i == 0:
                total[...] = part
            else:
                total[...] += part

    @pl.when(step == 3)
    def _():
        sort_rows(order, mixed_ref[...], across, sorted_rows)
        low = jnp.concatenate([near_ref[...], far_ref[...]])
        grad = dot_nn(sorted_rows[...], low).astype(jnp.bfloat16)
        refs[6][...] = grad[:half].reshape(refs[0].shape)
        refs[7][...] = grad[half:].reshape(refs[0].shape)
        rows = stay_ref.shape[0]
        unit, inverse = layer_parts(moved_ref[...].astype(jnp.float32))
        grad = total[...]
        sums_ref[...] = column_sums(grad * unit, grad)
        back = layer_back(grad, unit, inverse, scales_ref[0:1, :])
        stay_ref[...] = (near_ref[...].astype(jnp.float32) + back[:rows]).astype(jnp.bfloat16)
        gone_ref[...] = (far_ref[...].astype(jnp.float32) + back[rows:]).astype(jnp.bfloat16)


def tail_grads(order, grads, w_qkv, first, mixed, moved, near, far, scales):
    tokens, width = moved.shape
    half = tokens // 2
    whole = lambda *shape: pl.BlockSpec(shape, lambda j, order: (0,) * len(shape))
    rows = jax.ShapeDtypeStruct((half, width), jnp.bfloat16)
    piece = (8, width // 16, width)
    last = lambda j: jnp.minimum(j, 2)
    outs = pl.pallas_call(
        tail_kernel,
        grid_spec=pltpu.PrefetchScalarGridSpec(
            num_scalar_prefetch=1,
            grid=(4,),
            in_specs=[
                pl.BlockSpec((1, tokens, width), lambda j, order: (last(j), 0, 0)),
                pl.BlockSpec((1, width, width), lambda j, order: (0, 0, last(j))),
                whole(tokens, width),
                whole(tokens, width),
                whole(tokens, width),
                whole(half, width),
                whole(half, width),
                whole(3, width),
            ],
            out_specs=[whole(*piece)] * 8 + [whole(half, width)] * 2 + [whole(8, width)],
            scratch_shapes=[pltpu.VMEM((width, tokens), jnp.bfloat16)] * 2
            + [pltpu.VMEM((tokens, width), jnp.float32)],
        ),
        out_shape=[jax.ShapeDtypeStruct(piece, jnp.bfloat16)] * 8
        + [rows, rows, jax.ShapeDtypeStruct((8, width), jnp.float32)],
        compiler_params=pltpu.CompilerParams(vmem_limit_bytes=40 * 2**20),
        cost_estimate=NOTHING,
        name="tail",
    )(order, grads, w_qkv, first, mixed, moved, near, far, scales)
    return [(outs[i], outs[i + 1]) for i in range(0, 8, 2)], *outs[8:]


def group_kernel(plan, halves, pieces, order, *refs):
    refs = list(refs)
    groups = [[refs.pop(0) for _ in range(n)] for n in halves]
    joined = lambda group: jnp.concatenate([r[...] for r in group]) if len(group) > 1 else group[0][...]
    outs, (across, sorted_rows) = refs[:-2], refs[-2:]
    half = sorted_rows.shape[0] // 2
    before = None
    for i, (x, dy, lead, target) in enumerate(plan):
        turn = x != before
        before = x

        @pl.when(pl.program_id(0) == i)
        def _():
            if turn:
                sort_rows(order, joined(groups[x]), across, sorted_rows)
            right = joined(groups[dy]) if lead is None else groups[dy][0][0]
            grad = dot_nn(sorted_rows[...], right).astype(jnp.bfloat16)
            send_ref, keep_ref = outs[2 * target], outs[2 * target + 1]
            send_ref[...] = grad[:half].reshape(send_ref.shape)
            keep_ref[...] = grad[half:].reshape(keep_ref.shape)


def grad_group(order, operands, plan, name):
    width = operands[0][0].shape[-1]
    rows = width // 16
    tokens = sum(a.shape[-2] for a in operands[0])
    in_specs = []
    for n, group in enumerate(operands):
        for a in group:
            if a.ndim == 2:
                in_specs.append(pl.BlockSpec(a.shape, lambda j, order: (0, 0)))
            else:
                first = min(i for i, p in enumerate(plan) if p[1] == n)
                in_specs.append(
                    pl.BlockSpec(
                        (1, *a.shape[1:]),
                        lambda j, order, first=first, last=a.shape[0] - 1: (
                            jnp.clip(j - first, 0, last),
                            0,
                            0,
                        ),
                    )
                )
    out_specs, out_shape = [], []
    for target in range(1 + max(p[3] for p in plan)):
        steps = [i for i, p in enumerate(plan) if p[3] == target]
        spec = pl.BlockSpec(
            (8, rows, width),
            lambda j, order, first=steps[0], last=len(steps) - 1: (
                0,
                jnp.clip(j - first, 0, last),
                0,
            ),
        )
        out_specs += [spec, spec]
        out_shape += [jax.ShapeDtypeStruct((8, rows * len(steps), width), jnp.bfloat16)] * 2
    outs = pl.pallas_call(
        functools.partial(group_kernel, plan, [len(g) for g in operands], len(out_specs)),
        grid_spec=pltpu.PrefetchScalarGridSpec(
            num_scalar_prefetch=1,
            grid=(len(plan),),
            in_specs=in_specs,
            out_specs=out_specs,
            scratch_shapes=[pltpu.VMEM((width, tokens), jnp.bfloat16)] * 2,
        ),
        out_shape=out_shape,
        compiler_params=pltpu.CompilerParams(vmem_limit_bytes=32 * 2**20),
        cost_estimate=NOTHING,
        name=name,
    )(order, *[a for group in operands for a in group])
    return [(outs[i], outs[i + 1]) for i in range(0, len(outs), 2)]


def add_kernel(count, *refs):
    at = 0
    for n in range(count):
        keep, arrived = refs[2 * n], refs[2 * n + 1]
        rows = keep.shape[-2]
        for i, out in enumerate(refs[2 * count :]):
            out[0, at : at + rows, :] = keep[i, 0] + arrived[i, 0]
        at += rows


def add_halves(keeps, arrivals, name="add"):
    pairs = keeps[0].shape[0] // 2
    width = keeps[0].shape[2]
    rows = sum(k.shape[1] for k in keeps)
    operands = []
    for keep, arrived in zip(keeps, arrivals):
        operands += [a.reshape(2, pairs, *a.shape[1:]) for a in (keep, arrived)]
    out = pl.BlockSpec((1, rows, width), lambda j: (j, 0, 0))
    return pl.pallas_call(
        functools.partial(add_kernel, len(keeps)),
        grid=(pairs,),
        in_specs=[
            pl.BlockSpec((2, 1, *a.shape[2:]), lambda j: (0, j, 0, 0)) for a in operands
        ],
        out_specs=[out, out],
        out_shape=[jax.ShapeDtypeStruct((pairs, rows, width), jnp.bfloat16)] * 2,
        compiler_params=pltpu.CompilerParams(vmem_limit_bytes=16 * 2**20),
        cost_estimate=NOTHING,
        name=name,
    )(*operands)


def last_kernel(keep_ref, arrived_ref, *outs):
    total = keep_ref[0].astype(jnp.float32) + arrived_ref[0].astype(jnp.float32)
    width = total.shape[1]
    at = 0
    for out in outs:
        rows, columns = out.shape
        for n in range(columns // width):
            out[:, n * width : (n + 1) * width] = total[at : at + rows]
            at += rows


def last_sum(keep, arrived, shapes):
    return pl.pallas_call(
        last_kernel,
        out_shape=[jax.ShapeDtypeStruct(s, jnp.float32) for s in shapes],
        compiler_params=pltpu.CompilerParams(vmem_limit_bytes=16 * 2**20),
        cost_estimate=NOTHING,
        name="last",
    )(keep, arrived)


def swap(x, bit):
    return lax.ppermute(x, "page", [(i, i ^ bit) for i in range(16)])


pin = lax.optimization_barrier


def on_device(
    block_input,
    cotangent,
    norm_gain,
    norm_bias,
    w_qkv,
    w_out,
    w_query,
    w_keyval,
    w_cross,
    w_up,
    b_up,
    w_down,
    b_down,
    row_page,
    lengths,
):
    x = block_input[0]
    dy = cotangent[0]
    tokens, width = x.shape
    half = tokens // 2
    pages = lax.axis_size("page")
    device = lax.axis_index("page")
    stream = lax.axis_index("stream")
    scales = norm_gain[0].T
    shifts = norm_bias[0].T
    share = width // pages
    padded = jnp.concatenate([row_page, row_page[:SHIFT]])
    info = jnp.concatenate(
        [
            stream.astype(jnp.int32)[None],
            lengths,
            lax.dynamic_slice_in_dim(padded, device * WIN + SHIFT, WIN),
        ]
    )
    stay = [(pages + i, pages + i) for i in range(pages)]
    both = ("stream", "page")
    forth = [((i + 1) % pages, i) for i in range(pages)] + stay
    back = [(i, (i + 1) % pages) for i in range(pages)] + stay

    def partner_of(rows):
        return lax.ppermute(rows, "stream", [(0, 1), (1, 0)])

    moved = jnp.concatenate([x[half:], lax.ppermute(x[:half], both, forth)])
    first, unit_one, inverse_one = layer_norm(moved.astype(jnp.float32), scales[0], shifts[0])
    packed = matmul(first, w_qkv[0]).astype(jnp.bfloat16)
    moved_mixed, self_probs = attn_fwd(
        info, packed, packed, packed, 0, 6, 12, fill_self_bias, "selff"
    )
    gone, near = moved_mixed[half:], moved_mixed[:half]
    after_gone = moved[half:].astype(jnp.float32) + matmul(gone, w_out[0])
    second_gone = layer_norm(after_gone, scales[1], shifts[1])[0]
    partner_top = lax.ppermute(
        second_gone,
        both,
        [(i, pages + (i + 1) % pages) for i in range(pages)]
        + [(pages + i, i) for i in range(pages)],
    )
    back_mixed = lax.ppermute(gone, both, back)
    after_low = moved[:half].astype(jnp.float32) + matmul(near, w_out[0])
    second_low = layer_norm(after_low, scales[1], shifts[1])[0]
    partner_low = partner_of(second_low)
    back_mixed, second_low, partner_top = pin((back_mixed, second_low, partner_top))
    after_top = x[:half].astype(jnp.float32) + matmul(back_mixed, w_out[0])
    second_top = layer_norm(after_top, scales[1], shifts[1])[0]
    after_self = jnp.concatenate([after_top, after_low])
    second = jnp.concatenate([second_top, second_low])
    cross_q = matmul(second, w_query[0]).astype(jnp.bfloat16)
    cross_q, after_self, partner_top, partner_low = pin(
        (cross_q, after_self, partner_top, partner_low)
    )
    partner = jnp.concatenate([partner_top, partner_low])
    cross_pair = matmul(partner, w_keyval[0]).astype(jnp.bfloat16)
    cross_mixed, cross_probs = attn_fwd(
        info, cross_q, cross_pair, cross_pair, 0, 0, 6, fill_cross_bias, "crossf"
    )
    if pages == 16:
        ordinal = jnp.arange(16, dtype=jnp.int32)
        turned = 15 - ordinal
        turned = (turned & 1) << 3 | (turned & 2) << 1 | (turned & 4) >> 1 | (turned & 8) >> 3
        order = device.astype(jnp.int32) ^ turned
        output, grad_third, after_cross, up_bias, down, up = feed_forward(
            order, after_self, cross_mixed, dy, scales, shifts, w_cross, w_up, b_up, w_down, b_down
        )
        grad_cross_in, cross_low, grad_cmix, sums_three = third_back(
            grad_third, after_cross, dy, scales, w_cross
        )

        def onward(keeps, sends, bit):
            return add_halves(keeps, [swap(s, bit) for s in sends])

        grad_cmix, down_keep, up_keep = pin((grad_cmix, down[1], up[1]))
        down = onward([down_keep], [down[0]], 1)
        up = onward([up_keep], [up[0]], 1)
        grad_cmix, down, up = pin((grad_cmix, down, up))
        cross_grads = attn_bwd(
            cross_q, cross_pair, cross_pair, 0, 0, 6, grad_cmix, cross_probs, "crossb"
        )

        def given(rows):
            keys = dot_nt(cross_grads[1, rows], w_keyval[0][:, :width])
            return (keys + dot_nt(cross_grads[2, rows], w_keyval[0][:, width:])).astype(jnp.bfloat16)

        returned_top = lax.ppermute(
            given(slice(0, half)),
            both,
            [(i, pages + i) for i in range(pages)]
            + [(pages + (i + 1) % pages, i) for i in range(pages)],
        )
        returned_low = partner_of(given(slice(half, tokens)))
        query_back = dot_nt(cross_grads[0], w_query[0])
        far_back = lax.ppermute(query_back[:half].astype(jnp.bfloat16), both, forth)
        far_grad = lax.ppermute(cross_low[:half], both, forth)
        (cross_part,) = grad_group(
            order,
            (
                (cross_mixed,),
                (second_top, second_low),
                (partner_top, partner_low),
                (cross_low,),
                (cross_grads,),
            ),
            ((0, 3, None, 0), (1, 4, 0, 0), (2, 4, 1, 0), (2, 4, 2, 0)),
            "gcross",
        )
        down = onward([down[1]], [down[0]], 4)
        up = onward([up[1]], [up[0]], 2)
        returned_top, returned_low, far_back, far_grad, cross_part, down, up = pin(
            (returned_top, returned_low, far_back, far_grad, cross_part, down, up)
        )
        low_near, low_far, sums_two = second_back(
            query_back, far_back, returned_low, returned_top, after_self, after_gone,
            grad_cross_in, far_grad, scales,
        )
        low_near, cross_keep = pin((low_near, cross_part[1]))
        cross_part = onward([cross_keep], [cross_part[0]], 1)
        low_near, cross_part = pin((low_near, cross_part))
        self_grads = self_back(packed, low_near, low_far, w_out, self_probs)
        self_grads, up_keep = pin((self_grads, up[1]))
        up = onward([up_keep], [up[0]], 4)
        self_grads, up = pin((self_grads, up))
        parts, input_stay, input_gone, sums_one = tail_grads(
            order, self_grads, w_qkv, first, moved_mixed, moved, low_near, low_far, scales
        )
        parts = [parts[1], parts[2], parts[0], parts[3]]
        parts, cross_keep, down_keep = pin((parts, cross_part[1], down[1]))
        down = onward([down_keep], [down[0]], 8)
        cross_part = onward([cross_keep], [cross_part[0]], 2)
        sends, keeps = [p[0] for p in parts], [p[1] for p in parts]
        cross_part, keeps, down = pin((cross_part, keeps, down))
        pair_part = onward(keeps[:2], sends[:2], 1)
        rest_part = onward(keeps[2:], sends[2:], 1)
        pair_part, rest_part, input_gone, up, sums_one = pin(
            (pair_part, rest_part, input_gone, up, sums_one)
        )
        input_top = lax.ppermute(input_gone, both, back)
        sums = jnp.concatenate(
            [sums_one[:2], sums_two[:2], sums_three[:3], up_bias.reshape(4, width)]
        )
        sums = sums + swap(sums, 1)
        pair_keep, sums = pin((pair_part[1], sums))
        pair_part = onward([pair_keep], [pair_part[0]], 2)
        cross_keep, up_keep, pair_part = pin((cross_part[1], up[1], pair_part))
        (grad_up,) = last_sum(up_keep, swap(up[0], 8), [(48, 4 * width)])
        cross_part = onward([cross_keep], [cross_part[0]], 4)
        cross_part, rest_keep, grad_up = pin((cross_part, rest_part[1], grad_up))
        rest_part = onward([rest_keep], [rest_part[0]], 2)
        rest_part, pair_keep, cross_keep = pin((rest_part, pair_part[1], cross_part[1]))
        pair_part = onward([pair_keep], [pair_part[0]], 4)
        grad_cross, grad_query, grad_keyval = last_sum(
            cross_keep,
            swap(cross_part[0], 8),
            [(48, width), (48, width), (48, 2 * width)],
        )
        rest_keep, pair_part, grad_cross, grad_query, grad_keyval, sums = pin(
            (rest_part[1], pair_part, grad_cross, grad_query, grad_keyval, sums)
        )
        rest_part = onward([rest_keep], [rest_part[0]], 4)
        rest_part, pair_keep, sums = pin((rest_part, pair_part[1], sums))
        sums = sums + swap(sums, 2)
        (grad_pair,) = last_sum(pair_keep, swap(pair_part[0], 8), [(48, 2 * width)])
        (grad_down,) = last_sum(down[1], swap(down[0], 2), [(192, width)])
        sums = sums + swap(sums, 4)
        rest_keep, grad_pair, sums = pin((rest_part[1], grad_pair, sums))
        grad_first, grad_out = last_sum(
            rest_keep, swap(rest_part[0], 8), [(48, width), (48, width)]
        )
        sums = sums + swap(sums, 8)
        grad_qkv = jnp.concatenate([grad_first, grad_pair], 1)
        mine = lax.dynamic_slice_in_dim(sums[:7], device * share, share, 1)
        gains, biases = mine[0:6:2], mine[1:6:2]
        down_bias = mine[6]
        up_bias = lax.dynamic_slice_in_dim(sums[7:].reshape(-1), device * 192, 192)
        input_grad = jnp.concatenate([input_top, input_stay])
    else:
        _, unit_two, inverse_two = layer_norm(after_self, scales[1], shifts[1])
        after_cross = after_self + matmul(cross_mixed, w_cross[0])
        third, unit_three, inverse_three = layer_norm(after_cross, scales[2], shifts[2])
        value, slope = gelu_pair(matmul(third, w_up[0]) + b_up[0])
        hidden = value.astype(jnp.bfloat16)
        output = (after_cross + matmul(hidden, w_down[0]) + b_down[0]).astype(jnp.bfloat16)
        upstream = dy.astype(jnp.float32)
        pre_low = (dot_nt(dy, w_down[0]) * slope).astype(jnp.bfloat16)
        back_three, gain_three, shift_three = norm_back(
            dot_nt(pre_low, w_up[0]), unit_three, inverse_three, scales[2]
        )
        grad_cross_in = upstream + back_three
        cross_low = grad_cross_in.astype(jnp.bfloat16)
        grad_cmix = dot_nt(cross_low, w_cross[0]).astype(jnp.bfloat16)
        cross_grads = attn_bwd(
            cross_q, cross_pair, cross_pair, 0, 0, 6, grad_cmix, cross_probs, "crossb"
        )
        pair = jnp.concatenate([cross_grads[1], cross_grads[2]], 1)
        returned = partner_of(dot_nt(pair, w_keyval[0]).astype(jnp.bfloat16))
        back_two, gain_two, shift_two = norm_back(
            dot_nt(cross_grads[0], w_query[0]) + returned.astype(jnp.float32),
            unit_two,
            inverse_two,
            scales[1],
        )
        self_low = (grad_cross_in + back_two).astype(jnp.bfloat16)
        moved_low = jnp.concatenate([self_low[half:], lax.ppermute(self_low[:half], both, forth)])
        grad_smix = dot_nt(moved_low, w_out[0]).astype(jnp.bfloat16)
        self_grads = attn_bwd(packed, packed, packed, 0, 6, 12, grad_smix, self_probs, "selfb")
        packed_grad = jnp.concatenate([self_grads[0], self_grads[1], self_grads[2]], 1)
        back_one, gain_one, shift_one = norm_back(
            dot_nt(packed_grad, w_qkv[0]), unit_one, inverse_one, scales[0]
        )
        moved_grad = (moved_low.astype(jnp.float32) + back_one).astype(jnp.bfloat16)
        input_grad = jnp.concatenate([lax.ppermute(moved_grad[half:], both, back), moved_grad[:half]])

        def summed(grad):
            return lax.psum_scatter(grad, "page", scatter_dimension=0, tiled=True)

        def scattered(left, right):
            return summed(
                lax.dot_general(
                    left, right, (((0,), (0,)), ((), ())), preferred_element_type=jnp.float32
                )
            )

        grad_down = scattered(hidden, dy)
        grad_up = scattered(third, pre_low)
        grad_cross = scattered(cross_mixed, cross_low)
        grad_query = scattered(second, cross_grads[0])
        grad_keyval = scattered(partner, pair)
        grad_out = scattered(jnp.concatenate([back_mixed, near]), self_low)
        grad_qkv = scattered(first, packed_grad)
        gains = summed(jnp.stack([gain_one, gain_two, gain_three], 1)).T
        biases = summed(jnp.stack([shift_one, shift_two, shift_three], 1)).T
        down_bias = summed(jnp.sum(upstream, axis=0))
        up_bias = summed(jnp.sum(pre_low.astype(jnp.float32), axis=0))
    return (
        output[None],
        input_grad[None],
        gains.T[None],
        biases.T[None],
        grad_qkv[None],
        grad_out[None],
        grad_query[None],
        grad_keyval[None],
        grad_cross[None],
        grad_up[None],
        up_bias[None],
        grad_down[None],
        down_bias[None],
    )


def solution(mesh):
    tokens = P("stream", "page", None)
    whole = P("stream", None, None)
    placed = (tokens, tokens) + (whole,) * 8 + (P("stream", None), whole, P("stream", None))
    return jax.shard_map(
        on_device,
        mesh=mesh,
        in_specs=placed + (P(), P("page")),
        out_specs=(tokens,) * 10 + (P("stream", "page"), tokens, P("stream", "page")),
        check_vma=False,
    )
```

```python
import functools

import jax
import jax.numpy as jnp
from jax import lax
from jax.experimental import pallas as pl
from jax.experimental.pallas import tpu as pltpu
from jax.sharding import PartitionSpec as P

HEADS = 12
HEAD = 64
WIN = 12
SHIFT = 6
NORM_EPS = 1e-05
MASKED = -1e30


def dot_nt(a,b):
    return lax.dot_general(a,b,(((1,),(1,)),((),())),preferred_element_type=jnp.float32)
def dot_nn(a,b):
    return lax.dot_general(a,b,(((1,),(0,)),((),())),preferred_element_type=jnp.float32)

def fill_self_bias(info, bias, first=0):
    tokens, count = bias.shape
    half=tokens//2
    cols=tokens//12
    def codes(shape,dim,start):
        t=lax.broadcasted_iota(jnp.int32,shape,dim)+start
        row=jnp.zeros(shape,jnp.int32)
        page=jnp.full(shape,info[2],jnp.int32)
        for r in range(1,12):
            inside=t>=r*cols
            row=jnp.where(inside,r,row)
            page=jnp.where(inside,info[2+r],page)
        c=t-row*cols
        win=jnp.zeros(shape,jnp.int32)
        for w in range(1,cols//12):
            win=jnp.where((c>=6+12*(w-1))&(c<6+12*w),w,win)
        win=jnp.where(c>=cols-6,cols//12+1,win)
        slot=jnp.where(t<half,t+half,t-half)
        return page*16+win,slot
    ck,sk=codes((tokens,1),0,0)
    cq,sq=codes((1,count),1,first)
    length=info[1]
    @pl.when(info[0]==1)
    def _():
        ok=(sk<=sq)&(sk<length)
        bias[...]=jnp.where(ok,0.0,MASKED)
    @pl.when(info[0]==0)
    def _():
        bias[...]=jnp.where(ck==cq,0.0,MASKED)

def fill_cross_bias(info,bias,first=0):
    tokens=bias.shape[0]
    t=lax.broadcasted_iota(jnp.int32,bias.shape,0)
    bias[...]=jnp.where((t<info[1])|(info[0]==1),0.0,MASKED)

def lane_pick(e,scale):
    lane=lax.broadcasted_iota(jnp.int32,(1,2*HEAD),1)
    return jnp.where((lane>=HEAD)==bool(e),scale,0.0).astype(jnp.bfloat16)

def fwd_kernel(fill, info, q_ref, k_ref, v_ref, o_ref, p_ref, bias):
    @pl.when(pl.program_id(0) == 0)
    def _():
        fill(info, bias)

    q, k = q_ref[...], k_ref[...]
    vt = v_ref[...].T
    scores = [dot_nt(k, q * lane_pick(e, HEAD**-0.5)) + bias[...] for e in range(2)]
    outs = []
    for e in range(2):
        weights = jnp.exp(scores[e] - jnp.max(scores[e], axis=0, keepdims=True))
        inverse = 1.0 / jnp.sum(weights, axis=0, keepdims=True)
        probs = (weights * inverse).astype(jnp.bfloat16)
        p_ref[e] = probs
        outs.append(dot_nn(vt[e * HEAD : (e + 1) * HEAD], probs))
    o_ref[...] = jnp.concatenate(outs, 0).T.astype(jnp.bfloat16)


NOTHING = pl.CostEstimate(flops=1000, bytes_accessed=1000, transcendentals=0)


def attn_fwd(info, q, k, v, qo, ko, vo, fill, name):
    tokens = q.shape[0]
    spec = lambda off: pl.BlockSpec((tokens, 128), lambda j, info: (0, off + j))
    return pl.pallas_call(
        functools.partial(fwd_kernel, fill),
        grid_spec=pltpu.PrefetchScalarGridSpec(
            num_scalar_prefetch=1,
            grid=(HEADS // 2,),
            in_specs=[spec(qo), spec(ko), spec(vo)],
            out_specs=[spec(0), pl.BlockSpec((2, tokens, tokens), lambda j, info: (j, 0, 0))],
            scratch_shapes=[pltpu.VMEM((tokens, tokens), jnp.float32)],
        ),
        out_shape=[
            jax.ShapeDtypeStruct((tokens, HEADS * HEAD), jnp.bfloat16),
            pltpu.HBM((HEADS, tokens, tokens), jnp.bfloat16),
        ],
        compiler_params=pltpu.CompilerParams(vmem_limit_bytes=24 * 2**20),
        cost_estimate=NOTHING,
        name=name,
    )(info, q, k, v)


def bwd_kernel(q_ref, k_ref, v_ref, do_ref, p_ref, d_ref):
    grads = backward_heads(q_ref[...], k_ref[...], v_ref[...], do_ref[...], p_ref)
    for i in range(3):
        d_ref[i] = grads[i]


def attn_bwd(q, k, v, qo, ko, vo, do, probs, name):
    tokens = q.shape[0]
    spec = lambda off: pl.BlockSpec((tokens, 128), lambda j: (0, off + j))
    return pl.pallas_call(
        bwd_kernel,
        grid=(HEADS // 2,),
        in_specs=[spec(qo), spec(ko), spec(vo), spec(0)]
        + [pl.BlockSpec((2, tokens, tokens), lambda j: (j, 0, 0))],
        out_specs=pl.BlockSpec((3, tokens, 128), lambda j: (0, 0, j)),
        out_shape=jax.ShapeDtypeStruct((3, tokens, HEADS * HEAD), jnp.bfloat16),
        compiler_params=pltpu.CompilerParams(vmem_limit_bytes=24 * 2**20),
        cost_estimate=NOTHING,
        name=name,
    )(q, k, v, do, pltpu.with_memory_space_constraint(probs, pltpu.HBM))


def layer_norm(inputs, scales, shifts):
    average = jnp.mean(inputs, axis=1, keepdims=True)
    centred = inputs - average
    spread = jnp.mean(centred * centred, axis=1, keepdims=True)
    inverse = lax.rsqrt(spread + NORM_EPS)
    unit = centred * inverse
    return (unit * scales + shifts).astype(jnp.bfloat16), unit, inverse


def norm_back(upstream, unit, inverse, scales):
    scaled = upstream * scales
    inner = (
        scaled
        - jnp.mean(scaled, axis=1, keepdims=True)
        - unit * jnp.mean(scaled * unit, axis=1, keepdims=True)
    )
    return (inverse * inner, jnp.sum(upstream * unit, axis=0), jnp.sum(upstream, axis=0))


def matmul(left, right):
    return jnp.dot(left, right, preferred_element_type=jnp.float32)


def gelu_pair(pre):
    root = 0.7978845608028654
    square = pre * pre
    gate = 0.5 + 0.5 * jnp.tanh(pre * (root + root * 0.044715 * square))
    value = pre * gate
    return value, gate + value * (1.0 - gate) * (2 * root + 6 * root * 0.044715 * square)


def layer_parts(v):
    average = jnp.mean(v, axis=1, keepdims=True)
    centred = v - average
    inverse = lax.rsqrt(jnp.mean(centred * centred, axis=1, keepdims=True) + NORM_EPS)
    return centred * inverse, inverse


def layer_back(grad, unit, inverse, scale):
    scaled = grad * scale
    return inverse * (
        scaled
        - jnp.mean(scaled, axis=1, keepdims=True)
        - unit * jnp.mean(scaled * unit, axis=1, keepdims=True)
    )


def column_sums(*values):
    rows = [jnp.sum(v, axis=0, keepdims=True) for v in values]
    rows.append(jnp.zeros((8 - len(rows), rows[0].shape[1]), jnp.float32))
    return jnp.concatenate(rows)


def sort_rows(order, x, across, sorted_rows):
    rows = sorted_rows.shape[0] // 16
    across[...] = x.T
    for n in range(16):
        start = pl.multiple_of(order[n] * rows, 16)
        sorted_rows[n * rows : (n + 1) * rows, :] = across[pl.ds(start, rows), :]


def feed_kernel(
    order, after_ref, mixed_ref, dy_ref, scales_ref, shifts_ref, cross_ref, down_bias_ref,
    up_ref, up_bias_ref, down_ref,
    out_ref, grad_ref, kept_ref, bias_ref,
    down_send, down_keep, up_send, up_keep,
    third_rows, across, sorted_rows, after, total, grad_total,
):
    step = pl.program_id(0)
    rows = dy_ref.shape[1] // 16
    half = 8 * rows

    @pl.when(step == 0)
    def _():
        after[...] = after_ref[...] + dot_nn(mixed_ref[...], cross_ref[0])
        unit = layer_parts(after[...])[0]
        third_rows[...] = (unit * scales_ref[2:3, :] + shifts_ref[2:3, :]).astype(jnp.bfloat16)
        sort_rows(order, third_rows[...], across, sorted_rows)
        total[...] = after[...] + down_bias_ref[...]
        grad_total[...] = jnp.zeros_like(grad_total)

    dy, third = dy_ref[...], third_rows[...]
    tile = up_ref.shape[2] // 2
    deep = tile // 2
    parts = [slice(0, tile), slice(tile, 2 * tile)]
    pre = [dot_nn(third, up_ref[0, :, p]) + up_bias_ref[:, p] for p in parts]
    grad_hidden = [dot_nt(dy, down_ref[0, p, :]) for p in parts]
    out = grad_third = 0.0
    grads = []
    for i, p in enumerate(parts):
        value, slope = gelu_pair(pre[i])
        hidden = value.astype(jnp.bfloat16)
        low = (grad_hidden[i] * slope).astype(jnp.bfloat16)
        bias_ref[0, :, p] = jnp.sum(low.astype(jnp.float32), axis=0, keepdims=True)
        grad = dot_nn(sorted_rows[...], low).astype(jnp.bfloat16)
        up_send[:, :, p] = grad[:half].reshape(8, rows, tile)
        up_keep[:, :, p] = grad[half:].reshape(8, rows, tile)
        grads.append(dot_nn(hidden.T, dy).astype(jnp.bfloat16))
        out += dot_nn(hidden, down_ref[0, p, :])
        grad_third += dot_nt(low, up_ref[0, :, p])
    total[...] += out
    grad_total[...] += grad_third
    for odd in range(2):
        for far in range(2):

            @pl.when((order[15] % 2 == odd) & (order[15] // 2 % 2 == far))
            def _():
                for n in range(2):
                    both = grads[n ^ far ^ 1]
                    down_send[n] = both[deep * (1 - odd) : deep * (2 - odd)]
                    down_keep[n] = both[deep * odd : deep * (odd + 1)]

    @pl.when(step == pl.num_programs(0) - 1)
    def _():
        out_ref[...] = total[...].astype(jnp.bfloat16)
        grad_ref[...] = grad_total[...]
        kept_ref[...] = after[...]


def third_kernel(third_ref, after_ref, dy_ref, scales_ref, cross_ref, grad_ref, low_ref, mix_ref, sums_ref):
    upstream = dy_ref[...].astype(jnp.float32)
    unit, inverse = layer_parts(after_ref[...])
    grad = third_ref[...]
    sums_ref[...] = column_sums(grad * unit, grad, upstream)
    grad_ref[...] = upstream + layer_back(grad, unit, inverse, scales_ref[2:3, :])
    low_ref[...] = grad_ref[...].astype(jnp.bfloat16)
    mix_ref[...] = dot_nt(low_ref[...], cross_ref[0]).astype(jnp.bfloat16)


def third_back(grad, after, dy, scales, w_cross):
    full = jax.ShapeDtypeStruct(after.shape, jnp.float32)
    low = jax.ShapeDtypeStruct(after.shape, jnp.bfloat16)
    return pl.pallas_call(
        third_kernel,
        out_shape=[full, low, low, jax.ShapeDtypeStruct((8, after.shape[1]), jnp.float32)],
        compiler_params=pltpu.CompilerParams(vmem_limit_bytes=32 * 2**20),
        cost_estimate=NOTHING,
        name="third",
    )(grad, after, dy, scales, w_cross)


def feed_forward(order, after, mixed, dy, scales, shifts, w_cross, w_up, b_up, w_down, b_down):
    tokens, width = dy.shape
    deep = w_up.shape[2]
    tile = deep // 4
    rows = width // 16
    whole = lambda *shape: pl.BlockSpec(shape, lambda j, order: (0,) * len(shape))
    where = lambda j, order: order[8 + j] // 4
    once = lambda *shape: pl.BlockSpec(
        shape, lambda j, order: (0,) * len(shape), pipeline_mode=pl.Buffered(1)
    )
    token = once(tokens, width)
    down_half = jax.ShapeDtypeStruct((8, deep // 16, width), jnp.bfloat16)
    up_half = jax.ShapeDtypeStruct((8, 4 * rows, tile), jnp.bfloat16)
    down_piece = pl.BlockSpec((2, deep // 16, width), lambda j, order: (j, 0, 0))
    up_piece = pl.BlockSpec((8, rows, tile), lambda j, order: (0, where(j, order), 0))
    low = jax.ShapeDtypeStruct((tokens, width), jnp.bfloat16)
    full = jax.ShapeDtypeStruct((tokens, width), jnp.float32)
    out = pl.pallas_call(
        feed_kernel,
        grid_spec=pltpu.PrefetchScalarGridSpec(
            num_scalar_prefetch=1,
            grid=(4,),
            in_specs=[
                token,
                token,
                token,
                whole(3, width),
                whole(3, width),
                once(1, width, width),
                whole(1, width),
                pl.BlockSpec((1, width, tile), lambda j, order: (0, 0, where(j, order))),
                pl.BlockSpec((1, tile), lambda j, order: (0, where(j, order))),
                pl.BlockSpec((1, tile, width), lambda j, order: (0, where(j, order), 0)),
            ],
            out_specs=[
                token,
                token,
                token,
                pl.BlockSpec((1, 1, tile), lambda j, order: (where(j, order), 0, 0)),
                down_piece,
                down_piece,
                up_piece,
                up_piece,
            ],
            scratch_shapes=[pltpu.VMEM((tokens, width), jnp.bfloat16)]
            + [pltpu.VMEM((width, tokens), jnp.bfloat16)] * 2
            + [pltpu.VMEM((tokens, width), jnp.float32)] * 3,
        ),
        out_shape=[
            low,
            full,
            full,
            jax.ShapeDtypeStruct((4, 1, tile), jnp.float32),
            down_half,
            down_half,
            up_half,
            up_half,
        ],
        compiler_params=pltpu.CompilerParams(vmem_limit_bytes=36 * 2**20),
        cost_estimate=NOTHING,
        name="feed",
    )(order, after, mixed, dy, scales, shifts, w_cross, b_down, w_up, b_up, w_down)
    return (*out[:4], (out[4], out[5]), (out[6], out[7]))


def backward_heads(q, k, v, do, p_ref):
    kt = k.T
    queries = []
    keys = values = 0.0
    picked = [do * lane_pick(e, 1.0) for e in range(2)]
    grads = [dot_nt(v, picked[e]) for e in range(2)]
    for e in range(2):
        probs = p_ref[e]
        wide = probs.astype(jnp.float32)
        part = wide * grads[e]
        total = jnp.sum(part, axis=0, keepdims=True)
        ds = (part - wide * total).astype(jnp.bfloat16)
        values += dot_nn(probs, picked[e])
        keys += dot_nn(ds, q * lane_pick(e, HEAD**-0.5))
        queries.append(dot_nn(kt[e * HEAD : (e + 1) * HEAD], ds) * HEAD**-0.5)
    queries = jnp.concatenate(queries, 0).T
    return [g.astype(jnp.bfloat16) for g in (queries, keys, values)]


def self_back_kernel(q_ref, k_ref, v_ref, near_ref, far_ref, out_ref, p_ref, d_ref):
    low = jnp.concatenate([near_ref[...], far_ref[...]])
    do = dot_nt(low, out_ref[0]).astype(jnp.bfloat16)
    grads = backward_heads(q_ref[...], k_ref[...], v_ref[...], do, p_ref)
    for i in range(3):
        d_ref[i] = grads[i]


def self_back(packed, near, far, w_out, probs):
    tokens, width = packed.shape[0], near.shape[1]
    spec = lambda off: pl.BlockSpec((tokens, 128), lambda j: (0, off + j))
    rows = pl.BlockSpec(near.shape, lambda j: (0, 0))
    return pl.pallas_call(
        self_back_kernel,
        grid=(HEADS // 2,),
        in_specs=[spec(0), spec(6), spec(12), rows, rows]
        + [pl.BlockSpec((1, 128, width), lambda j: (0, j, 0))]
        + [pl.BlockSpec((2, tokens, tokens), lambda j: (j, 0, 0))],
        out_specs=pl.BlockSpec((3, tokens, 128), lambda j: (0, 0, j)),
        out_shape=jax.ShapeDtypeStruct((3, tokens, width), jnp.bfloat16),
        compiler_params=pltpu.CompilerParams(vmem_limit_bytes=24 * 2**20),
        cost_estimate=NOTHING,
        name="selfb",
    )(packed, packed, packed, near, far, w_out, pltpu.with_memory_space_constraint(probs, pltpu.HBM))


def second_kernel(
    near_back_ref, far_back_ref, near_given_ref, far_given_ref, near_after_ref, far_after_ref,
    near_grad_ref, far_grad_ref, scales_ref, near_ref, far_ref, sums_ref,
):
    sums = 0.0
    for back, given, after, grad, out in (
        (near_back_ref, near_given_ref, near_after_ref, near_grad_ref, near_ref),
        (far_back_ref, far_given_ref, far_after_ref, far_grad_ref, far_ref),
    ):
        unit, inverse = layer_parts(after[...])
        upstream = back[...].astype(jnp.float32) + given[...].astype(jnp.float32)
        sums += column_sums(upstream * unit, upstream)
        below = layer_back(upstream, unit, inverse, scales_ref[1:2, :])
        out[...] = (grad[...].astype(jnp.float32) + below).astype(jnp.bfloat16)
    sums_ref[...] = sums


def second_back(back, far_back, near_given, far_given, after, far_after, grad, far_grad, scales):
    half, width = near_given.shape
    low = pl.BlockSpec((half, width), lambda j: (1, 0))
    rows = pl.BlockSpec((half, width), lambda j: (0, 0))
    out = jax.ShapeDtypeStruct((half, width), jnp.bfloat16)
    return pl.pallas_call(
        second_kernel,
        grid=(1,),
        in_specs=[low, rows, rows, rows, low, rows, low, rows]
        + [pl.BlockSpec((3, width), lambda j: (0, 0))],
        out_specs=[rows, rows, pl.BlockSpec((8, width), lambda j: (0, 0))],
        out_shape=[out, out, jax.ShapeDtypeStruct((8, width), jnp.float32)],
        compiler_params=pltpu.CompilerParams(vmem_limit_bytes=24 * 2**20),
        cost_estimate=NOTHING,
        name="second",
    )(back, far_back, near_given, far_given, after, far_after, grad, far_grad, scales)


def tail_kernel(
    order, d_ref, w_ref, first_ref, mixed_ref, moved_ref, near_ref, far_ref, scales_ref, *refs,
):
    step = pl.program_id(0)
    stay_ref, gone_ref, sums_ref = refs[8:11]
    across, sorted_rows, total = refs[11:]
    half = sorted_rows.shape[0] // 2

    @pl.when(step == 0)
    def _():
        sort_rows(order, first_ref[...], across, sorted_rows)

    for i in range(3):

        @pl.when(step == i)
        def _():
            part = dot_nt(d_ref[0], w_ref[0])
            grad = dot_nn(sorted_rows[...], d_ref[0]).astype(jnp.bfloat16)
            refs[2 * i][...] = grad[:half].reshape(refs[0].shape)
            refs[2 * i + 1][...] = grad[half:].reshape(refs[0].shape)
            if i == 0:
                total[...] = part
            else:
                total[...] += part

    @pl.when(step == 3)
    def _():
        sort_rows(order, mixed_ref[...], across, sorted_rows)
        low = jnp.concatenate([near_ref[...], far_ref[...]])
        grad = dot_nn(sorted_rows[...], low).astype(jnp.bfloat16)
        refs[6][...] = grad[:half].reshape(refs[0].shape)
        refs[7][...] = grad[half:].reshape(refs[0].shape)
        rows = stay_ref.shape[0]
        unit, inverse = layer_parts(moved_ref[...].astype(jnp.float32))
        grad = total[...]
        sums_ref[...] = column_sums(grad * unit, grad)
        back = layer_back(grad, unit, inverse, scales_ref[0:1, :])
        stay_ref[...] = (near_ref[...].astype(jnp.float32) + back[:rows]).astype(jnp.bfloat16)
        gone_ref[...] = (far_ref[...].astype(jnp.float32) + back[rows:]).astype(jnp.bfloat16)


def tail_grads(order, grads, w_qkv, first, mixed, moved, near, far, scales):
    tokens, width = moved.shape
    half = tokens // 2
    whole = lambda *shape: pl.BlockSpec(shape, lambda j, order: (0,) * len(shape))
    rows = jax.ShapeDtypeStruct((half, width), jnp.bfloat16)
    piece = (8, width // 16, width)
    last = lambda j: jnp.minimum(j, 2)
    outs = pl.pallas_call(
        tail_kernel,
        grid_spec=pltpu.PrefetchScalarGridSpec(
            num_scalar_prefetch=1,
            grid=(4,),
            in_specs=[
                pl.BlockSpec((1, tokens, width), lambda j, order: (last(j), 0, 0)),
                pl.BlockSpec((1, width, width), lambda j, order: (0, 0, last(j))),
                whole(tokens, width),
                whole(tokens, width),
                whole(tokens, width),
                whole(half, width),
                whole(half, width),
                whole(3, width),
            ],
            out_specs=[whole(*piece)] * 8 + [whole(half, width)] * 2 + [whole(8, width)],
            scratch_shapes=[pltpu.VMEM((width, tokens), jnp.bfloat16)] * 2
            + [pltpu.VMEM((tokens, width), jnp.float32)],
        ),
        out_shape=[jax.ShapeDtypeStruct(piece, jnp.bfloat16)] * 8
        + [rows, rows, jax.ShapeDtypeStruct((8, width), jnp.float32)],
        compiler_params=pltpu.CompilerParams(vmem_limit_bytes=40 * 2**20),
        cost_estimate=NOTHING,
        name="tail",
    )(order, grads, w_qkv, first, mixed, moved, near, far, scales)
    return [(outs[i], outs[i + 1]) for i in range(0, 8, 2)], *outs[8:]


def group_kernel(plan, halves, pieces, order, *refs):
    refs = list(refs)
    groups = [[refs.pop(0) for _ in range(n)] for n in halves]
    joined = lambda group: jnp.concatenate([r[...] for r in group]) if len(group) > 1 else group[0][...]
    outs, (across, sorted_rows) = refs[:-2], refs[-2:]
    half = sorted_rows.shape[0] // 2
    before = None
    for i, (x, dy, lead, target) in enumerate(plan):
        turn = x != before
        before = x

        @pl.when(pl.program_id(0) == i)
        def _():
            if turn:
                sort_rows(order, joined(groups[x]), across, sorted_rows)
            right = joined(groups[dy]) if lead is None else groups[dy][0][0]
            grad = dot_nn(sorted_rows[...], right).astype(jnp.bfloat16)
            send_ref, keep_ref = outs[2 * target], outs[2 * target + 1]
            send_ref[...] = grad[:half].reshape(send_ref.shape)
            keep_ref[...] = grad[half:].reshape(keep_ref.shape)


def grad_group(order, operands, plan, name):
    width = operands[0][0].shape[-1]
    rows = width // 16
    tokens = sum(a.shape[-2] for a in operands[0])
    in_specs = []
    for n, group in enumerate(operands):
        for a in group:
            if a.ndim == 2:
                in_specs.append(pl.BlockSpec(a.shape, lambda j, order: (0, 0)))
            else:
                first = min(i for i, p in enumerate(plan) if p[1] == n)
                in_specs.append(
                    pl.BlockSpec(
                        (1, *a.shape[1:]),
                        lambda j, order, first=first, last=a.shape[0] - 1: (
                            jnp.clip(j - first, 0, last),
                            0,
                            0,
                        ),
                    )
                )
    out_specs, out_shape = [], []
    for target in range(1 + max(p[3] for p in plan)):
        steps = [i for i, p in enumerate(plan) if p[3] == target]
        spec = pl.BlockSpec(
            (8, rows, width),
            lambda j, order, first=steps[0], last=len(steps) - 1: (
                0,
                jnp.clip(j - first, 0, last),
                0,
            ),
        )
        out_specs += [spec, spec]
        out_shape += [jax.ShapeDtypeStruct((8, rows * len(steps), width), jnp.bfloat16)] * 2
    outs = pl.pallas_call(
        functools.partial(group_kernel, plan, [len(g) for g in operands], len(out_specs)),
        grid_spec=pltpu.PrefetchScalarGridSpec(
            num_scalar_prefetch=1,
            grid=(len(plan),),
            in_specs=in_specs,
            out_specs=out_specs,
            scratch_shapes=[pltpu.VMEM((width, tokens), jnp.bfloat16)] * 2,
        ),
        out_shape=out_shape,
        compiler_params=pltpu.CompilerParams(vmem_limit_bytes=32 * 2**20),
        cost_estimate=NOTHING,
        name=name,
    )(order, *[a for group in operands for a in group])
    return [(outs[i], outs[i + 1]) for i in range(0, len(outs), 2)]


def add_kernel(count, *refs):
    at = 0
    for n in range(count):
        keep, arrived = refs[2 * n], refs[2 * n + 1]
        rows = keep.shape[-2]
        for i, out in enumerate(refs[2 * count :]):
            out[0, at : at + rows, :] = keep[i, 0] + arrived[i, 0]
        at += rows


def add_halves(keeps, arrivals, name="add"):
    pairs = keeps[0].shape[0] // 2
    width = keeps[0].shape[2]
    rows = sum(k.shape[1] for k in keeps)
    operands = []
    for keep, arrived in zip(keeps, arrivals):
        operands += [a.reshape(2, pairs, *a.shape[1:]) for a in (keep, arrived)]
    out = pl.BlockSpec((1, rows, width), lambda j: (j, 0, 0))
    return pl.pallas_call(
        functools.partial(add_kernel, len(keeps)),
        grid=(pairs,),
        in_specs=[
            pl.BlockSpec((2, 1, *a.shape[2:]), lambda j: (0, j, 0, 0)) for a in operands
        ],
        out_specs=[out, out],
        out_shape=[jax.ShapeDtypeStruct((pairs, rows, width), jnp.bfloat16)] * 2,
        compiler_params=pltpu.CompilerParams(vmem_limit_bytes=16 * 2**20),
        cost_estimate=NOTHING,
        name=name,
    )(*operands)


def last_kernel(keep_ref, arrived_ref, *outs):
    total = keep_ref[0].astype(jnp.float32) + arrived_ref[0].astype(jnp.float32)
    width = total.shape[1]
    at = 0
    for out in outs:
        rows, columns = out.shape
        for n in range(columns // width):
            out[:, n * width : (n + 1) * width] = total[at : at + rows]
            at += rows


def last_sum(keep, arrived, shapes):
    return pl.pallas_call(
        last_kernel,
        out_shape=[jax.ShapeDtypeStruct(s, jnp.float32) for s in shapes],
        compiler_params=pltpu.CompilerParams(vmem_limit_bytes=16 * 2**20),
        cost_estimate=NOTHING,
        name="last",
    )(keep, arrived)


def swap(x, bit):
    return lax.ppermute(x, "page", [(i, i ^ bit) for i in range(16)])


pin = lax.optimization_barrier


def on_device(
    block_input,
    cotangent,
    norm_gain,
    norm_bias,
    w_qkv,
    w_out,
    w_query,
    w_keyval,
    w_cross,
    w_up,
    b_up,
    w_down,
    b_down,
    row_page,
    lengths,
):
    x = block_input[0]
    dy = cotangent[0]
    tokens, width = x.shape
    half = tokens // 2
    pages = lax.axis_size("page")
    device = lax.axis_index("page")
    stream = lax.axis_index("stream")
    scales = norm_gain[0].T
    shifts = norm_bias[0].T
    share = width // pages
    padded = jnp.concatenate([row_page, row_page[:SHIFT]])
    info = jnp.concatenate(
        [
            stream.astype(jnp.int32)[None],
            lengths,
            lax.dynamic_slice_in_dim(padded, device * WIN + SHIFT, WIN),
        ]
    )
    stay = [(pages + i, pages + i) for i in range(pages)]
    both = ("stream", "page")
    forth = [((i + 1) % pages, i) for i in range(pages)] + stay
    back = [(i, (i + 1) % pages) for i in range(pages)] + stay

    def partner_of(rows):
        return lax.ppermute(rows, "stream", [(0, 1), (1, 0)])

    moved = jnp.concatenate([x[half:], lax.ppermute(x[:half], both, forth)])
    first, unit_one, inverse_one = layer_norm(moved.astype(jnp.float32), scales[0], shifts[0])
    packed = matmul(first, w_qkv[0]).astype(jnp.bfloat16)
    moved_mixed, self_probs = attn_fwd(
        info, packed, packed, packed, 0, 6, 12, fill_self_bias, "selff"
    )
    gone, near = moved_mixed[half:], moved_mixed[:half]
    after_gone = moved[half:].astype(jnp.float32) + matmul(gone, w_out[0])
    second_gone = layer_norm(after_gone, scales[1], shifts[1])[0]
    partner_top = lax.ppermute(
        second_gone,
        both,
        [(i, pages + (i + 1) % pages) for i in range(pages)]
        + [(pages + i, i) for i in range(pages)],
    )
    back_mixed = lax.ppermute(gone, both, back)
    after_low = moved[:half].astype(jnp.float32) + matmul(near, w_out[0])
    second_low = layer_norm(after_low, scales[1], shifts[1])[0]
    partner_low = partner_of(second_low)
    back_mixed, second_low, partner_top = pin((back_mixed, second_low, partner_top))
    after_top = x[:half].astype(jnp.float32) + matmul(back_mixed, w_out[0])
    second_top = layer_norm(after_top, scales[1], shifts[1])[0]
    after_self = jnp.concatenate([after_top, after_low])
    second = jnp.concatenate([second_top, second_low])
    cross_q = matmul(second, w_query[0]).astype(jnp.bfloat16)
    cross_q, after_self, partner_top, partner_low = pin(
        (cross_q, after_self, partner_top, partner_low)
    )
    partner = jnp.concatenate([partner_top, partner_low])
    cross_pair = matmul(partner, w_keyval[0]).astype(jnp.bfloat16)
    cross_mixed, cross_probs = attn_fwd(
        info, cross_q, cross_pair, cross_pair, 0, 0, 6, fill_cross_bias, "crossf"
    )
    if pages == 16:
        ordinal = jnp.arange(16, dtype=jnp.int32)
        turned = 15 - ordinal
        turned = (turned & 1) << 3 | (turned & 2) << 1 | (turned & 4) >> 1 | (turned & 8) >> 3
        order = device.astype(jnp.int32) ^ turned
        output, grad_third, after_cross, up_bias, down, up = feed_forward(
            order, after_self, cross_mixed, dy, scales, shifts, w_cross, w_up, b_up, w_down, b_down
        )
        grad_cross_in, cross_low, grad_cmix, sums_three = third_back(
            grad_third, after_cross, dy, scales, w_cross
        )

        def onward(keeps, sends, bit):
            return add_halves(keeps, [swap(s, bit) for s in sends])

        grad_cmix, down_keep, up_keep = pin((grad_cmix, down[1], up[1]))
        down = onward([down_keep], [down[0]], 1)
        up = onward([up_keep], [up[0]], 1)
        grad_cmix, down, up = pin((grad_cmix, down, up))
        cross_grads = attn_bwd(
            cross_q, cross_pair, cross_pair, 0, 0, 6, grad_cmix, cross_probs, "crossb"
        )

        def given(rows):
            keys = dot_nt(cross_grads[1, rows], w_keyval[0][:, :width])
            return (keys + dot_nt(cross_grads[2, rows], w_keyval[0][:, width:])).astype(jnp.bfloat16)

        returned_top = lax.ppermute(
            given(slice(0, half)),
            both,
            [(i, pages + i) for i in range(pages)]
            + [(pages + (i + 1) % pages, i) for i in range(pages)],
        )
        returned_low = partner_of(given(slice(half, tokens)))
        query_back = dot_nt(cross_grads[0], w_query[0])
        far_back = lax.ppermute(query_back[:half].astype(jnp.bfloat16), both, forth)
        far_grad = lax.ppermute(cross_low[:half], both, forth)
        (cross_part,) = grad_group(
            order,
            (
                (cross_mixed,),
                (second_top, second_low),
                (partner_top, partner_low),
                (cross_low,),
                (cross_grads,),
            ),
            ((0, 3, None, 0), (1, 4, 0, 0), (2, 4, 1, 0), (2, 4, 2, 0)),
            "gcross",
        )
        down = onward([down[1]], [down[0]], 4)
        up = onward([up[1]], [up[0]], 2)
        returned_top, returned_low, far_back, far_grad, cross_part, down, up = pin(
            (returned_top, returned_low, far_back, far_grad, cross_part, down, up)
        )
        low_near, low_far, sums_two = second_back(
            query_back, far_back, returned_low, returned_top, after_self, after_gone,
            grad_cross_in, far_grad, scales,
        )
        low_near, cross_keep = pin((low_near, cross_part[1]))
        cross_part = onward([cross_keep], [cross_part[0]], 1)
        low_near, cross_part = pin((low_near, cross_part))
        self_grads = self_back(packed, low_near, low_far, w_out, self_probs)
        self_grads, up_keep = pin((self_grads, up[1]))
        up = onward([up_keep], [up[0]], 4)
        self_grads, up = pin((self_grads, up))
        parts, input_stay, input_gone, sums_one = tail_grads(
            order, self_grads, w_qkv, first, moved_mixed, moved, low_near, low_far, scales
        )
        parts = [parts[1], parts[2], parts[0], parts[3]]
        parts, cross_keep, down_keep = pin((parts, cross_part[1], down[1]))
        down = onward([down_keep], [down[0]], 8)
        cross_part = onward([cross_keep], [cross_part[0]], 2)
        sends, keeps = [p[0] for p in parts], [p[1] for p in parts]
        cross_part, keeps, down = pin((cross_part, keeps, down))
        pair_part = onward(keeps[:2], sends[:2], 1)
        rest_part = onward(keeps[2:], sends[2:], 1)
        pair_part, rest_part, input_gone, up, sums_one = pin(
            (pair_part, rest_part, input_gone, up, sums_one)
        )
        sums = jnp.concatenate(
            [sums_one[:2], sums_two[:2], sums_three[:3], up_bias.reshape(4, width)]
        )
        sums = sums + swap(sums, 1)
        pair_keep, sums = pin((pair_part[1], sums))
        pair_part = onward([pair_keep], [pair_part[0]], 2)
        cross_keep, up_keep, pair_part = pin((cross_part[1], up[1], pair_part))
        (grad_up,) = last_sum(up_keep, swap(up[0], 8), [(48, 4 * width)])
        cross_part = onward([cross_keep], [cross_part[0]], 4)
        cross_part, rest_keep, grad_up = pin((cross_part, rest_part[1], grad_up))
        rest_part = onward([rest_keep], [rest_part[0]], 2)
        rest_part, pair_keep, cross_keep, input_gone = pin(
            (rest_part, pair_part[1], cross_part[1], input_gone)
        )
        input_top = lax.ppermute(input_gone, both, back)
        pair_part = onward([pair_keep], [pair_part[0]], 4)
        grad_cross, grad_query, grad_keyval = last_sum(
            cross_keep,
            swap(cross_part[0], 8),
            [(48, width), (48, width), (48, 2 * width)],
        )
        rest_keep, pair_part, grad_cross, grad_query, grad_keyval, sums = pin(
            (rest_part[1], pair_part, grad_cross, grad_query, grad_keyval, sums)
        )
        rest_part = onward([rest_keep], [rest_part[0]], 4)
        rest_part, pair_keep, sums = pin((rest_part, pair_part[1], sums))
        sums = sums + swap(sums, 2)
        (grad_pair,) = last_sum(pair_keep, swap(pair_part[0], 8), [(48, 2 * width)])
        (grad_down,) = last_sum(down[1], swap(down[0], 2), [(192, width)])
        sums = sums + swap(sums, 4)
        rest_keep, grad_pair, sums = pin((rest_part[1], grad_pair, sums))
        grad_first, grad_out = last_sum(
            rest_keep, swap(rest_part[0], 8), [(48, width), (48, width)]
        )
        sums = sums + swap(sums, 8)
        grad_qkv = jnp.concatenate([grad_first, grad_pair], 1)
        mine = lax.dynamic_slice_in_dim(sums[:7], device * share, share, 1)
        gains, biases = mine[0:6:2], mine[1:6:2]
        down_bias = mine[6]
        up_bias = lax.dynamic_slice_in_dim(sums[7:].reshape(-1), device * 192, 192)
        input_grad = jnp.concatenate([input_top, input_stay])
    else:
        _, unit_two, inverse_two = layer_norm(after_self, scales[1], shifts[1])
        after_cross = after_self + matmul(cross_mixed, w_cross[0])
        third, unit_three, inverse_three = layer_norm(after_cross, scales[2], shifts[2])
        value, slope = gelu_pair(matmul(third, w_up[0]) + b_up[0])
        hidden = value.astype(jnp.bfloat16)
        output = (after_cross + matmul(hidden, w_down[0]) + b_down[0]).astype(jnp.bfloat16)
        upstream = dy.astype(jnp.float32)
        pre_low = (dot_nt(dy, w_down[0]) * slope).astype(jnp.bfloat16)
        back_three, gain_three, shift_three = norm_back(
            dot_nt(pre_low, w_up[0]), unit_three, inverse_three, scales[2]
        )
        grad_cross_in = upstream + back_three
        cross_low = grad_cross_in.astype(jnp.bfloat16)
        grad_cmix = dot_nt(cross_low, w_cross[0]).astype(jnp.bfloat16)
        cross_grads = attn_bwd(
            cross_q, cross_pair, cross_pair, 0, 0, 6, grad_cmix, cross_probs, "crossb"
        )
        pair = jnp.concatenate([cross_grads[1], cross_grads[2]], 1)
        returned = partner_of(dot_nt(pair, w_keyval[0]).astype(jnp.bfloat16))
        back_two, gain_two, shift_two = norm_back(
            dot_nt(cross_grads[0], w_query[0]) + returned.astype(jnp.float32),
            unit_two,
            inverse_two,
            scales[1],
        )
        self_low = (grad_cross_in + back_two).astype(jnp.bfloat16)
        moved_low = jnp.concatenate([self_low[half:], lax.ppermute(self_low[:half], both, forth)])
        grad_smix = dot_nt(moved_low, w_out[0]).astype(jnp.bfloat16)
        self_grads = attn_bwd(packed, packed, packed, 0, 6, 12, grad_smix, self_probs, "selfb")
        packed_grad = jnp.concatenate([self_grads[0], self_grads[1], self_grads[2]], 1)
        back_one, gain_one, shift_one = norm_back(
            dot_nt(packed_grad, w_qkv[0]), unit_one, inverse_one, scales[0]
        )
        moved_grad = (moved_low.astype(jnp.float32) + back_one).astype(jnp.bfloat16)
        input_grad = jnp.concatenate([lax.ppermute(moved_grad[half:], both, back), moved_grad[:half]])

        def summed(grad):
            return lax.psum_scatter(grad, "page", scatter_dimension=0, tiled=True)

        def scattered(left, right):
            return summed(
                lax.dot_general(
                    left, right, (((0,), (0,)), ((), ())), preferred_element_type=jnp.float32
                )
            )

        grad_down = scattered(hidden, dy)
        grad_up = scattered(third, pre_low)
        grad_cross = scattered(cross_mixed, cross_low)
        grad_query = scattered(second, cross_grads[0])
        grad_keyval = scattered(partner, pair)
        grad_out = scattered(jnp.concatenate([back_mixed, near]), self_low)
        grad_qkv = scattered(first, packed_grad)
        gains = summed(jnp.stack([gain_one, gain_two, gain_three], 1)).T
        biases = summed(jnp.stack([shift_one, shift_two, shift_three], 1)).T
        down_bias = summed(jnp.sum(upstream, axis=0))
        up_bias = summed(jnp.sum(pre_low.astype(jnp.float32), axis=0))
    return (
        output[None],
        input_grad[None],
        gains.T[None],
        biases.T[None],
        grad_qkv[None],
        grad_out[None],
        grad_query[None],
        grad_keyval[None],
        grad_cross[None],
        grad_up[None],
        up_bias[None],
        grad_down[None],
        down_bias[None],
    )


def solution(mesh):
    tokens = P("stream", "page", None)
    whole = P("stream", None, None)
    placed = (tokens, tokens) + (whole,) * 8 + (P("stream", None), whole, P("stream", None))
    return jax.shard_map(
        on_device,
        mesh=mesh,
        in_specs=placed + (P(), P("page")),
        out_specs=(tokens,) * 10 + (P("stream", "page"), tokens, P("stream", "page")),
        check_vma=False,
    )
```
